32 devices in a mesh: fsdp: 16 (over z, y, core), tp: 2 (over x).
Axes of the slice: x: 2, y: 2, z: 4, core: 2. Of those that a mesh axis runs over, the one named last changes fastest.
Arguments:
- inputs: bfloat16 [17664, 1024], P(('fsdp', 'tp')), may hold values from -6 to 6
- skip_inputs: bfloat16 [2, 17664, 1024], P(None, ('fsdp', 'tp')), may hold values from -6 to 6
- skip_weight: bfloat16 [2, 2048, 1024], P(None, 'fsdp', 'tp'), may hold values from -0.125 to 0.125
- skip_bias: bfloat16 [2, 1024], P(None, ('fsdp', 'tp')), may hold values from -1.5 to 1.5
- first_gain: bfloat16 [2, 1024], P(None, ('fsdp', 'tp')), may hold values from 0.5 to 1.5
- first_shift: bfloat16 [2, 1024], P(None, ('fsdp', 'tp')), may hold values from -1.5 to 1.5
- attention_in: bfloat16 [2, 1024, 3, 1024], P(None, 'fsdp', None, 'tp'), may hold values from -0.1875 to 0.1875
- attention_out: bfloat16 [2, 1024, 1024], P(None, 'tp', 'fsdp'), may hold values from -0.75 to 0.75
- out_bias: bfloat16 [2, 1024], P(None, ('fsdp', 'tp')), may hold values from -1.5 to 1.5
- second_gain: bfloat16 [2, 1024], P(None, ('fsdp', 'tp')), may hold values from 0.5 to 1.5
- second_shift: bfloat16 [2, 1024], P(None, ('fsdp', 'tp')), may hold values from -1.5 to 1.5
- up_weight: bfloat16 [2, 1024, 4096], P(None, 'fsdp', 'tp'), may hold values from -0.1875 to 0.1875
- up_bias: bfloat16 [2, 4096], P(None, ('fsdp', 'tp')), may hold values from -2.5 to 2.5
- down_weight: bfloat16 [2, 4096, 1024], P(None, 'tp', 'fsdp'), may hold values from -0.1875 to 0.1875
- down_bias: bfloat16 [2, 1024], P(None, ('fsdp', 'tp')), may hold values from -1.5 to 1.5
- cotangent: bfloat16 [17664, 1024], P(('fsdp', 'tp')), may hold values from -6 to 6
Outputs:
- output: float32 [17664, 1024], P(('fsdp', 'tp'))
- input_grad: float32 [17664, 1024], P(('fsdp', 'tp'))
- skip_grad: float32 [2, 17664, 1024], P(None, ('fsdp', 'tp'))
- skip_weight_grad: float32 [2, 2048, 1024], P(None, 'fsdp', 'tp')
- skip_bias_grad: float32 [2, 1024], P(None, ('fsdp', 'tp'))
- first_gain_grad: float32 [2, 1024], P(None, ('fsdp', 'tp'))
- first_shift_grad: float32 [2, 1024], P(None, ('fsdp', 'tp'))
- attention_in_grad: float32 [2, 1024, 3, 1024], P(None, 'fsdp', None, 'tp')
- attention_out_grad: float32 [2, 1024, 1024], P(None, 'tp', 'fsdp')
- out_bias_grad: float32 [2, 1024], P(None, ('fsdp', 'tp'))
- second_gain_grad: float32 [2, 1024], P(None, ('fsdp', 'tp'))
- second_shift_grad: float32 [2, 1024], P(None, ('fsdp', 'tp'))
- up_weight_grad: float32 [2, 1024, 4096], P(None, 'fsdp', 'tp')
- up_bias_grad: float32 [2, 4096], P(None, ('fsdp', 'tp'))
- down_weight_grad: float32 [2, 4096, 1024], P(None, 'tp', 'fsdp')
- down_bias_grad: float32 [2, 1024], P(None, ('fsdp', 'tp'))
The draws below stay inside these ranges and needn't reach their ends.
All inputs are finite; a program needn't handle non-finite values.
Results may differ from the reference program's by a relative error of at most 0.023.
Values may be sent and summed in bfloat16 or wider, within the bound.
No kernel may reach another device: no remote copies, remote signals or barrier semaphores. Data moves between devices by JAX's collectives and lax.ppermute only.
A program may use at most 384 MiB of HBM per device.

```python
import jax
import jax.numpy as jnp
from jax import lax

D = 1024
HEADS = 16
HEAD_DIM = 64
FF = 4096
SEQ_LEN = 1104
LAYERS = 2
TOKENS = 17664


def levels(stream_key, dims, shards, least, largest):
    level = 1.0
    for axis_at, blocks in shards:
        draws = jax.random.uniform(jax.random.fold_in(jax.random.fold_in(stream_key, 6), axis_at), (blocks,), jnp.float32, least / len(shards), largest / len(shards))
        level = level * jnp.repeat(jnp.exp(draws), dims[axis_at] // blocks).reshape((-1,) + (1,) * (len(dims) - 1 - axis_at))
    return level


def centred(key, extent, width, most, split=(), dtype=jnp.bfloat16):
    factor_of = levels(key, extent, split, -0.22, 0.18) if split else 1.0
    array = jax.random.normal(key, extent, jnp.float32) * width * factor_of
    return jnp.minimum(jnp.maximum(array, -most), most).astype(dtype)


def setup_inputs(seed: int = 0) -> dict:
    key_of = jax.random.split(jax.random.key(seed), 17)
    return {
        "inputs": centred(key_of[0], (TOKENS, D), 1.0, 6.0, ((0, 32),)),
        "skip_inputs": centred(key_of[1], (LAYERS, TOKENS, D), 1.0, 6.0, ((1, 32),)),
        "skip_weight": centred(key_of[2], (LAYERS, 2 * D, D), (2 * D) ** -0.5, 0.125, ((1, 16), (2, 2))),
        "skip_bias": centred(key_of[3], (LAYERS, D), 0.3, 1.5, ((1, 32),)),
        "first_gain": jnp.clip(1.0 + 0.1 * jax.random.normal(key_of[4], (LAYERS, D), jnp.float32), 0.5, 1.5).astype(jnp.bfloat16),
        "first_shift": centred(key_of[5], (LAYERS, D), 0.3, 1.5, ((1, 32),)),
        "attention_in": centred(key_of[6], (LAYERS, D, 3, D), D ** -0.5, 0.1875, ((1, 16), (3, 2))),
        "attention_out": centred(key_of[7], (LAYERS, D, D), HEAD_DIM ** -0.5, 0.75, ((1, 2), (2, 16))),
        "out_bias": centred(key_of[8], (LAYERS, D), 0.3, 1.5, ((1, 32),)),
        "second_gain": jnp.clip(1.0 + 0.1 * jax.random.normal(key_of[9], (LAYERS, D), jnp.float32), 0.5, 1.5).astype(jnp.bfloat16),
        "second_shift": centred(key_of[10], (LAYERS, D), 0.3, 1.5, ((1, 32),)),
        "up_weight": centred(key_of[11], (LAYERS, D, FF), D ** -0.5, 0.1875, ((1, 16), (2, 2))),
        "up_bias": centred(key_of[12], (LAYERS, FF), 0.5, 2.5, ((1, 32),)),
        "down_weight": centred(key_of[13], (LAYERS, FF, D), (FF // 4) ** -0.5, 0.1875, ((1, 2), (2, 16))),
        "down_bias": centred(key_of[14], (LAYERS, D), 0.3, 1.5, ((1, 32),)),
        "cotangent": centred(key_of[15], (TOKENS, D), 1.0, 6.0, ((0, 32),)),
    }


epsilon = 1e-05

@jax.custom_vjp
def low(v):
    return lax.optimization_barrier(v.astype(jnp.bfloat16)).astype(jnp.float32)

@jax.custom_vjp
def low_back(v):
    return v

def low_keep(v):
    return (low(v), None)

def low_pass(kept, grad):
    return (grad,)

def back_keep(v):
    return (v, None)

def back_low(kept, grad):
    return (low(grad),)
low.defvjp(low_keep, low_pass)
low_back.defvjp(back_keep, back_low)

def product(form, left, right):
    return jnp.einsum(form, left, right, precision=lax.Precision.HIGHEST)

def layer_norm(values_in, gain, shift):
    center = values_in - lax.optimization_barrier(jnp.mean(values_in, -1, keepdims=True))
    spread = lax.optimization_barrier(jnp.mean(center * center, -1, keepdims=True))
    return center * lax.rsqrt(spread + epsilon) * gain + shift

def one_layer(stream, skip_rows, params):
    skip_weight, skip_bias, first_gain, first_shift, attention_in, attention_out, out_bias, second_gain, second_shift, up_weight, up_bias, down_weight, down_bias = params
    joined = jnp.concatenate([low(stream), skip_rows], 1)
    hidden = low_back(product('tc,ce->te', joined, skip_weight)) + skip_bias
    first_norm = low(layer_norm(hidden, first_gain, first_shift))
    triple = low(low_back(product('td,dch->tch', first_norm, attention_in)))
    query = triple[:, 0].reshape(SEQ_LEN, HEADS, HEAD_DIM)
    key_rows = triple[:, 1].reshape(SEQ_LEN, HEADS, HEAD_DIM)
    value_rows = triple[:, 2].reshape(SEQ_LEN, HEADS, HEAD_DIM)
    scores = low_back(product('qhd,khd->hqk', query, key_rows) * HEAD_DIM ** (-0.5))
    row_top = lax.optimization_barrier(jnp.max(scores, -1, keepdims=True))
    exp_scores = jnp.exp(scores - row_top)
    probs = exp_scores / lax.optimization_barrier(jnp.sum(exp_scores, -1, keepdims=True))
    mixed = low(low_back(product('hqk,khd->qhd', low(probs), value_rows))).reshape(SEQ_LEN, D)
    middle = hidden + low_back(product('th,hd->td', mixed, attention_out)) + out_bias
    second_norm = low(layer_norm(middle, second_gain, second_shift))
    preact = low_back(product('td,df->tf', second_norm, up_weight)) + up_bias
    activated = low(jax.nn.gelu(preact, approximate=False))
    return middle + low_back(product('tf,fd->td', activated, down_weight)) + down_bias

def stacked_forward(stream, skip_rows, params):
    for layer_index in range(LAYERS):
        stream = one_layer(stream, skip_rows[layer_index], tuple((p[layer_index] for p in params)))
    return stream

def reference(inputs, skip_inputs, skip_weight, skip_bias, first_gain, first_shift, attention_in, attention_out, out_bias, second_gain, second_shift, up_weight, up_bias, down_weight, down_bias, cotangent):
    params = tuple((p.astype(jnp.float32) for p in (skip_weight, skip_bias, first_gain, first_shift, attention_in, attention_out, out_bias, second_gain, second_shift, up_weight, up_bias, down_weight, down_bias)))
    seq_count = inputs.shape[0] // SEQ_LEN
    streams = inputs.astype(jnp.float32).reshape(seq_count, SEQ_LEN, D)
    skip_rows = skip_inputs.astype(jnp.float32).reshape(LAYERS, seq_count, SEQ_LEN, D).transpose(1, 0, 2, 3)
    tangents = cotangent.astype(jnp.float32).reshape(seq_count, SEQ_LEN, D)

    def one_sequence(totals, items):
        stream, skips_here, tangent = items
        result, pullback = jax.vjp(stacked_forward, stream, skips_here, params)
        stream_grad, skips_grad, param_grads = pullback(tangent)
        return (jax.tree.map(jnp.add, totals, param_grads), (result, stream_grad, skips_grad))
    start = tuple((jnp.zeros(p.shape, jnp.float32) for p in params))
    totals, (results, stream_grads, skips_grads) = lax.scan(one_sequence, start, (streams, skip_rows, tangents))
    output = results.reshape(-1, D)
    input_grad = stream_grads.reshape(-1, D)
    skip_grad = skips_grads.transpose(1, 0, 2, 3).reshape(LAYERS, -1, D)
    return (output, input_grad, skip_grad, totals[0], totals[1], totals[2], totals[3], totals[4], totals[5], totals[6], totals[7], totals[8], totals[9], totals[10], totals[11], totals[12])
```

```python
import jax
import jax.numpy as jnp
from jax import lax
from jax.experimental import pallas as pl
from jax.experimental.pallas import tpu as pltpu
from jax.sharding import PartitionSpec as P

HEAD_DIM = 64
FF = 4096
SEQ_LEN = 1104
LAYERS = 2


epsilon = 1e-05


def norm_apply(values_in, gain, shift):
    center = values_in - jnp.mean(values_in, -1, keepdims=True)
    spread = jnp.mean(center * center, -1, keepdims=True)
    return center * lax.rsqrt(spread + epsilon) * gain + shift


def gelu_exact(values_in):
    return jax.nn.gelu(values_in, approximate=False)


def split_heads(triple_seq):
    head_count = triple_seq.shape[2] // HEAD_DIM
    return (triple_seq.reshape(SEQ_LEN, 3, head_count, HEAD_DIM), head_count)


def attend(triple_seq):
    heads_split, head_count = split_heads(triple_seq)
    query, key_rows, value_rows = (heads_split[:, 0], heads_split[:, 1], heads_split[:, 2])
    half_rows = SEQ_LEN // 2
    score_scale = HEAD_DIM ** (-0.5)
    outputs, totals = ([], [])
    for part_index in range(2):
        query_part = query[part_index * half_rows : (part_index + 1) * half_rows]
        scores = (
            jnp.einsum("qhd,khd->hqk", query_part, key_rows, preferred_element_type=jnp.float32)
            * score_scale
        )
        row_top = jnp.max(scores, -1, keepdims=True)
        exp_scores = jnp.exp(scores - row_top)
        row_total = jnp.sum(exp_scores, -1, keepdims=True)
        low_probs = (exp_scores / row_total).astype(jnp.bfloat16)
        mixed = jnp.einsum(
            "hqk,khd->qhd", low_probs, value_rows, preferred_element_type=jnp.float32
        )
        outputs.append(mixed.astype(jnp.bfloat16).reshape(half_rows, head_count * HEAD_DIM))
        totals.append((row_top + jnp.log(row_total))[..., 0])
    return (jnp.concatenate(outputs, 0), jnp.concatenate(totals, 1))


def attend_back(items):
    triple_seq, log_total, mixed_grad = items
    heads_split, head_count = split_heads(triple_seq)
    query, key_rows, value_rows = (heads_split[:, 0], heads_split[:, 1], heads_split[:, 2])
    grad_heads = mixed_grad.reshape(SEQ_LEN, head_count, HEAD_DIM)
    half_rows = SEQ_LEN // 2
    score_scale = HEAD_DIM ** (-0.5)
    key_grad = jnp.zeros((SEQ_LEN, head_count, HEAD_DIM), jnp.float32)
    value_grad = jnp.zeros((SEQ_LEN, head_count, HEAD_DIM), jnp.float32)
    query_grads = []
    for part_index in range(2):
        rows_here = slice(part_index * half_rows, (part_index + 1) * half_rows)
        query_part = query[rows_here]
        grad_part = grad_heads[rows_here]
        scores = (
            jnp.einsum("qhd,khd->hqk", query_part, key_rows, preferred_element_type=jnp.float32)
            * score_scale
        )
        probs = jnp.exp(scores - log_total[:, rows_here][..., None])
        low_probs = probs.astype(jnp.bfloat16)
        value_grad = value_grad + jnp.einsum(
            "hqk,qhd->khd", low_probs, grad_part, preferred_element_type=jnp.float32
        )
        prob_grad = jnp.einsum(
            "qhd,khd->hqk", grad_part, value_rows, preferred_element_type=jnp.float32
        )
        score_grad = (probs * (prob_grad - jnp.sum(prob_grad * probs, -1, keepdims=True))).astype(
            jnp.bfloat16
        )
        query_grads.append(
            jnp.einsum("hqk,khd->qhd", score_grad, key_rows, preferred_element_type=jnp.float32)
            * score_scale
        )
        key_grad = (
            key_grad
            + jnp.einsum("hqk,qhd->khd", score_grad, query_part, preferred_element_type=jnp.float32)
            * score_scale
        )
    stacked = jnp.stack([jnp.concatenate(query_grads, 0), key_grad, value_grad], 1)
    return stacked.reshape(SEQ_LEN, 3, head_count * HEAD_DIM).astype(jnp.bfloat16)


def general_body(
    inputs,
    skip_inputs,
    skip_weight,
    skip_bias,
    first_gain,
    first_shift,
    attention_in,
    attention_out,
    out_bias,
    second_gain,
    second_shift,
    up_weight,
    up_bias,
    down_weight,
    down_bias,
    cotangent,
):

    def fetch_layer(layer_index):
        small_params = (
            lax.all_gather(skip_bias[layer_index], ("fsdp", "tp"), axis=0, tiled=True),
            lax.all_gather(first_gain[layer_index], ("fsdp", "tp"), axis=0, tiled=True),
            lax.all_gather(first_shift[layer_index], ("fsdp", "tp"), axis=0, tiled=True),
            lax.all_gather(out_bias[layer_index], ("fsdp", "tp"), axis=0, tiled=True),
            lax.all_gather(second_gain[layer_index], ("fsdp", "tp"), axis=0, tiled=True),
            lax.all_gather(second_shift[layer_index], ("fsdp", "tp"), axis=0, tiled=True),
            lax.all_gather(up_bias[layer_index], ("fsdp", "tp"), axis=0, tiled=True),
            lax.all_gather(down_bias[layer_index], ("fsdp", "tp"), axis=0, tiled=True),
        )
        block = (
            lax.all_gather(skip_weight[layer_index], "fsdp", axis=0, tiled=True),
            lax.all_gather(attention_in[layer_index], "fsdp", axis=0, tiled=True),
            lax.all_gather(attention_out[layer_index], "fsdp", axis=1, tiled=True),
            lax.all_gather(up_weight[layer_index], "fsdp", axis=0, tiled=True),
            lax.all_gather(down_weight[layer_index], "fsdp", axis=1, tiled=True),
        )
        weight_up, weight_down = (block[3], block[4])
        unit_width = weight_up.shape[1]
        bias_up = lax.dynamic_slice_in_dim(
            small_params[6], lax.axis_index("tp") * unit_width, unit_width
        )
        return (small_params, block[0], block[1], block[2], weight_up, bias_up, weight_down)

    def rows_of(normed):
        return lax.all_gather(normed, "tp", axis=0, tiled=True)

    def sum_rows(partial_value):
        return lax.psum_scatter(
            partial_value.astype(jnp.bfloat16), "tp", scatter_dimension=0, tiled=True
        ).astype(jnp.float32)

    def grad_rows_of(grad_low):
        return lax.all_gather(grad_low, "tp", axis=0, tiled=True)

    def sum_row_grads(partial_value):
        return lax.psum_scatter(
            partial_value.astype(jnp.bfloat16), "tp", scatter_dimension=0, tiled=True
        ).astype(jnp.float32)

    def forward(stream, skip_rows, weights):
        small_params, weight_skip, weight_qkv, weight_out, weight_up, bias_up, weight_down = weights
        joined = jnp.concatenate([stream.astype(jnp.bfloat16), skip_rows], 1)
        rows_joined = rows_of(joined)
        hidden_part = jnp.dot(rows_joined, weight_skip, preferred_element_type=jnp.float32)
        hidden = (
            lax.all_to_all(
                hidden_part.astype(jnp.bfloat16), "tp", split_axis=0, concat_axis=1, tiled=True
            ).astype(hidden_part.dtype)
            + small_params[0]
        )
        first_norm = norm_apply(hidden, small_params[1], small_params[2]).astype(jnp.bfloat16)
        rows_first = rows_of(first_norm)
        triple = jnp.einsum(
            "td,dch->tch", rows_first, weight_qkv, preferred_element_type=jnp.float32
        ).astype(jnp.bfloat16)
        seq_count = rows_first.shape[0] // SEQ_LEN
        head_out, log_total = lax.map(attend, triple.reshape(seq_count, SEQ_LEN, 3, -1))
        head_out = head_out.reshape(rows_first.shape[0], -1)
        middle = (
            hidden
            + sum_rows(jnp.dot(head_out, weight_out, preferred_element_type=jnp.float32))
            + small_params[3]
        )
        second_norm = norm_apply(middle, small_params[4], small_params[5]).astype(jnp.bfloat16)
        rows_second = rows_of(second_norm)
        preact = jnp.dot(rows_second, weight_up, preferred_element_type=jnp.float32) + bias_up
        activated = gelu_exact(preact).astype(jnp.bfloat16)
        branch = sum_rows(jnp.dot(activated, weight_down, preferred_element_type=jnp.float32))
        result = middle + branch + small_params[7]
        kept = (
            rows_joined,
            hidden,
            rows_first,
            triple,
            head_out,
            log_total,
            middle,
            rows_second,
            preact,
            activated,
        )
        return (result, kept)

    streams = [inputs.astype(jnp.float32)]
    stored = []
    for layer_index in range(LAYERS):
        weights = fetch_layer(layer_index)
        result, kept_here = forward(streams[layer_index], skip_inputs[layer_index], weights)
        stored.append((weights, kept_here))
        streams.append(result)
    output = streams[LAYERS]
    stream_grad = cotangent.astype(jnp.float32)
    skip_parts = [None] * LAYERS
    small_parts = [None] * LAYERS
    block_parts = [None] * LAYERS
    for layer_index in reversed(range(LAYERS)):
        weights = fetch_layer(layer_index)
        unused_result, kept = forward(streams[layer_index], skip_inputs[layer_index], weights)
        (
            backward_small_params,
            backward_weight_skip,
            backward_weight_qkv,
            backward_weight_out,
            backward_weight_up,
            backward_bias_up,
            backward_weight_down,
        ) = weights
        (
            backward_rows_joined,
            backward_hidden,
            backward_rows_first,
            backward_triple,
            backward_head_out,
            backward_log_total,
            backward_middle,
            backward_rows_second,
            backward_preact,
            backward_activated,
        ) = kept
        down_bias_grad = jnp.sum(stream_grad, 0)
        grad_rows = grad_rows_of(stream_grad.astype(jnp.bfloat16))
        act_grad = jnp.einsum(
            "td,fd->tf", grad_rows, backward_weight_down, preferred_element_type=jnp.float32
        )
        down_weight_grad = jnp.einsum(
            "tf,td->fd", backward_activated, grad_rows, preferred_element_type=jnp.float32
        )
        gelu_unused, gelu_pull = jax.vjp(gelu_exact, backward_preact)
        pre_grad = gelu_pull(act_grad)[0]
        up_bias_part = jnp.sum(pre_grad, 0)
        pre_low = pre_grad.astype(jnp.bfloat16)
        up_weight_grad = jnp.einsum(
            "td,tf->df", backward_rows_second, pre_low, preferred_element_type=jnp.float32
        )
        second_grad = sum_row_grads(
            jnp.einsum("tf,df->td", pre_low, backward_weight_up, preferred_element_type=jnp.float32)
        )
        up_bias_full = lax.dynamic_update_slice_in_dim(
            jnp.zeros((FF,), jnp.float32),
            up_bias_part,
            lax.axis_index("tp") * up_bias_part.shape[0],
            0,
        )
        norm_unused, second_pull = jax.vjp(
            norm_apply, backward_middle, backward_small_params[4], backward_small_params[5]
        )
        middle_norm_grad, second_gain_grad, second_shift_grad = second_pull(second_grad)
        middle_grad = stream_grad + middle_norm_grad
        out_bias_grad = jnp.sum(middle_grad, 0)
        middle_rows = grad_rows_of(middle_grad.astype(jnp.bfloat16))
        mixed_grad = jnp.einsum(
            "td,hd->th", middle_rows, backward_weight_out, preferred_element_type=jnp.float32
        ).astype(jnp.bfloat16)
        out_weight_grad = jnp.einsum(
            "th,td->hd", backward_head_out, middle_rows, preferred_element_type=jnp.float32
        )
        backward_seq_count = backward_rows_first.shape[0] // SEQ_LEN
        triple_grad = lax.map(
            attend_back,
            (
                backward_triple.reshape(backward_seq_count, SEQ_LEN, 3, -1),
                backward_log_total,
                mixed_grad.reshape(backward_seq_count, SEQ_LEN, -1),
            ),
        )
        triple_grad = triple_grad.reshape(backward_triple.shape)
        qkv_weight_grad = jnp.einsum(
            "td,tch->dch", backward_rows_first, triple_grad, preferred_element_type=jnp.float32
        )
        first_grad = sum_row_grads(
            jnp.einsum(
                "tch,dch->td", triple_grad, backward_weight_qkv, preferred_element_type=jnp.float32
            )
        )
        norm_unused_two, first_pull = jax.vjp(
            norm_apply, backward_hidden, backward_small_params[1], backward_small_params[2]
        )
        hidden_norm_grad, first_gain_grad, first_shift_grad = first_pull(first_grad)
        hidden_grad = middle_grad + hidden_norm_grad
        skip_bias_grad = jnp.sum(hidden_grad, 0)
        hidden_low = hidden_grad.astype(jnp.bfloat16)
        hidden_cols = lax.all_to_all(hidden_low, "tp", split_axis=1, concat_axis=0, tiled=True)
        joined_grad = sum_row_grads(
            jnp.einsum(
                "te,ce->tc", hidden_cols, backward_weight_skip, preferred_element_type=jnp.float32
            )
        )
        skip_weight_grad = jnp.einsum(
            "tc,te->ce", backward_rows_joined, hidden_cols, preferred_element_type=jnp.float32
        )
        small_grads = (
            lax.psum_scatter(skip_bias_grad, ("fsdp", "tp"), scatter_dimension=0, tiled=True),
            lax.psum_scatter(
                first_gain_grad.astype(jnp.float32), ("fsdp", "tp"), scatter_dimension=0, tiled=True
            ),
            lax.psum_scatter(
                first_shift_grad.astype(jnp.float32),
                ("fsdp", "tp"),
                scatter_dimension=0,
                tiled=True,
            ),
            lax.psum_scatter(out_bias_grad, ("fsdp", "tp"), scatter_dimension=0, tiled=True),
            lax.psum_scatter(
                second_gain_grad.astype(jnp.float32),
                ("fsdp", "tp"),
                scatter_dimension=0,
                tiled=True,
            ),
            lax.psum_scatter(
                second_shift_grad.astype(jnp.float32),
                ("fsdp", "tp"),
                scatter_dimension=0,
                tiled=True,
            ),
            lax.psum_scatter(up_bias_full, ("fsdp", "tp"), scatter_dimension=0, tiled=True),
            lax.psum_scatter(down_bias_grad, ("fsdp", "tp"), scatter_dimension=0, tiled=True),
        )
        block_grads = (
            lax.psum_scatter(
                skip_weight_grad.astype(jnp.bfloat16), "fsdp", scatter_dimension=0, tiled=True
            ).astype(jnp.float32),
            lax.psum_scatter(
                qkv_weight_grad.astype(jnp.bfloat16), "fsdp", scatter_dimension=0, tiled=True
            ).astype(jnp.float32),
            lax.psum_scatter(
                out_weight_grad.astype(jnp.bfloat16), "fsdp", scatter_dimension=1, tiled=True
            ).astype(jnp.float32),
            lax.psum_scatter(
                up_weight_grad.astype(jnp.bfloat16), "fsdp", scatter_dimension=0, tiled=True
            ).astype(jnp.float32),
            lax.psum_scatter(
                down_weight_grad.astype(jnp.bfloat16), "fsdp", scatter_dimension=1, tiled=True
            ).astype(jnp.float32),
        )
        width = backward_weight_skip.shape[0] // 2
        stream_grad, skip_part, small_grads, block_grads = (
            joined_grad[:, :width],
            joined_grad[:, width:],
            small_grads,
            block_grads,
        )
        skip_parts[layer_index] = skip_part
        small_parts[layer_index] = small_grads
        block_parts[layer_index] = block_grads

    def stack_small(position):
        return jnp.stack([small_parts[index_layer][position] for index_layer in range(LAYERS)])

    def stack_block(position):
        return jnp.stack([block_parts[index_layer][position] for index_layer in range(LAYERS)])

    return (
        output,
        stream_grad,
        jnp.stack(skip_parts),
        stack_block(0),
        stack_small(0),
        stack_small(1),
        stack_small(2),
        stack_block(1),
        stack_block(2),
        stack_small(3),
        stack_small(4),
        stack_small(5),
        stack_block(3),
        stack_small(6),
        stack_block(4),
        stack_small(7),
    )


BOTH = ("fsdp", "tp")
GAUSS = 0.3989422804014327


def ring_order(chips):
    half = chips // 2
    return [2 * i for i in range(half)] + [2 * i + 1 for i in reversed(range(half))]


def choose_body(mesh):
    fsdp_size, tp_size = (mesh.shape["fsdp"], mesh.shape["tp"])
    if tp_size != 2 or fsdp_size < 4 or fsdp_size & (fsdp_size - 1):
        return general_body
    return lambda *arrays: fast_body(fsdp_size, *arrays)


def row_chunks(count):
    return [(begin, min(384, count - begin)) for begin in range(0, count, 384)]


NT = (((1,), (1,)), ((), ()))
TN = (((0,), (0,)), ((), ()))


def head_lanes(value, head):
    lane = lax.broadcasted_iota(jnp.int32, value.shape, 1)
    return jnp.where((lane >= HEAD_DIM) == (head == 1), value, jnp.zeros_like(value))


def attention_forward(triple):
    tokens, width = (triple.shape[0], triple.shape[1] // 3)
    pairs = width // (2 * HEAD_DIM)

    def kernel(query_ref, key_ref, value_ref, out_ref, total_ref):
        keys = key_ref[...]
        values = value_ref[...]
        for begin, rows in row_chunks(tokens):
            query = query_ref[begin : begin + rows, :] * jnp.bfloat16(HEAD_DIM**-0.5)
            mixed, totals = ([], [])
            for head in range(2):
                scores = lax.dot_general(
                    head_lanes(query, head), keys, NT, preferred_element_type=jnp.float32
                )
                top = jnp.max(scores, -1, keepdims=True)
                grown = jnp.exp(scores - top)
                total = jnp.sum(grown, -1, keepdims=True)
                mixed.append(
                    jnp.dot(
                        grown.astype(jnp.bfloat16), values, preferred_element_type=jnp.float32
                    )
                    / total
                )
                totals.append(top + jnp.log(total))
            lane = lax.broadcasted_iota(jnp.int32, mixed[0].shape, 1)
            out_ref[begin : begin + rows, :] = jnp.where(
                lane < HEAD_DIM, mixed[0], mixed[1]
            ).astype(jnp.bfloat16)
            both = jnp.where(lane < HEAD_DIM, totals[0], totals[1]).T
            total_ref[0, 0:1, begin : begin + rows] = both[0:1, :]
            total_ref[0, 1:2, begin : begin + rows] = both[HEAD_DIM : HEAD_DIM + 1, :]

    def part(index):
        return pl.BlockSpec((tokens, 2 * HEAD_DIM), lambda i: (0, index * pairs + i))

    return pl.pallas_call(
        kernel,
        grid=(pairs,),
        in_specs=[part(0), part(1), part(2)],
        out_specs=[part(0), pl.BlockSpec((1, 2, tokens), lambda i: (i, 0, 0))],
        out_shape=[
            jax.ShapeDtypeStruct((tokens, width), jnp.bfloat16),
            jax.ShapeDtypeStruct((pairs, 2, tokens), jnp.float32),
        ],
        compiler_params=pltpu.CompilerParams(vmem_limit_bytes=48 << 20),
        cost_estimate=pl.CostEstimate(
            flops=16 * pairs * tokens * tokens * HEAD_DIM,
            bytes_accessed=8 * tokens * width,
            transcendentals=2 * pairs * tokens * tokens,
        ),
    )(triple, triple, triple)


def attention_backward(triple, head_out, log_total, mixed_grad):
    tokens, width = (triple.shape[0], triple.shape[1] // 3)
    pairs = width // (2 * HEAD_DIM)
    score_scale = HEAD_DIM**-0.5

    def kernel(
        query_ref, key_ref, value_ref, out_ref, total_ref, grad_ref, dq_ref, dk_ref, dv_ref, sum_ref
    ):
        query = query_ref[...] * jnp.bfloat16(score_scale)
        grad = grad_ref[...]
        product = grad.astype(jnp.float32) * out_ref[...].astype(jnp.float32)
        ones = jnp.ones((8, 2 * HEAD_DIM), jnp.float32)
        deltas = [
            lax.dot_general(
                head_lanes(ones, head),
                product,
                NT,
                precision=lax.Precision.HIGHEST,
                preferred_element_type=jnp.float32,
            )[0:1, :]
            for head in range(2)
        ]
        for begin, rows in row_chunks(tokens):
            keys = key_ref[begin : begin + rows, :]
            values = value_ref[begin : begin + rows, :]
            key_grads, value_grads = ([], [])
            for head in range(2):
                keys_here = head_lanes(keys, head)
                scores = lax.dot_general(
                    keys_here, query, NT, preferred_element_type=jnp.float32
                )
                probs = jnp.exp(scores - total_ref[0, head : head + 1, :])
                prob_grad = lax.dot_general(
                    head_lanes(values, head), grad, NT, preferred_element_type=jnp.float32
                )
                score_grad = (probs * (prob_grad - deltas[head])).astype(jnp.bfloat16)
                value_grads.append(
                    jnp.dot(
                        probs.astype(jnp.bfloat16), grad, preferred_element_type=jnp.float32
                    )
                )
                key_grads.append(jnp.dot(score_grad, query, preferred_element_type=jnp.float32))
                query_grad = lax.dot_general(
                    score_grad, keys_here, TN, preferred_element_type=jnp.float32
                )
                if begin == 0 and head == 0:
                    sum_ref[...] = query_grad
                else:
                    sum_ref[...] += query_grad
            lane = lax.broadcasted_iota(jnp.int32, key_grads[0].shape, 1)
            dk_ref[begin : begin + rows, :] = jnp.where(
                lane < HEAD_DIM, key_grads[0], key_grads[1]
            ).astype(jnp.bfloat16)
            dv_ref[begin : begin + rows, :] = jnp.where(
                lane < HEAD_DIM, value_grads[0], value_grads[1]
            ).astype(jnp.bfloat16)
        dq_ref[...] = (sum_ref[...] * score_scale).astype(jnp.bfloat16)

    def part(index):
        return pl.BlockSpec((tokens, 2 * HEAD_DIM), lambda i: (0, index * pairs + i))

    grads = pl.pallas_call(
        kernel,
        grid=(pairs,),
        in_specs=[
            part(0),
            part(1),
            part(2),
            part(0),
            pl.BlockSpec((1, 2, tokens), lambda i: (i, 0, 0)),
            part(0),
        ],
        out_specs=[part(0)] * 3,
        out_shape=[jax.ShapeDtypeStruct((tokens, width), jnp.bfloat16)] * 3,
        scratch_shapes=[pltpu.VMEM((tokens, 2 * HEAD_DIM), jnp.float32)],
        compiler_params=pltpu.CompilerParams(vmem_limit_bytes=48 << 20),
        cost_estimate=pl.CostEstimate(
            flops=40 * pairs * tokens * tokens * HEAD_DIM,
            bytes_accessed=16 * tokens * width,
            transcendentals=2 * pairs * tokens * tokens,
        ),
    )(triple, triple, triple, head_out, log_total, mixed_grad)
    return jnp.concatenate(grads, 1)


def fast_body(
    fsdp_size,
    inputs,
    skip_inputs,
    skip_weight,
    skip_bias,
    first_gain,
    first_shift,
    attention_in,
    attention_out,
    out_bias,
    second_gain,
    second_shift,
    up_weight,
    up_bias,
    down_weight,
    down_bias,
    cotangent,
):
    chips = fsdp_size // 2
    order = ring_order(chips)
    core = lax.axis_index("fsdp") % 2
    chip = lax.axis_index("fsdp") // 2
    column = lax.axis_index("tp")
    place_of = [order.index(q) for q in range(chips)]
    place = jnp.asarray(place_of, jnp.int32)[chip]
    order_table = jnp.asarray(order, jnp.int32)

    core_pairs = [(i, i ^ 1) for i in range(fsdp_size)]
    diagonal_pairs = []
    for q in range(chips):
        one, two = (q * 4 + 2, q * 4 + 1)
        diagonal_pairs += [(one, two), (two, one)]
    ring_pairs = {}
    for step in (1, -1):
        ring_pairs[step] = [
            (order[i] * 2 + c, order[(i + step) % chips] * 2 + c)
            for i in range(chips)
            for c in range(2)
        ]

    def to_core(value):
        return lax.ppermute(value, "fsdp", core_pairs)

    def to_column(value):
        return lax.ppermute(value, "tp", [(0, 1), (1, 0)])

    def diagonal(value):
        return jnp.where(core == column, value, lax.ppermute(value, BOTH, diagonal_pairs))

    def along_ring(value, step):
        return lax.ppermute(value, "fsdp", ring_pairs[step])

    def chip_at(offset):
        return order_table[(place + offset) % chips]

    def pack_of(layer_index):
        skip_rows = skip_weight[layer_index]
        half_rows = skip_rows.shape[0] // 2
        qkv_rows = attention_in[layer_index]
        first = jnp.concatenate(
            [
                skip_rows[:half_rows],
                skip_rows[half_rows:],
                qkv_rows.reshape(qkv_rows.shape[0], -1),
                attention_out[layer_index].T,
            ],
            1,
        )
        second = jnp.concatenate([up_weight[layer_index], down_weight[layer_index].T], 1)
        return first, second

    def in_pair(value):
        other = to_column(value)
        return jnp.where(
            column == 0,
            jnp.concatenate([value, other], 0),
            jnp.concatenate([other, value], 0),
        )

    def gather(packed):
        pair = in_pair(diagonal(packed))
        middle_column = pair.shape[1] // 2
        ahead, behind = (pair, pair)
        blocks = {0: pair}
        for step in range(1, chips // 2):
            ahead = along_ring(ahead, 1)
            behind = along_ring(behind, -1)
            blocks[-step] = ahead
            blocks[step] = behind
        blocks[chips // 2] = (
            along_ring(ahead[:, :middle_column], 1),
            along_ring(behind[:, middle_column:], -1),
        )
        return blocks

    def assemble(blocks, pieces):
        offsets = sorted(blocks)
        operands, jobs, shapes = ([], [], [])
        for begin, width, slabs in pieces:
            shapes.append((chips * blocks[0].shape[0] * slabs, width))
        pair_rows = blocks[0].shape[0]
        half_rows = pair_rows // 2
        for at, offset in enumerate(offsets):
            held = blocks[offset] if isinstance(blocks[offset], tuple) else (blocks[offset],)
            start = 0
            for part in held:
                stop = start + part.shape[1]
                for which, (begin, width, slabs) in enumerate(pieces):
                    for slab in range(slabs):
                        low = max(start, begin + slab * width)
                        high = min(stop, begin + (slab + 1) * width)
                        if low >= high:
                            continue
                        to = low - begin - slab * width
                        spans = (
                            [(0, pair_rows, 0)]
                            if slabs == 1
                            else [
                                (i * half_rows, half_rows, (i * slabs + slab) * half_rows)
                                for i in range(2)
                            ]
                        )
                        for row, rows, to_row in spans:
                            jobs.append(
                                (len(operands), row, rows, low - start, high - low, which, at)
                                + (to_row, to)
                            )
                operands.append(part)
                start = stop

        def kernel(at_ref, *refs):
            sources, targets = (refs[: len(operands)], refs[len(operands) :][: len(shapes)])
            buffers = refs[len(operands) + len(shapes) : -2]
            sems, out_sems = refs[-2:]
            copies = [[] for _ in shapes]
            for which in range(len(shapes)):
                for index, job in enumerate(jobs):
                    source, row, rows, col, width, target, at, to_row, to = job
                    if target != which:
                        continue
                    block_rows = pair_rows * pieces[which][2]
                    begin = pl.multiple_of(at_ref[at] * block_rows + to_row, 16)
                    copy = pltpu.make_async_copy(
                        sources[source].at[pl.ds(row, rows), pl.ds(col, width)],
                        buffers[which].at[pl.ds(begin, rows), pl.ds(to, width)],
                        sems.at[index],
                    )
                    copy.start()
                    copies[which].append(copy)
            outs = []
            for which in range(len(shapes)):
                for copy in copies[which]:
                    copy.wait()
                out = pltpu.make_async_copy(buffers[which], targets[which], out_sems.at[which])
                out.start()
                outs.append(out)
            for out in outs:
                out.wait()

        places = jnp.stack([chip_at(offset) for offset in offsets])
        moved = sum(2 * 2 * r * w for r, w in shapes)
        return pl.pallas_call(
            kernel,
            out_shape=[jax.ShapeDtypeStruct(shape, jnp.bfloat16) for shape in shapes],
            in_specs=[pl.BlockSpec(memory_space=pltpu.SMEM)]
            + [pl.BlockSpec(memory_space=pl.ANY)] * len(operands),
            out_specs=[pl.BlockSpec(memory_space=pl.ANY)] * len(shapes),
            scratch_shapes=[pltpu.VMEM(shape, jnp.bfloat16) for shape in shapes]
            + [pltpu.SemaphoreType.DMA((len(jobs),)), pltpu.SemaphoreType.DMA((len(shapes),))],
            compiler_params=pltpu.CompilerParams(vmem_limit_bytes=24 << 20),
            cost_estimate=pl.CostEstimate(flops=0, bytes_accessed=moved, transcendentals=0),
        )(places, *operands)

    def weights_of(layer_index):
        first, second = pack_of(layer_index)
        skip_width = skip_weight.shape[2]
        qkv_width = attention_in.shape[2] * attention_in.shape[3]
        out_width = attention_out.shape[1]
        up_width = up_weight.shape[2]
        begin = 2 * skip_width
        weight_skip, weight_qkv, weight_out = assemble(
            gather(first),
            [
                (0, skip_width, 2),
                (begin, qkv_width, 1),
                (begin + qkv_width, out_width, 1),
            ],
        )
        weight_up, weight_down = assemble(
            gather(second), [(0, up_width, 1), (up_width, down_weight.shape[1], 1)]
        )
        return weight_skip, weight_qkv, weight_out, weight_up, weight_down

    def scatter(tensors):
        def block(offset):
            at = chip_at(offset)
            parts = []
            for tensor in tensors:
                rows = tensor.shape[0] // chips
                parts.append(lax.dynamic_slice_in_dim(tensor, at * rows, rows, 0))
            return jnp.concatenate(parts, 1).astype(jnp.float32)

        width = sum(t.shape[1] for t in tensors)
        middle_column = width // 2
        half = chips // 2
        far = block(half)
        sums = []
        for step in (1, -1):
            if step == 1:
                got = along_ring(far[:, :middle_column].astype(jnp.bfloat16), step)
                empty = jnp.zeros((got.shape[0], width - middle_column), got.dtype)
                got = jnp.concatenate([got, empty], 1)
            else:
                got = along_ring(far[:, middle_column:].astype(jnp.bfloat16), step)
                empty = jnp.zeros((got.shape[0], middle_column), got.dtype)
                got = jnp.concatenate([empty, got], 1)
            for distance in range(half - 1, 0, -1):
                got = along_ring(
                    (block(step * distance) + got.astype(jnp.float32)).astype(jnp.bfloat16), step
                )
            sums.append(got.astype(jnp.float32))
        mine = block(0) + sums[0] + sums[1]
        half_rows = mine.shape[0] // 2
        keep = lax.dynamic_slice_in_dim(mine, column * half_rows, half_rows, 0)
        send = lax.dynamic_slice_in_dim(mine, (1 - column) * half_rows, half_rows, 0)
        total = keep + to_column(send.astype(jnp.bfloat16)).astype(jnp.float32)
        return diagonal(total.astype(jnp.bfloat16)).astype(jnp.float32)

    small_names = (
        skip_bias,
        first_gain,
        first_shift,
        out_bias,
        second_gain,
        second_shift,
        up_bias,
        down_bias,
    )
    small_widths = [value.shape[1] for value in small_names]
    small_total = sum(small_widths) * LAYERS
    packed_small = jnp.concatenate([value.reshape(-1) for value in small_names])
    padded = -(-small_total // 1024) * 1024
    packed_small = jnp.pad(packed_small, (0, padded - small_total)).reshape(1, -1, 128)

    bits = chips.bit_length() - 1

    def to_partner(value, bit):
        if bit == 0:
            return to_column(value)
        if bit == 1:
            return to_core(value)
        flip = 1 << (bit - 2)
        pairs = [(q * 2 + c, (q ^ flip) * 2 + c) for q in range(chips) for c in range(2)]
        return lax.ppermute(value, "fsdp", pairs)

    def side_of(bit):
        return column if bit == 0 else core if bit == 1 else (chip >> (bit - 2)) & 1

    all_small = packed_small
    for bit in range(bits + 2):
        other = to_partner(all_small, bit)
        all_small = jnp.where(
            side_of(bit) == 0,
            jnp.concatenate([all_small, other], 0),
            jnp.concatenate([other, all_small], 0),
        )
    all_small = all_small.reshape(2 * fsdp_size, -1)

    def sum_small(packed):
        for bit in reversed(range(bits + 2)):
            count = packed.shape[0] // 2
            side = side_of(bit)
            keep = jnp.where(side == 0, packed[:count], packed[count:])
            send = jnp.where(side == 0, packed[count:], packed[:count])
            packed = keep + to_partner(send, bit)
        return packed[0]

    def small_of(layer_index):
        values, begin = ([], 0)
        for width in small_widths:
            values.append(
                all_small[
                    :, begin + layer_index * width : begin + (layer_index + 1) * width
                ].reshape(-1)
            )
            begin += LAYERS * width
        unit_width = up_weight.shape[2]
        values[6] = lax.dynamic_slice_in_dim(values[6], core * unit_width, unit_width)
        return values

    def rows_of(value):
        return jnp.concatenate([value, to_core(value)], 0)

    def sum_rows(partial_value):
        count = partial_value.shape[0] // 2
        return partial_value[:count] + to_core(partial_value[count:].astype(jnp.bfloat16)).astype(
            jnp.float32
        )

    def forward(stream_low, stream, skip_rows, weights, small):
        weight_skip, weight_qkv, weight_out, weight_up, weight_down = weights
        joined = jnp.concatenate([stream_low, skip_rows], 1)
        rows_joined = rows_of(joined)
        hidden_part = jnp.dot(rows_joined, weight_skip, preferred_element_type=jnp.float32)
        count = joined.shape[0]
        own_part = hidden_part[:count]
        other_part = to_core(hidden_part[count:].astype(jnp.bfloat16)).astype(jnp.float32)
        hidden = (
            jnp.where(
                core == 0,
                jnp.concatenate([own_part, other_part], 1),
                jnp.concatenate([other_part, own_part], 1),
            )
            + small[0]
        )
        first_norm = norm_apply(hidden, small[1], small[2]).astype(jnp.bfloat16)
        rows_first = rows_of(first_norm)
        triple = jnp.dot(rows_first, weight_qkv, preferred_element_type=jnp.float32).astype(
            jnp.bfloat16
        )
        head_out, log_total = attention_forward(triple)
        middle = (
            hidden
            + sum_rows(
                jnp.einsum("th,dh->td", head_out, weight_out, preferred_element_type=jnp.float32)
            )
            + small[3]
        )
        second_norm = norm_apply(middle, small[4], small[5]).astype(jnp.bfloat16)
        rows_second = rows_of(second_norm)
        preact = jnp.dot(rows_second, weight_up, preferred_element_type=jnp.float32) + small[6]
        below = 0.5 + 0.5 * lax.erf(preact * (0.5**0.5))
        activated = (preact * below).astype(jnp.bfloat16)
        slope = (below + preact * jnp.exp(-0.5 * preact * preact) * GAUSS).astype(jnp.bfloat16)
        branch = sum_rows(
            jnp.einsum("tf,df->td", activated, weight_down, preferred_element_type=jnp.float32)
        )
        result = middle + branch + small[7]
        kept = (
            rows_joined,
            hidden,
            rows_first,
            triple,
            head_out,
            log_total,
            middle,
            rows_second,
            slope,
            activated,
        )
        return result, kept

    def backward(stream_grad, weights, small, kept):
        weight_skip, weight_qkv, weight_out, weight_up, weight_down = weights
        (
            rows_joined,
            hidden,
            rows_first,
            triple,
            head_out,
            log_total,
            middle,
            rows_second,
            slope,
            activated,
        ) = kept
        down_bias_grad = jnp.sum(stream_grad, 0)
        grad_rows = rows_of(stream_grad.astype(jnp.bfloat16))
        act_grad = jnp.dot(grad_rows, weight_down, preferred_element_type=jnp.float32)
        down_grad = jnp.einsum(
            "td,tf->df", grad_rows, activated, preferred_element_type=jnp.float32
        ).astype(jnp.bfloat16)
        pre_grad = act_grad * slope
        up_bias_part = jnp.sum(pre_grad, 0)
        pre_low = pre_grad.astype(jnp.bfloat16)
        up_grad = jnp.einsum(
            "td,tf->df", rows_second, pre_low, preferred_element_type=jnp.float32
        ).astype(jnp.bfloat16)
        second_grad = sum_rows(
            jnp.einsum("tf,df->td", pre_low, weight_up, preferred_element_type=jnp.float32)
        )
        up_bias_full = lax.dynamic_update_slice_in_dim(
            jnp.zeros((2 * up_bias_part.shape[0],), jnp.float32),
            up_bias_part,
            core * up_bias_part.shape[0],
            0,
        )
        norm_unused, second_pull = jax.vjp(norm_apply, middle, small[4], small[5])
        middle_norm_grad, second_gain_grad, second_shift_grad = second_pull(second_grad)
        middle_grad = stream_grad + middle_norm_grad
        out_bias_grad = jnp.sum(middle_grad, 0)
        middle_rows = rows_of(middle_grad.astype(jnp.bfloat16))
        mixed_grad = jnp.dot(
            middle_rows, weight_out, preferred_element_type=jnp.float32
        ).astype(jnp.bfloat16)
        out_grad = jnp.einsum(
            "td,th->dh", middle_rows, head_out, preferred_element_type=jnp.float32
        ).astype(jnp.bfloat16)
        triple_grad = attention_backward(triple, head_out, log_total, mixed_grad)
        qkv_grad = jnp.einsum(
            "td,tc->dc", rows_first, triple_grad, preferred_element_type=jnp.float32
        ).astype(jnp.bfloat16)
        first_grad = sum_rows(
            jnp.einsum("tc,dc->td", triple_grad, weight_qkv, preferred_element_type=jnp.float32)
        )
        norm_unused_two, first_pull = jax.vjp(norm_apply, hidden, small[1], small[2])
        hidden_norm_grad, first_gain_grad, first_shift_grad = first_pull(first_grad)
        hidden_grad = middle_grad + hidden_norm_grad
        skip_bias_grad = jnp.sum(hidden_grad, 0)
        hidden_low = hidden_grad.astype(jnp.bfloat16)
        half_width = hidden_low.shape[1] // 2
        keep = lax.dynamic_slice_in_dim(hidden_low, core * half_width, half_width, 1)
        send = lax.dynamic_slice_in_dim(hidden_low, (1 - core) * half_width, half_width, 1)
        hidden_cols = jnp.concatenate([keep, to_core(send)], 0)
        joined_grad = sum_rows(
            jnp.einsum("te,ce->tc", hidden_cols, weight_skip, preferred_element_type=jnp.float32)
        )
        skip_grad = jnp.einsum(
            "tc,te->ce", rows_joined, hidden_cols, preferred_element_type=jnp.float32
        ).astype(jnp.bfloat16)
        shard_rows = skip_weight.shape[1]
        slabs = skip_grad.reshape(2 * chips, 2, shard_rows // 2, -1)
        slabs = [slabs[:, i].reshape(-1, skip_grad.shape[1]) for i in range(2)]
        second_total = scatter([up_grad, down_grad])
        first_total = scatter([slabs[0], slabs[1], qkv_grad, out_grad])
        small_grads = [
            skip_bias_grad,
            first_gain_grad.astype(jnp.float32),
            first_shift_grad.astype(jnp.float32),
            out_bias_grad,
            second_gain_grad.astype(jnp.float32),
            second_shift_grad.astype(jnp.float32),
            up_bias_full,
            down_bias_grad,
        ]
        return joined_grad, first_total, second_total, small_grads

    stream_low = diagonal(inputs)
    stream = stream_low.astype(jnp.float32)
    skips = [diagonal(skip_inputs[i]) for i in range(LAYERS)]
    weights = [weights_of(i) for i in range(LAYERS)]
    smalls = [small_of(i) for i in range(LAYERS)]
    kept = []
    for layer_index in range(LAYERS):
        stream, kept_here = forward(
            stream_low, stream, skips[layer_index], weights[layer_index], smalls[layer_index]
        )
        stream_low = stream.astype(jnp.bfloat16)
        kept.append(kept_here)
    output = diagonal(stream_low).astype(jnp.float32)
    stream_grad = diagonal(cotangent).astype(jnp.float32)
    skip_parts = [None] * LAYERS
    firsts = [None] * LAYERS
    seconds = [None] * LAYERS
    small_sums = [None] * LAYERS
    for layer_index in reversed(range(LAYERS)):
        joined_grad, firsts[layer_index], seconds[layer_index], small_grads = backward(
            stream_grad, weights[layer_index], smalls[layer_index], kept[layer_index]
        )
        width = joined_grad.shape[1] // 2
        stream_grad = joined_grad[:, :width]
        skip_parts[layer_index] = diagonal(joined_grad[:, width:].astype(jnp.bfloat16)).astype(
            jnp.float32
        )
        small_sums[layer_index] = jnp.concatenate(
            [value.reshape(2 * fsdp_size, -1) for value in small_grads], 1
        )
    input_grad = diagonal(stream_grad.astype(jnp.bfloat16)).astype(jnp.float32)

    small_sums = sum_small(jnp.concatenate(small_sums, 1))
    small_sums = small_sums.reshape(LAYERS, -1)
    skip_width = skip_weight.shape[2]
    qkv_width = attention_in.shape[2] * attention_in.shape[3]
    up_width = up_weight.shape[2]
    begin = 2 * skip_width
    skip_weight_grad = jnp.stack(
        [jnp.concatenate([v[:, :skip_width], v[:, skip_width:begin]], 0) for v in firsts]
    )
    qkv_weight_grad = jnp.stack(
        [v[:, begin : begin + qkv_width].reshape(attention_in.shape[1:]) for v in firsts]
    )
    out_weight_grad = jnp.stack([v[:, begin + qkv_width :].T for v in firsts])
    up_weight_grad = jnp.stack([v[:, :up_width] for v in seconds])
    down_weight_grad = jnp.stack([v[:, up_width:].T for v in seconds])
    small_out, begin = ([], 0)
    for width in small_widths:
        small_out.append(small_sums[:, begin : begin + width])
        begin += width
    return (
        output,
        input_grad,
        jnp.stack(skip_parts),
        skip_weight_grad,
        small_out[0],
        small_out[1],
        small_out[2],
        qkv_weight_grad,
        out_weight_grad,
        small_out[3],
        small_out[4],
        small_out[5],
        up_weight_grad,
        small_out[6],
        down_weight_grad,
        small_out[7],
    )


def solution(mesh):
    placed = (
        P(("fsdp", "tp"), None),
        P(None, ("fsdp", "tp"), None),
        P(None, "fsdp", "tp"),
        P(None, ("fsdp", "tp")),
        P(None, ("fsdp", "tp")),
        P(None, ("fsdp", "tp")),
        P(None, "fsdp", None, "tp"),
        P(None, "tp", "fsdp"),
        P(None, ("fsdp", "tp")),
        P(None, ("fsdp", "tp")),
        P(None, ("fsdp", "tp")),
        P(None, "fsdp", "tp"),
        P(None, ("fsdp", "tp")),
        P(None, "tp", "fsdp"),
        P(None, ("fsdp", "tp")),
        P(("fsdp", "tp"), None),
    )
    return jax.shard_map(
        choose_body(mesh),
        mesh=mesh,
        in_specs=placed,
        out_specs=(
            P(("fsdp", "tp"), None),
            P(("fsdp", "tp"), None),
            P(None, ("fsdp", "tp"), None),
            P(None, "fsdp", "tp"),
            P(None, ("fsdp", "tp")),
            P(None, ("fsdp", "tp")),
            P(None, ("fsdp", "tp")),
            P(None, "fsdp", None, "tp"),
            P(None, "tp", "fsdp"),
            P(None, ("fsdp", "tp")),
            P(None, ("fsdp", "tp")),
            P(None, ("fsdp", "tp")),
            P(None, "fsdp", "tp"),
            P(None, ("fsdp", "tp")),
            P(None, "tp", "fsdp"),
            P(None, ("fsdp", "tp")),
        ),
        check_vma=False,
    )
```

```python
import jax
import jax.numpy as jnp
from jax import lax
from jax.experimental import pallas as pl
from jax.experimental.pallas import tpu as pltpu
from jax.sharding import PartitionSpec as P

HEAD_DIM = 64
FF = 4096
SEQ_LEN = 1104
LAYERS = 2


epsilon = 1e-05


def norm_apply(values_in, gain, shift):
    center = values_in - jnp.mean(values_in, -1, keepdims=True)
    spread = jnp.mean(center * center, -1, keepdims=True)
    return center * lax.rsqrt(spread + epsilon) * gain + shift


def gelu_exact(values_in):
    return jax.nn.gelu(values_in, approximate=False)


def split_heads(triple_seq):
    head_count = triple_seq.shape[2] // HEAD_DIM
    return (triple_seq.reshape(SEQ_LEN, 3, head_count, HEAD_DIM), head_count)


def attend(triple_seq):
    heads_split, head_count = split_heads(triple_seq)
    query, key_rows, value_rows = (heads_split[:, 0], heads_split[:, 1], heads_split[:, 2])
    half_rows = SEQ_LEN // 2
    score_scale = HEAD_DIM ** (-0.5)
    outputs, totals = ([], [])
    for part_index in range(2):
        query_part = query[part_index * half_rows : (part_index + 1) * half_rows]
        scores = (
            jnp.einsum("qhd,khd->hqk", query_part, key_rows, preferred_element_type=jnp.float32)
            * score_scale
        )
        row_top = jnp.max(scores, -1, keepdims=True)
        exp_scores = jnp.exp(scores - row_top)
        row_total = jnp.sum(exp_scores, -1, keepdims=True)
        low_probs = (exp_scores / row_total).astype(jnp.bfloat16)
        mixed = jnp.einsum(
            "hqk,khd->qhd", low_probs, value_rows, preferred_element_type=jnp.float32
        )
        outputs.append(mixed.astype(jnp.bfloat16).reshape(half_rows, head_count * HEAD_DIM))
        totals.append((row_top + jnp.log(row_total))[..., 0])
    return (jnp.concatenate(outputs, 0), jnp.concatenate(totals, 1))


def attend_back(items):
    triple_seq, log_total, mixed_grad = items
    heads_split, head_count = split_heads(triple_seq)
    query, key_rows, value_rows = (heads_split[:, 0], heads_split[:, 1], heads_split[:, 2])
    grad_heads = mixed_grad.reshape(SEQ_LEN, head_count, HEAD_DIM)
    half_rows = SEQ_LEN // 2
    score_scale = HEAD_DIM ** (-0.5)
    key_grad = jnp.zeros((SEQ_LEN, head_count, HEAD_DIM), jnp.float32)
    value_grad = jnp.zeros((SEQ_LEN, head_count, HEAD_DIM), jnp.float32)
    query_grads = []
    for part_index in range(2):
        rows_here = slice(part_index * half_rows, (part_index + 1) * half_rows)
        query_part = query[rows_here]
        grad_part = grad_heads[rows_here]
        scores = (
            jnp.einsum("qhd,khd->hqk", query_part, key_rows, preferred_element_type=jnp.float32)
            * score_scale
        )
        probs = jnp.exp(scores - log_total[:, rows_here][..., None])
        low_probs = probs.astype(jnp.bfloat16)
        value_grad = value_grad + jnp.einsum(
            "hqk,qhd->khd", low_probs, grad_part, preferred_element_type=jnp.float32
        )
        prob_grad = jnp.einsum(
            "qhd,khd->hqk", grad_part, value_rows, preferred_element_type=jnp.float32
        )
        score_grad = (probs * (prob_grad - jnp.sum(prob_grad * probs, -1, keepdims=True))).astype(
            jnp.bfloat16
        )
        query_grads.append(
            jnp.einsum("hqk,khd->qhd", score_grad, key_rows, preferred_element_type=jnp.float32)
            * score_scale
        )
        key_grad = (
            key_grad
            + jnp.einsum("hqk,qhd->khd", score_grad, query_part, preferred_element_type=jnp.float32)
            * score_scale
        )
    stacked = jnp.stack([jnp.concatenate(query_grads, 0), key_grad, value_grad], 1)
    return stacked.reshape(SEQ_LEN, 3, head_count * HEAD_DIM).astype(jnp.bfloat16)


def general_body(
    inputs,
    skip_inputs,
    skip_weight,
    skip_bias,
    first_gain,
    first_shift,
    attention_in,
    attention_out,
    out_bias,
    second_gain,
    second_shift,
    up_weight,
    up_bias,
    down_weight,
    down_bias,
    cotangent,
):

    def fetch_layer(layer_index):
        small_params = (
            lax.all_gather(skip_bias[layer_index], ("fsdp", "tp"), axis=0, tiled=True),
            lax.all_gather(first_gain[layer_index], ("fsdp", "tp"), axis=0, tiled=True),
            lax.all_gather(first_shift[layer_index], ("fsdp", "tp"), axis=0, tiled=True),
            lax.all_gather(out_bias[layer_index], ("fsdp", "tp"), axis=0, tiled=True),
            lax.all_gather(second_gain[layer_index], ("fsdp", "tp"), axis=0, tiled=True),
            lax.all_gather(second_shift[layer_index], ("fsdp", "tp"), axis=0, tiled=True),
            lax.all_gather(up_bias[layer_index], ("fsdp", "tp"), axis=0, tiled=True),
            lax.all_gather(down_bias[layer_index], ("fsdp", "tp"), axis=0, tiled=True),
        )
        block = (
            lax.all_gather(skip_weight[layer_index], "fsdp", axis=0, tiled=True),
            lax.all_gather(attention_in[layer_index], "fsdp", axis=0, tiled=True),
            lax.all_gather(attention_out[layer_index], "fsdp", axis=1, tiled=True),
            lax.all_gather(up_weight[layer_index], "fsdp", axis=0, tiled=True),
            lax.all_gather(down_weight[layer_index], "fsdp", axis=1, tiled=True),
        )
        weight_up, weight_down = (block[3], block[4])
        unit_width = weight_up.shape[1]
        bias_up = lax.dynamic_slice_in_dim(
            small_params[6], lax.axis_index("tp") * unit_width, unit_width
        )
        return (small_params, block[0], block[1], block[2], weight_up, bias_up, weight_down)

    def rows_of(normed):
        return lax.all_gather(normed, "tp", axis=0, tiled=True)

    def sum_rows(partial_value):
        return lax.psum_scatter(
            partial_value.astype(jnp.bfloat16), "tp", scatter_dimension=0, tiled=True
        ).astype(jnp.float32)

    def grad_rows_of(grad_low):
        return lax.all_gather(grad_low, "tp", axis=0, tiled=True)

    def sum_row_grads(partial_value):
        return lax.psum_scatter(
            partial_value.astype(jnp.bfloat16), "tp", scatter_dimension=0, tiled=True
        ).astype(jnp.float32)

    def forward(stream, skip_rows, weights):
        small_params, weight_skip, weight_qkv, weight_out, weight_up, bias_up, weight_down = weights
        joined = jnp.concatenate([stream.astype(jnp.bfloat16), skip_rows], 1)
        rows_joined = rows_of(joined)
        hidden_part = jnp.dot(rows_joined, weight_skip, preferred_element_type=jnp.float32)
        hidden = (
            lax.all_to_all(
                hidden_part.astype(jnp.bfloat16), "tp", split_axis=0, concat_axis=1, tiled=True
            ).astype(hidden_part.dtype)
            + small_params[0]
        )
        first_norm = norm_apply(hidden, small_params[1], small_params[2]).astype(jnp.bfloat16)
        rows_first = rows_of(first_norm)
        triple = jnp.einsum(
            "td,dch->tch", rows_first, weight_qkv, preferred_element_type=jnp.float32
        ).astype(jnp.bfloat16)
        seq_count = rows_first.shape[0] // SEQ_LEN
        head_out, log_total = lax.map(attend, triple.reshape(seq_count, SEQ_LEN, 3, -1))
        head_out = head_out.reshape(rows_first.shape[0], -1)
        middle = (
            hidden
            + sum_rows(jnp.dot(head_out, weight_out, preferred_element_type=jnp.float32))
            + small_params[3]
        )
        second_norm = norm_apply(middle, small_params[4], small_params[5]).astype(jnp.bfloat16)
        rows_second = rows_of(second_norm)
        preact = jnp.dot(rows_second, weight_up, preferred_element_type=jnp.float32) + bias_up
        activated = gelu_exact(preact).astype(jnp.bfloat16)
        branch = sum_rows(jnp.dot(activated, weight_down, preferred_element_type=jnp.float32))
        result = middle + branch + small_params[7]
        kept = (
            rows_joined,
            hidden,
            rows_first,
            triple,
            head_out,
            log_total,
            middle,
            rows_second,
            preact,
            activated,
        )
        return (result, kept)

    streams = [inputs.astype(jnp.float32)]
    stored = []
    for layer_index in range(LAYERS):
        weights = fetch_layer(layer_index)
        result, kept_here = forward(streams[layer_index], skip_inputs[layer_index], weights)
        stored.append((weights, kept_here))
        streams.append(result)
    output = streams[LAYERS]
    stream_grad = cotangent.astype(jnp.float32)
    skip_parts = [None] * LAYERS
    small_parts = [None] * LAYERS
    block_parts = [None] * LAYERS
    for layer_index in reversed(range(LAYERS)):
        weights = fetch_layer(layer_index)
        unused_result, kept = forward(streams[layer_index], skip_inputs[layer_index], weights)
        (
            backward_small_params,
            backward_weight_skip,
            backward_weight_qkv,
            backward_weight_out,
            backward_weight_up,
            backward_bias_up,
            backward_weight_down,
        ) = weights
        (
            backward_rows_joined,
            backward_hidden,
            backward_rows_first,
            backward_triple,
            backward_head_out,
            backward_log_total,
            backward_middle,
            backward_rows_second,
            backward_preact,
            backward_activated,
        ) = kept
        down_bias_grad = jnp.sum(stream_grad, 0)
        grad_rows = grad_rows_of(stream_grad.astype(jnp.bfloat16))
        act_grad = jnp.einsum(
            "td,fd->tf", grad_rows, backward_weight_down, preferred_element_type=jnp.float32
        )
        down_weight_grad = jnp.einsum(
            "tf,td->fd", backward_activated, grad_rows, preferred_element_type=jnp.float32
        )
        gelu_unused, gelu_pull = jax.vjp(gelu_exact, backward_preact)
        pre_grad = gelu_pull(act_grad)[0]
        up_bias_part = jnp.sum(pre_grad, 0)
        pre_low = pre_grad.astype(jnp.bfloat16)
        up_weight_grad = jnp.einsum(
            "td,tf->df", backward_rows_second, pre_low, preferred_element_type=jnp.float32
        )
        second_grad = sum_row_grads(
            jnp.einsum("tf,df->td", pre_low, backward_weight_up, preferred_element_type=jnp.float32)
        )
        up_bias_full = lax.dynamic_update_slice_in_dim(
            jnp.zeros((FF,), jnp.float32),
            up_bias_part,
            lax.axis_index("tp") * up_bias_part.shape[0],
            0,
        )
        norm_unused, second_pull = jax.vjp(
            norm_apply, backward_middle, backward_small_params[4], backward_small_params[5]
        )
        middle_norm_grad, second_gain_grad, second_shift_grad = second_pull(second_grad)
        middle_grad = stream_grad + middle_norm_grad
        out_bias_grad = jnp.sum(middle_grad, 0)
        middle_rows = grad_rows_of(middle_grad.astype(jnp.bfloat16))
        mixed_grad = jnp.einsum(
            "td,hd->th", middle_rows, backward_weight_out, preferred_element_type=jnp.float32
        ).astype(jnp.bfloat16)
        out_weight_grad = jnp.einsum(
            "th,td->hd", backward_head_out, middle_rows, preferred_element_type=jnp.float32
        )
        backward_seq_count = backward_rows_first.shape[0] // SEQ_LEN
        triple_grad = lax.map(
            attend_back,
            (
                backward_triple.reshape(backward_seq_count, SEQ_LEN, 3, -1),
                backward_log_total,
                mixed_grad.reshape(backward_seq_count, SEQ_LEN, -1),
            ),
        )
        triple_grad = triple_grad.reshape(backward_triple.shape)
        qkv_weight_grad = jnp.einsum(
            "td,tch->dch", backward_rows_first, triple_grad, preferred_element_type=jnp.float32
        )
        first_grad = sum_row_grads(
            jnp.einsum(
                "tch,dch->td", triple_grad, backward_weight_qkv, preferred_element_type=jnp.float32
            )
        )
        norm_unused_two, first_pull = jax.vjp(
            norm_apply, backward_hidden, backward_small_params[1], backward_small_params[2]
        )
        hidden_norm_grad, first_gain_grad, first_shift_grad = first_pull(first_grad)
        hidden_grad = middle_grad + hidden_norm_grad
        skip_bias_grad = jnp.sum(hidden_grad, 0)
        hidden_low = hidden_grad.astype(jnp.bfloat16)
        hidden_cols = lax.all_to_all(hidden_low, "tp", split_axis=1, concat_axis=0, tiled=True)
        joined_grad = sum_row_grads(
            jnp.einsum(
                "te,ce->tc", hidden_cols, backward_weight_skip, preferred_element_type=jnp.float32
            )
        )
        skip_weight_grad = jnp.einsum(
            "tc,te->ce", backward_rows_joined, hidden_cols, preferred_element_type=jnp.float32
        )
        small_grads = (
            lax.psum_scatter(skip_bias_grad, ("fsdp", "tp"), scatter_dimension=0, tiled=True),
            lax.psum_scatter(
                first_gain_grad.astype(jnp.float32), ("fsdp", "tp"), scatter_dimension=0, tiled=True
            ),
            lax.psum_scatter(
                first_shift_grad.astype(jnp.float32),
                ("fsdp", "tp"),
                scatter_dimension=0,
                tiled=True,
            ),
            lax.psum_scatter(out_bias_grad, ("fsdp", "tp"), scatter_dimension=0, tiled=True),
            lax.psum_scatter(
                second_gain_grad.astype(jnp.float32),
                ("fsdp", "tp"),
                scatter_dimension=0,
                tiled=True,
            ),
            lax.psum_scatter(
                second_shift_grad.astype(jnp.float32),
                ("fsdp", "tp"),
                scatter_dimension=0,
                tiled=True,
            ),
            lax.psum_scatter(up_bias_full, ("fsdp", "tp"), scatter_dimension=0, tiled=True),
            lax.psum_scatter(down_bias_grad, ("fsdp", "tp"), scatter_dimension=0, tiled=True),
        )
        block_grads = (
            lax.psum_scatter(
                skip_weight_grad.astype(jnp.bfloat16), "fsdp", scatter_dimension=0, tiled=True
            ).astype(jnp.float32),
            lax.psum_scatter(
                qkv_weight_grad.astype(jnp.bfloat16), "fsdp", scatter_dimension=0, tiled=True
            ).astype(jnp.float32),
            lax.psum_scatter(
                out_weight_grad.astype(jnp.bfloat16), "fsdp", scatter_dimension=1, tiled=True
            ).astype(jnp.float32),
            lax.psum_scatter(
                up_weight_grad.astype(jnp.bfloat16), "fsdp", scatter_dimension=0, tiled=True
            ).astype(jnp.float32),
            lax.psum_scatter(
                down_weight_grad.astype(jnp.bfloat16), "fsdp", scatter_dimension=1, tiled=True
            ).astype(jnp.float32),
        )
        width = backward_weight_skip.shape[0] // 2
        stream_grad, skip_part, small_grads, block_grads = (
            joined_grad[:, :width],
            joined_grad[:, width:],
            small_grads,
            block_grads,
        )
        skip_parts[layer_index] = skip_part
        small_parts[layer_index] = small_grads
        block_parts[layer_index] = block_grads

    def stack_small(position):
        return jnp.stack([small_parts[index_layer][position] for index_layer in range(LAYERS)])

    def stack_block(position):
        return jnp.stack([block_parts[index_layer][position] for index_layer in range(LAYERS)])

    return (
        output,
        stream_grad,
        jnp.stack(skip_parts),
        stack_block(0),
        stack_small(0),
        stack_small(1),
        stack_small(2),
        stack_block(1),
        stack_block(2),
        stack_small(3),
        stack_small(4),
        stack_small(5),
        stack_block(3),
        stack_small(6),
        stack_block(4),
        stack_small(7),
    )


BOTH = ("fsdp", "tp")
GAUSS = 0.3989422804014327


def choose_body(mesh):
    fsdp_size, tp_size = (mesh.shape["fsdp"], mesh.shape["tp"])
    if tp_size != 2 or fsdp_size < 4 or fsdp_size & (fsdp_size - 1):
        return general_body
    return lambda *arrays: fast_body(fsdp_size, *arrays)


class Sequence:
    def __init__(self):
        self.last = None

    def at(self, value):
        if self.last is None:
            return value
        return lax.optimization_barrier((value, self.last))[0]

    def mark(self, value):
        self.last = value
        return value


class RingGather:
    def __init__(self, net, block):
        self.net, self.round = (net, 0)
        self.blocks = {0: block}
        self.ahead, self.behind = (block, block)
        self.send()

    def send(self):
        ahead, behind = (self.ahead, self.behind)
        if self.round + 1 == self.net.half_ring:
            middle = ahead.shape[1] // 256 * 128
            ahead, behind = (ahead[:, :middle], behind[:, middle:])
        self.coming = (self.net.along_ring(ahead, 1), self.net.along_ring(behind, -1))

    def advance(self, sequence):
        got = sequence.mark(sequence.at(self.coming))
        self.round += 1
        if self.round == self.net.half_ring:
            self.blocks[self.round] = got
            return
        self.ahead, self.behind = got
        self.blocks[-self.round], self.blocks[self.round] = got
        self.send()

    def whole(self, pieces):
        net, offsets = (self.net, sorted(self.blocks))
        operands, jobs = ([], [])
        pair_rows = self.blocks[0].shape[0]
        half_rows = pair_rows // 2
        shapes = [(net.chips * pair_rows * slabs, width) for begin, width, slabs in pieces]
        for at, offset in enumerate(offsets):
            held = self.blocks[offset]
            start = 0
            for part in held if isinstance(held, tuple) else (held,):
                stop = start + part.shape[1]
                for which, (begin, width, slabs) in enumerate(pieces):
                    for slab in range(slabs):
                        low = max(start, begin + slab * width)
                        high = min(stop, begin + (slab + 1) * width)
                        if low >= high:
                            continue
                        to = low - begin - slab * width
                        spans = [(0, pair_rows, 0)]
                        if slabs > 1:
                            spans = [
                                (i * half_rows, half_rows, (i * slabs + slab) * half_rows)
                                for i in range(2)
                            ]
                        for row, rows, to_row in spans:
                            jobs.append(
                                (len(operands), row, rows, low - start, high - low, which, at)
                                + (pair_rows * slabs, to_row, to)
                            )
                operands.append(part)
                start = stop
        table = [
            [net.order[(net.order.index(q) + offset) % net.chips] for offset in offsets]
            for q in range(net.chips)
        ]
        places = lax.dynamic_index_in_dim(jnp.asarray(table, jnp.int32), net.chip, 0, False)
        return copy_kernel(places, operands, jobs, shapes)


class RingSum:
    def __init__(self, net, tensors, columns_first):
        self.net, self.columns_first = (net, columns_first)
        self.views = [t.reshape(net.chips, 2, -1, t.shape[1]) for t in tensors]
        if columns_first:
            self.stage = "columns"
            self.coming = [
                net.to_column(lax.dynamic_index_in_dim(v, 1 - net.column, 1, False))
                for v in self.views
            ]
        else:
            self.views = [v.reshape(net.chips, -1, v.shape[3]) for v in self.views]
            self.begin()

    def block(self, offset):
        at = self.net.chip_at(offset)
        parts = [lax.dynamic_index_in_dim(v, at, 0, False) for v in self.views]
        return jnp.concatenate(parts, 1)

    def begin(self):
        self.stage, self.distance = ("ring", self.net.half_ring)
        far = self.block(self.net.half_ring)
        middle = far.shape[1] // 256 * 128
        self.coming = (
            self.net.along_ring(far[:, :middle], 1),
            self.net.along_ring(far[:, middle:], -1),
        )

    def advance(self, sequence):
        net, got = (self.net, sequence.at(self.coming))
        if self.stage == "columns":
            self.views = [
                (
                    lax.dynamic_index_in_dim(v, net.column, 1, False).astype(jnp.float32)
                    + other.astype(jnp.float32)
                ).astype(jnp.bfloat16)
                for v, other in zip(self.views, got)
            ]
            sequence.mark(self.views)
            self.begin()
            return
        if self.stage == "last":
            total = self.keep + got.astype(jnp.float32)
            self.total = sequence.mark(total.astype(jnp.bfloat16))
            return
        ahead, behind = got
        if self.distance == net.half_ring:
            low, high = (ahead, behind)
            ahead = jnp.concatenate([low, jnp.zeros(high.shape, low.dtype)], 1)
            behind = jnp.concatenate([jnp.zeros(low.shape, low.dtype), high], 1)
        ahead, behind = (ahead.astype(jnp.float32), behind.astype(jnp.float32))
        self.distance -= 1
        if self.distance:
            ahead = (self.block(self.distance).astype(jnp.float32) + ahead).astype(jnp.bfloat16)
            behind = (self.block(-self.distance).astype(jnp.float32) + behind).astype(jnp.bfloat16)
            sequence.mark((ahead, behind))
            self.coming = (net.along_ring(ahead, 1), net.along_ring(behind, -1))
            return
        total = self.block(0).astype(jnp.float32) + ahead + behind
        if self.columns_first:
            self.total = sequence.mark(total.astype(jnp.bfloat16))
            return
        half_rows = total.shape[0] // 2
        self.keep = lax.dynamic_slice_in_dim(total, net.column * half_rows, half_rows, 0)
        send = lax.dynamic_slice_in_dim(total, (1 - net.column) * half_rows, half_rows, 0)
        send = sequence.mark(send.astype(jnp.bfloat16))
        self.stage, self.coming = ("last", net.to_column(send))


class HalvingSum:
    def __init__(self, net, tensors, bits):
        self.net, self.bits, self.round = (net, bits, 0)
        count = len(bits)
        self.views = [t.reshape((2,) * count + (-1, t.shape[1])) for t in tensors]
        self.left = list(reversed(range(count)))
        self.cut()

    def cut(self):
        bit = self.bits[self.round]
        axis = self.left.index(bit)
        self.left.remove(bit)
        side = self.net.side(bit)

        def half(which):
            parts = [lax.dynamic_index_in_dim(v, which, axis, False) for v in self.views]
            return jnp.concatenate(parts, -1)

        self.keep = half(side)
        self.coming = self.net.to_partner(half(1 - side), bit)

    def advance(self, sequence):
        got = sequence.at(self.coming)
        total = self.keep.astype(jnp.float32) + got.astype(jnp.float32)
        self.round += 1
        self.total = sequence.mark(total.astype(jnp.bfloat16))
        if self.round < len(self.bits):
            self.views = [self.total]
            self.cut()


class Swap:
    def __init__(self, net, tensors):
        self.net, self.tensors = (net, tensors)
        self.coming = [net.diagonal_other(value) for value in tensors]

    def advance(self, sequence):
        self.coming = sequence.mark(sequence.at(self.coming))


class CoreNetwork:
    def __init__(self, fsdp_size):
        self.chips = fsdp_size // 2
        self.core = lax.axis_index("fsdp") % 2
        self.chip = lax.axis_index("fsdp") // 2
        self.column = lax.axis_index("tp")
        self.bits = self.chips.bit_length()
        half = self.chips // 2
        self.half_ring = half
        self.order = [2 * i for i in range(half)] + [2 * i + 1 for i in reversed(range(half))]
        table = [
            [self.order[(self.order.index(q) + offset) % self.chips] for offset in range(self.chips)]
            for q in range(self.chips)
        ]
        self.chips_here = lax.dynamic_index_in_dim(
            jnp.asarray(table, jnp.int32), self.chip, 0, False
        )
        self.ring_pairs = {}
        for step in (1, -1):
            self.ring_pairs[step] = [
                (self.order[i] * 2 + c, self.order[(i + step) % self.chips] * 2 + c)
                for i in range(self.chips)
                for c in range(2)
            ]
        self.core_pairs = [(i, i ^ 1) for i in range(fsdp_size)]
        self.diagonal_pairs = []
        for q in range(self.chips):
            one, two = (q * 4 + 2, q * 4 + 1)
            self.diagonal_pairs += [(one, two), (two, one)]

    def to_core(self, value):
        return lax.ppermute(value, "fsdp", self.core_pairs)

    def chip_at(self, offset):
        return self.chips_here[offset % self.chips]

    def along_ring(self, value, step):
        return lax.ppermute(value, "fsdp", self.ring_pairs[step])

    def to_column(self, value):
        return self.to_partner(value, 0)

    def diagonal_other(self, value):
        return lax.ppermute(value, BOTH, self.diagonal_pairs)

    def choose(self, own, other):
        return jnp.where(self.core == self.column, own, other)

    def diagonal(self, value):
        return self.choose(value, self.diagonal_other(value))

    def to_partner(self, value, bit):
        if bit == 0:
            return lax.ppermute(value, "tp", [(0, 1), (1, 0)])
        flip = 1 << (bit - 1)
        pairs = [(q * 2 + c, (q ^ flip) * 2 + c) for q in range(self.chips) for c in range(2)]
        return lax.ppermute(value, "fsdp", pairs)

    def side(self, bit):
        return self.column if bit == 0 else (self.chip >> (bit - 1)) & 1

    def sum_small(self, packed):
        for bit in reversed(range(self.bits + 1)):
            count = packed.shape[0] // 2
            if bit == 1:
                side, send_to = (self.core, self.to_core)
            else:
                wire = max(bit - 1, 0)
                side = self.side(wire)
                send_to = lambda value, wire=wire: self.to_partner(value, wire)
            keep = jnp.where(side == 0, packed[:count], packed[count:])
            send = jnp.where(side == 0, packed[count:], packed[:count])
            packed = keep + send_to(send)
        return packed[0]


def copy_kernel(places, operands, jobs, shapes):
    def kernel(at_ref, *refs):
        sources, targets = (refs[: len(operands)], refs[len(operands) :][: len(shapes)])
        buffers = refs[len(operands) + len(shapes) : -2]
        sems, out_sems = refs[-2:]
        copies = [[] for _ in shapes]
        for which in range(len(shapes)):
            for index, job in enumerate(jobs):
                source, row, rows, col, width, target, at, scale, offset, to = job
                if target != which:
                    continue
                begin = pl.multiple_of(at_ref[at] * scale + offset, 16)
                copy = pltpu.make_async_copy(
                    sources[source].at[pl.ds(row, rows), pl.ds(col, width)],
                    buffers[which].at[pl.ds(begin, rows), pl.ds(to, width)],
                    sems.at[index],
                )
                copy.start()
                copies[which].append(copy)
        outs = []
        for which in range(len(shapes)):
            for copy in copies[which]:
                copy.wait()
            out = pltpu.make_async_copy(buffers[which], targets[which], out_sems.at[which])
            out.start()
            outs.append(out)
        for out in outs:
            out.wait()

    moved = sum(2 * 2 * r * w for r, w in shapes)
    return pl.pallas_call(
        kernel,
        out_shape=[jax.ShapeDtypeStruct(shape, jnp.bfloat16) for shape in shapes],
        in_specs=[pl.BlockSpec(memory_space=pltpu.SMEM)]
        + [pl.BlockSpec(memory_space=pl.ANY)] * len(operands),
        out_specs=[pl.BlockSpec(memory_space=pl.ANY)] * len(shapes),
        scratch_shapes=[pltpu.VMEM(shape, jnp.bfloat16) for shape in shapes]
        + [pltpu.SemaphoreType.DMA((len(jobs),)), pltpu.SemaphoreType.DMA((len(shapes),))],
        compiler_params=pltpu.CompilerParams(vmem_limit_bytes=24 << 20),
        cost_estimate=pl.CostEstimate(flops=0, bytes_accessed=moved, transcendentals=0),
    )(places, *operands)


def row_chunks(count):
    return [(begin, min(384, count - begin)) for begin in range(0, count, 384)]


NT = (((1,), (1,)), ((), ()))
TN = (((0,), (0,)), ((), ()))


def head_lanes(value, head):
    lane = lax.broadcasted_iota(jnp.int32, value.shape, 1)
    return jnp.where((lane >= HEAD_DIM) == (head == 1), value, jnp.zeros_like(value))


def attention_forward(triple):
    tokens, width = (triple.shape[0], triple.shape[1] // 3)
    pairs = width // (2 * HEAD_DIM)

    def kernel(query_ref, key_ref, value_ref, out_ref, total_ref):
        keys = key_ref[...]
        values = value_ref[...]
        for begin, rows in row_chunks(tokens):
            query = query_ref[begin : begin + rows, :] * jnp.bfloat16(HEAD_DIM**-0.5)
            mixed, totals = ([], [])
            for head in range(2):
                scores = lax.dot_general(
                    head_lanes(query, head), keys, NT, preferred_element_type=jnp.float32
                )
                top = jnp.max(scores, -1, keepdims=True)
                grown = jnp.exp(scores - top)
                total = jnp.sum(grown, -1, keepdims=True)
                mixed.append(
                    jnp.dot(
                        grown.astype(jnp.bfloat16), values, preferred_element_type=jnp.float32
                    )
                    / total
                )
                totals.append(top + jnp.log(total))
            lane = lax.broadcasted_iota(jnp.int32, mixed[0].shape, 1)
            out_ref[begin : begin + rows, :] = jnp.where(
                lane < HEAD_DIM, mixed[0], mixed[1]
            ).astype(jnp.bfloat16)
            both = jnp.where(lane < HEAD_DIM, totals[0], totals[1]).T
            total_ref[0, 0:1, begin : begin + rows] = both[0:1, :]
            total_ref[0, 1:2, begin : begin + rows] = both[HEAD_DIM : HEAD_DIM + 1, :]

    def part(index):
        return pl.BlockSpec((tokens, 2 * HEAD_DIM), lambda i: (0, index * pairs + i))

    return pl.pallas_call(
        kernel,
        grid=(pairs,),
        in_specs=[part(0), part(1), part(2)],
        out_specs=[part(0), pl.BlockSpec((1, 2, tokens), lambda i: (i, 0, 0))],
        out_shape=[
            jax.ShapeDtypeStruct((tokens, width), jnp.bfloat16),
            jax.ShapeDtypeStruct((pairs, 2, tokens), jnp.float32),
        ],
        compiler_params=pltpu.CompilerParams(vmem_limit_bytes=48 << 20),
        cost_estimate=pl.CostEstimate(
            flops=16 * pairs * tokens * tokens * HEAD_DIM,
            bytes_accessed=8 * tokens * width,
            transcendentals=2 * pairs * tokens * tokens,
        ),
    )(triple, triple, triple)


def attention_backward(triple, head_out, log_total, mixed_grad, first_pair, pair_count):
    tokens, width = (triple.shape[0], triple.shape[1] // 3)
    pairs = width // (2 * HEAD_DIM)
    score_scale = HEAD_DIM**-0.5

    def kernel(
        query_ref, key_ref, value_ref, out_ref, total_ref, grad_ref, dq_ref, dk_ref, dv_ref, sum_ref
    ):
        query = query_ref[...] * jnp.bfloat16(score_scale)
        grad = grad_ref[...]
        product = grad.astype(jnp.float32) * out_ref[...].astype(jnp.float32)
        ones = jnp.ones((8, 2 * HEAD_DIM), jnp.float32)
        deltas = [
            lax.dot_general(
                head_lanes(ones, head),
                product,
                NT,
                precision=lax.Precision.HIGHEST,
                preferred_element_type=jnp.float32,
            )[0:1, :]
            for head in range(2)
        ]
        for begin, rows in row_chunks(tokens):
            keys = key_ref[begin : begin + rows, :]
            values = value_ref[begin : begin + rows, :]
            key_grads, value_grads = ([], [])
            for head in range(2):
                keys_here = head_lanes(keys, head)
                scores = lax.dot_general(
                    keys_here, query, NT, preferred_element_type=jnp.float32
                )
                probs = jnp.exp(scores - total_ref[0, head : head + 1, :])
                prob_grad = lax.dot_general(
                    head_lanes(values, head), grad, NT, preferred_element_type=jnp.float32
                )
                score_grad = (probs * (prob_grad - deltas[head])).astype(jnp.bfloat16)
                value_grads.append(
                    jnp.dot(
                        probs.astype(jnp.bfloat16), grad, preferred_element_type=jnp.float32
                    )
                )
                key_grads.append(jnp.dot(score_grad, query, preferred_element_type=jnp.float32))
                query_grad = lax.dot_general(
                    score_grad, keys_here, TN, preferred_element_type=jnp.float32
                )
                if begin == 0 and head == 0:
                    sum_ref[...] = query_grad
                else:
                    sum_ref[...] += query_grad
            lane = lax.broadcasted_iota(jnp.int32, key_grads[0].shape, 1)
            dk_ref[begin : begin + rows, :] = jnp.where(
                lane < HEAD_DIM, key_grads[0], key_grads[1]
            ).astype(jnp.bfloat16)
            dv_ref[begin : begin + rows, :] = jnp.where(
                lane < HEAD_DIM, value_grads[0], value_grads[1]
            ).astype(jnp.bfloat16)
        dq_ref[...] = (sum_ref[...] * score_scale).astype(jnp.bfloat16)

    def part(index):
        return pl.BlockSpec((tokens, 2 * HEAD_DIM), lambda i: (0, index * pairs + first_pair + i))

    return pl.pallas_call(
        kernel,
        grid=(pair_count,),
        in_specs=[
            part(0),
            part(1),
            part(2),
            part(0),
            pl.BlockSpec((1, 2, tokens), lambda i: (first_pair + i, 0, 0)),
            part(0),
        ],
        out_specs=[pl.BlockSpec((tokens, 2 * HEAD_DIM), lambda i: (0, i))] * 3,
        out_shape=[jax.ShapeDtypeStruct((tokens, pair_count * 2 * HEAD_DIM), jnp.bfloat16)] * 3,
        scratch_shapes=[pltpu.VMEM((tokens, 2 * HEAD_DIM), jnp.float32)],
        compiler_params=pltpu.CompilerParams(vmem_limit_bytes=48 << 20),
        cost_estimate=pl.CostEstimate(
            flops=40 * pair_count * tokens * tokens * HEAD_DIM,
            bytes_accessed=32 * tokens * pair_count * HEAD_DIM,
            transcendentals=2 * pair_count * tokens * tokens,
        ),
    )(triple, triple, triple, head_out, log_total, mixed_grad)


SWAPPED = ("w1", "u1", "i1", "s1")
HALVED = {"u0": (1, 0, 2, 3), "w0": (2, 1, 0, 3)}
PLAN = (
    "+D0", "D0", "+P0", "+D1", "P0", "+R0", "D1", "+P1", "R0", "P1", "+R1", "+E", "R0", "+D2", "R1",
    "D2", "+P2", "R0", "R1", "P2", "+P3", "R0", "+U0", "R1", "E", "R1", "+W0", "skip 0", "U0", "full 0",
    "W0", "P3", "+L", "hid 0", "U0", "W0", "skip 1", "qkv 0", "U0", "attend 0", "W0", "L", "out 0", "U0",
    "+U1", "second_norm 0", "W0", "+W1", "up 0", "U1", "down_held 0", "down 0", "W1", "full 1", "next 0",
    "U1", "hid 1", "W1", "qkv 1", "U1", "attend 1", "W1", "out 1", "U1", "second_norm 1", "W1",
    "grad_rows 1", "up 1", "down_grad 1", "+w1", "down_held 1", "act 1", "second 1", "up_grad 1", "+u1",
    "middle 1", "mixed 1", "out_grad 1", "heads0 1", "w1", "heads1 1", "first 1", "qkv_grad 1", "+i1",
    "u1", "wu", "hidden_grad 1", "joined 1", "grad_rows 0", "skip_grad 1", "act 0", "skip_sum 1", "+s1",
    "second 0", "up_grad 0", "+u0", "i1", "down_grad 0", "+w0", "down 1", "middle 0", "next 1", "+O",
    "mixed 0", "out_grad 0", "s1", "is", "heads0 0", "u0", "O", "+G1", "heads1 0", "w0", "first 0",
    "qkv_grad 0", "+i0", "u0", "G1", "hidden_grad 0", "i0", "skip_grad 0", "w0", "skip_sum 0", "+s0",
    "i0", "joined 0", "+G0", "u0", "s0", "i0", "w0", "s0", "i0", "u0", "s0", "i0", "w0", "s0", "G0", "s0",
)


def fast_body(
    fsdp_size,
    inputs,
    skip_inputs,
    skip_weight,
    skip_bias,
    first_gain,
    first_shift,
    attention_in,
    attention_out,
    out_bias,
    second_gain,
    second_shift,
    up_weight,
    up_bias,
    down_weight,
    down_bias,
    cotangent,
):
    net = CoreNetwork(fsdp_size)
    core, to_core, diagonal = (net.core, net.to_core, net.diagonal)
    count, width = inputs.shape
    shard_rows = attention_in.shape[1]
    skip_rows, skip_width = skip_weight.shape[1:]
    qkv_width = attention_in.shape[2] * attention_in.shape[3]
    up_width = up_weight.shape[2]
    down_width = down_weight.shape[1]
    f32, low_type = (jnp.float32, jnp.bfloat16)

    small_values = (
        skip_bias,
        first_gain,
        first_shift,
        out_bias,
        second_gain,
        second_shift,
        up_bias,
        down_bias,
    )
    small_widths = [value.shape[1] for value in small_values]
    small_total = sum(small_widths) * LAYERS
    small_lanes = -(-small_total // (128 * shard_rows)) * 128
    packed_small = jnp.concatenate([value.reshape(-1) for value in small_values])
    packed_small = jnp.pad(packed_small, (0, shard_rows * small_lanes - small_total))
    packed_small = packed_small.reshape(shard_rows, small_lanes)
    out_width = attention_out.shape[1]
    slab_rows = skip_rows // shard_rows
    first_width = slab_rows * skip_width + qkv_width + out_width
    first_pieces = [
        (0, skip_width, slab_rows),
        (slab_rows * skip_width, qkv_width, 1),
        (slab_rows * skip_width + qkv_width, out_width, 1),
    ]

    def first_pack(layer_index, more):
        shard = skip_weight[layer_index].reshape(slab_rows, shard_rows, skip_width)
        return jnp.concatenate(
            [shard[i] for i in range(slab_rows)]
            + [attention_in[layer_index].reshape(shard_rows, -1), attention_out[layer_index].T]
            + more,
            1,
        )

    def second_pack(layer_index):
        return jnp.concatenate([up_weight[layer_index], down_weight[layer_index].T], 1)

    sequence = Sequence()
    sources = {
        "D0": lambda: first_pack(0, [packed_small]),
        "D2": lambda: second_pack(0),
        "D1": lambda: jnp.concatenate([first_pack(1, []), second_pack(1)], 1),
        "E": lambda: jnp.concatenate([inputs, skip_inputs[0]], 1),
        "L": lambda: jnp.concatenate([skip_inputs[1], cotangent], 1),
        "O": lambda: stream_lows[LAYERS],
        "G1": lambda: grads[1]["skip_part"],
        "G0": lambda: jnp.concatenate([grads[0]["input"], grads[0]["skip_part"]], 1),
    }
    moves, pairs, gathers, reduces, blocks, sums = ({}, {}, {}, {}, {}, {})

    def moved(key, value):
        blocks[key] = value
        if key == "D0":
            blocks["P0"] = value
        elif key == "D2":
            blocks["P2"] = value
        elif key == "D1":
            blocks["P1"] = value[:, :first_width]
            blocks["P3"] = value[:, first_width:]

    def paired(own, other):
        return jnp.where(
            net.column == 0,
            jnp.concatenate([own, other], 0),
            jnp.concatenate([other, own], 0),
        )

    def small_of(layer_index, all_small):
        values, begin = ([], 0)
        for size in small_widths:
            values.append(
                all_small[:, begin + layer_index * size : begin + (layer_index + 1) * size].reshape(
                    -1
                )
            )
            begin += LAYERS * size
        values[6] = lax.dynamic_slice_in_dim(values[6], core * up_width, up_width)
        return values

    weights = [{}, {}]
    smalls = [None, None]
    kept = [{}, {}]
    streams = [None] * (LAYERS + 1)
    stream_lows = [None] * (LAYERS + 1)

    def send(now, name, value):
        now[name] = to_core(sequence.mark(value))

    def received(now, name):
        return sequence.at(now.pop(name))

    def rows_with(own, other):
        return jnp.concatenate([own, other], 0)

    def skip_step(index):
        held, now = (weights[index], kept[index])
        if index == 0:
            held["half"], held["qkv"], held["out"], small_here = gathers["R0"].whole(
                first_pieces + [(first_width, small_lanes, 1)]
            )
            small_here = small_here.reshape(2 * net.chips, -1)
            small_other = to_core(small_here)
            all_small = jnp.where(
                core == 0,
                jnp.stack([small_here, small_other], 1),
                jnp.stack([small_other, small_here], 1),
            ).reshape(2 * fsdp_size, -1)
            for layer_index in range(LAYERS):
                smalls[layer_index] = small_of(layer_index, all_small)
        else:
            held["half"], held["qkv"], held["out"] = gathers["R1"].whole(first_pieces)
        send(now, "skip_other", held["half"])

    def in_columns(own, other):
        return jnp.where(
            core == 0, jnp.concatenate([own, other], 1), jnp.concatenate([other, own], 1)
        )

    def full_step(index):
        held, other = (weights[index], received(kept[index], "skip_other"))
        held["skip"] = sequence.mark(in_columns(held["half"], other))

    def hid_step(index):
        held, now, small = (weights[index], kept[index], smalls[index])
        if index == 0:
            stream_lows[0] = blocks["E"][:, :width]
            streams[0] = stream_lows[0].astype(f32)
            skip_here = blocks["E"][:, width:]
        else:
            skip_here = blocks["L"][:, :width]
        now["joined"] = jnp.concatenate([sequence.at(stream_lows[index]), skip_here], 1)
        part = jnp.dot(now["joined"], held["skip"], preferred_element_type=f32)
        now["hidden"] = part + small[0]
        now["first_norm"] = norm_apply(now["hidden"], small[1], small[2]).astype(low_type)
        send(now, "first_other", now["first_norm"])

    def qkv_step(index):
        held, now = (weights[index], kept[index])
        now["rows_first"] = rows_with(now["first_norm"], received(now, "first_other"))
        now["triple"] = sequence.mark(
            jnp.dot(now["rows_first"], held["qkv"], preferred_element_type=f32).astype(low_type)
        )

    def attend_step(index):
        now = kept[index]
        now["head_out"], now["log_total"] = attention_forward(sequence.at(now["triple"]))
        sequence.mark(now["head_out"])

    def out_step(index):
        held, now = (weights[index], kept[index])
        part = jnp.einsum(
            "th,dh->td", sequence.at(now["head_out"]), held["out"], preferred_element_type=f32
        )
        now["mixed_own"] = part[:count]
        send(now, "mixed_other", part[count:].astype(low_type))

    def second_norm_step(index):
        now, small = (kept[index], smalls[index])
        branch = now["mixed_own"] + received(now, "mixed_other").astype(f32)
        now["middle"] = now["hidden"] + branch + small[3]
        now["second_norm"] = norm_apply(now["middle"], small[4], small[5]).astype(low_type)
        send(now, "second_other", now["second_norm"])

    def up_step(index):
        held, now = (weights[index], kept[index])
        held["up"] = gathers["U%d" % index].whole([(0, up_width, 1)])[0]
        now["rows_second"] = rows_with(now["second_norm"], received(now, "second_other"))
        preact = (
            jnp.dot(now["rows_second"], held["up"], preferred_element_type=f32) + smalls[index][6]
        )
        below = 0.5 + 0.5 * lax.erf(preact * (0.5**0.5))
        now["activated"] = (preact * below).astype(low_type)
        now["slope"] = (below + preact * jnp.exp(-0.5 * preact * preact) * GAUSS).astype(low_type)
        sequence.mark(now["activated"])

    def down_held_step(index):
        weights[index]["down"] = gathers["W%d" % index].whole([(0, down_width, 1)])[0]

    def down_step(index):
        now = kept[index]
        part = jnp.einsum(
            "tf,df->td",
            sequence.at(now["activated"]),
            weights[index]["down"],
            preferred_element_type=f32,
        )
        now["branch_own"] = part[:count]
        send(now, "branch_other", part[count:].astype(low_type))

    def next_step(index):
        now = kept[index]
        branch = now["branch_own"] + received(now, "branch_other").astype(f32)
        streams[index + 1] = now["middle"] + branch + smalls[index][7]
        stream_lows[index + 1] = sequence.mark(streams[index + 1].astype(low_type))

    grads = [{}, {}]
    summed = {}

    def grad_rows_step(index):
        now = grads[index]
        if index == LAYERS - 1:
            now["stream_low"] = blocks["L"][:, width:]
            now["stream"] = now["stream_low"].astype(f32)
        else:
            now["stream_low"] = now["stream"].astype(low_type)
        now["down_bias"] = jnp.sum(now["stream"], 0)
        send(now, "stream_other", now["stream_low"])

    def grad_rows(index):
        now = grads[index]
        if "rows" not in now:
            now["rows"] = rows_with(now["stream_low"], received(now, "stream_other"))
            return now["rows"]
        return sequence.at(now["rows"])

    def down_grad_step(index):
        now = grads[index]
        now["down"] = sequence.mark(
            jnp.einsum(
                "td,tf->df",
                grad_rows(index),
                kept[index]["activated"],
                preferred_element_type=f32,
            ).astype(low_type)
        )
        sums["w%d" % index] = [now["down"]]

    def act_step(index):
        now = grads[index]
        act_grad = jnp.dot(
            grad_rows(index), weights[index]["down"], preferred_element_type=f32
        )
        pre_grad = act_grad * kept[index]["slope"]
        now["up_bias"] = jnp.sum(pre_grad, 0)
        now["pre_low"] = sequence.mark(pre_grad.astype(low_type))

    def second_step(index):
        now = grads[index]
        part = jnp.einsum(
            "tf,df->td",
            sequence.at(now["pre_low"]),
            weights[index]["up"],
            preferred_element_type=f32,
        )
        now["second_own"] = part[:count]
        send(now, "second_other", part[count:].astype(low_type))

    def up_grad_step(index):
        now = grads[index]
        now["up"] = sequence.mark(
            jnp.einsum(
                "td,tf->df",
                sequence.at(kept[index]["rows_second"]),
                now["pre_low"],
                preferred_element_type=f32,
            ).astype(low_type)
        )
        sums["u%d" % index] = [now["up"]]

    def middle_step(index):
        now, small = (grads[index], smalls[index])
        second_grad = now["second_own"] + received(now, "second_other").astype(f32)
        unused, pull = jax.vjp(norm_apply, kept[index]["middle"], small[4], small[5])
        norm_grad, now["second_gain"], now["second_shift"] = pull(second_grad)
        now["middle"] = now["stream"] + norm_grad
        now["out_bias"] = jnp.sum(now["middle"], 0)
        now["middle_low"] = now["middle"].astype(low_type)
        send(now, "middle_other", now["middle_low"])

    def mixed_step(index):
        now = grads[index]
        now["middle_rows"] = rows_with(now["middle_low"], received(now, "middle_other"))
        now["mixed"] = sequence.mark(
            jnp.dot(
                now["middle_rows"], weights[index]["out"], preferred_element_type=f32
            ).astype(low_type)
        )

    def out_grad_step(index):
        now = grads[index]
        now["out"] = sequence.mark(
            jnp.einsum(
                "td,th->dh",
                sequence.at(now["middle_rows"]),
                kept[index]["head_out"],
                preferred_element_type=f32,
            ).astype(low_type)
        )

    def attend_grad_step(index, part):
        now, old = (grads[index], kept[index])
        pairs = old["log_total"].shape[0]
        first, last = (pairs * part // 2, pairs * (part + 1) // 2)
        now["heads%d" % part] = attention_backward(
            old["triple"],
            old["head_out"],
            old["log_total"],
            sequence.at(now["mixed"]),
            first,
            last - first,
        )
        sequence.mark(now["heads%d" % part][0])

    def first_step(index):
        now = grads[index]
        now["triple"] = jnp.concatenate(
            [part for both in zip(now["heads0"], now["heads1"]) for part in both], 1
        )
        part = jnp.einsum(
            "tc,dc->td",
            sequence.at(now["triple"]),
            weights[index]["qkv"],
            preferred_element_type=f32,
        )
        now["first_own"] = part[:count]
        send(now, "first_other", part[count:].astype(low_type))

    def qkv_grad_step(index):
        now = grads[index]
        now["qkv"] = sequence.mark(
            jnp.einsum(
                "td,tc->dc",
                sequence.at(kept[index]["rows_first"]),
                now["triple"],
                preferred_element_type=f32,
            ).astype(low_type)
        )
        sums["i%d" % index] = [now["qkv"], now["out"]]

    def hidden_grad_step(index):
        now, small = (grads[index], smalls[index])
        first_grad = now["first_own"] + received(now, "first_other").astype(f32)
        unused, pull = jax.vjp(norm_apply, kept[index]["hidden"], small[1], small[2])
        norm_grad, now["first_gain"], now["first_shift"] = pull(first_grad)
        hidden_grad = now["middle"] + norm_grad
        now["skip_bias"] = jnp.sum(hidden_grad, 0)
        now["hidden_low"] = sequence.mark(hidden_grad.astype(low_type))

    def joined_step(index):
        now = grads[index]
        joined_grad = jnp.einsum(
            "te,ce->tc",
            sequence.at(now["hidden_low"]),
            weights[index]["skip"],
            preferred_element_type=f32,
        )
        now["skip_part"] = joined_grad[:, width:].astype(low_type)
        before = joined_grad[:, :width]
        if index:
            grads[index - 1]["stream"] = before
        else:
            now["input"] = before.astype(low_type)
        sequence.mark(now["skip_part"])

    def skip_grad_step(index):
        now = grads[index]
        full = jnp.einsum(
            "tc,te->ce",
            kept[index]["joined"],
            sequence.at(now["hidden_low"]),
            preferred_element_type=f32,
        ).astype(low_type)
        now["skip_keep"] = lax.dynamic_slice_in_dim(full, core * skip_width, skip_width, 1)
        send(
            now,
            "skip_other",
            lax.dynamic_slice_in_dim(full, (1 - core) * skip_width, skip_width, 1),
        )

    def skip_sum_step(index):
        now = grads[index]
        other = received(now, "skip_other").astype(f32)
        now["skip"] = sequence.mark((now["skip_keep"].astype(f32) + other).astype(low_type))
        slabs = now["skip"].reshape(-1, slab_rows, shard_rows, skip_width)
        sums["s%d" % index] = [
            slabs[:, i].reshape(-1, skip_width) for i in range(slab_rows)
        ]

    steps = {
        "skip": skip_step,
        "full": full_step,
        "hid": hid_step,
        "qkv": qkv_step,
        "attend": attend_step,
        "out": out_step,
        "second_norm": second_norm_step,
        "up": up_step,
        "down_held": down_held_step,
        "down": down_step,
        "next": next_step,
        "grad_rows": grad_rows_step,
        "down_grad": down_grad_step,
        "act": act_step,
        "second": second_step,
        "up_grad": up_grad_step,
        "middle": middle_step,
        "out_grad": out_grad_step,
        "mixed": mixed_step,
        "heads0": lambda index: attend_grad_step(index, 0),
        "heads1": lambda index: attend_grad_step(index, 1),
        "first": first_step,
        "qkv_grad": qkv_grad_step,
        "hidden_grad": hidden_grad_step,
        "joined": joined_step,
        "skip_grad": skip_grad_step,
        "skip_sum": skip_sum_step,
    }

    for item in PLAN:
        key = item[1:]
        if " " in item:
            name, index = item.split()
            steps[name](int(index))
        elif item[0] == "+":
            if key in sources:
                own = sources[key]()
                moves[key] = (own, net.diagonal_other(sequence.at(own)))
            elif key[0] == "P":
                pairs[key] = (blocks[key], net.to_column(sequence.at(blocks[key])))
            elif key[0] in "RUW":
                gathers[key] = RingGather(net, sequence.at(blocks[key]))
            elif key in ("w1", "u1", "i1", "s1"):
                reduces[key] = Swap(net, sequence.at(sums[key]))
            else:
                tensors = sequence.at(sums[key])
                if key in HALVED:
                    bits = [bit for bit in HALVED[key] if bit < net.bits]
                    bits += range(len(bits), net.bits)
                    reduces[key] = HalvingSum(net, tensors, bits)
                else:
                    reduces[key] = RingSum(net, tensors, False)
        elif item in moves:
            own, other = moves.pop(item)
            moved(item, sequence.mark(net.choose(own, sequence.at(other))))
        elif item in pairs:
            own, other = pairs.pop(item)
            other = sequence.at(other)
            both = sequence.mark(paired(own, other))
            if key in "01":
                blocks["R" + key] = both
            else:
                layer = str(int(key) - 2)
                blocks["U" + layer], blocks["W" + layer] = (both[:, :up_width], both[:, up_width:])
        elif item in gathers:
            gathers[item].advance(sequence)
        elif item in reduces:
            reduces[item].advance(sequence)
        else:
            chosen = [reduces[letter + "1"] for letter in item]
            own = jnp.concatenate([v for swap in chosen for v in swap.tensors], 1)
            other = sequence.at([v for swap in chosen for v in swap.coming])
            operand = sequence.mark(net.choose(own, jnp.concatenate(other, 1)))
            summed[item] = lax.psum_scatter(operand, "fsdp", scatter_dimension=0, tiled=True)
    output = blocks["O"].astype(f32)

    def back(*keys):
        return diagonal(jnp.concatenate([reduces[key].total for key in keys], 1)).astype(f32)

    def slabs_below(value):
        return jnp.concatenate(
            [value[:, i * skip_width : (i + 1) * skip_width] for i in range(slab_rows)], 0
        )

    second_one = summed["wu"].astype(f32)
    first_one = summed["is"].astype(f32)
    second_zero = back("w0", "u0")
    inner_zero = back("i0")
    skip_zero = back("s0")
    inner_one = first_one[:, : qkv_width + out_width]
    skip_grads = (slabs_below(skip_zero), slabs_below(first_one[:, qkv_width + out_width :]))
    down_grads = (second_zero[:, :down_width].T, second_one[:, :down_width].T)
    up_grads = (second_zero[:, down_width:], second_one[:, down_width:])
    out_grads = (inner_zero[:, qkv_width:].T, inner_one[:, qkv_width:].T)
    qkv_grads = [v[:, :qkv_width].reshape(attention_in.shape[1:]) for v in (inner_zero, inner_one)]

    names = (
        "skip_bias",
        "first_gain",
        "first_shift",
        "out_bias",
        "second_gain",
        "second_shift",
        "up_bias",
        "down_bias",
    )
    parts = []
    for now in grads:
        full = jnp.zeros((2 * up_width,), f32)
        now["up_bias"] = lax.dynamic_update_slice_in_dim(full, now["up_bias"], core * up_width, 0)
        parts += [now[name].astype(f32).reshape(2 * fsdp_size, -1) for name in names]
    small_sums = net.sum_small(jnp.concatenate(parts, 1)).reshape(LAYERS, -1)
    small_out, begin = ({}, 0)
    for name, size in zip(names, small_widths):
        small_out[name] = small_sums[:, begin : begin + size]
        begin += size
    return (
        output,
        blocks["G0"][:, :width].astype(f32),
        jnp.stack([blocks["G0"][:, width:].astype(f32), blocks["G1"].astype(f32)]),
        jnp.stack(skip_grads),
        small_out["skip_bias"],
        small_out["first_gain"],
        small_out["first_shift"],
        jnp.stack(qkv_grads),
        jnp.stack(out_grads),
        small_out["out_bias"],
        small_out["second_gain"],
        small_out["second_shift"],
        jnp.stack(up_grads),
        small_out["up_bias"],
        jnp.stack(down_grads),
        small_out["down_bias"],
    )


def solution(mesh):
    placed = (
        P(("fsdp", "tp"), None),
        P(None, ("fsdp", "tp"), None),
        P(None, "fsdp", "tp"),
        P(None, ("fsdp", "tp")),
        P(None, ("fsdp", "tp")),
        P(None, ("fsdp", "tp")),
        P(None, "fsdp", None, "tp"),
        P(None, "tp", "fsdp"),
        P(None, ("fsdp", "tp")),
        P(None, ("fsdp", "tp")),
        P(None, ("fsdp", "tp")),
        P(None, "fsdp", "tp"),
        P(None, ("fsdp", "tp")),
        P(None, "tp", "fsdp"),
        P(None, ("fsdp", "tp")),
        P(("fsdp", "tp"), None),
    )
    return jax.shard_map(
        choose_body(mesh),
        mesh=mesh,
        in_specs=placed,
        out_specs=(
            P(("fsdp", "tp"), None),
            P(("fsdp", "tp"), None),
            P(None, ("fsdp", "tp"), None),
            P(None, "fsdp", "tp"),
            P(None, ("fsdp", "tp")),
            P(None, ("fsdp", "tp")),
            P(None, ("fsdp", "tp")),
            P(None, "fsdp", None, "tp"),
            P(None, "tp", "fsdp"),
            P(None, ("fsdp", "tp")),
            P(None, ("fsdp", "tp")),
            P(None, ("fsdp", "tp")),
            P(None, "fsdp", "tp"),
            P(None, ("fsdp", "tp")),
            P(None, "tp", "fsdp"),
            P(None, ("fsdp", "tp")),
        ),
        check_vma=False,
    )
```

```python
import jax
import jax.numpy as jnp
from jax import lax
from jax.experimental import pallas as pl
from jax.experimental.pallas import tpu as pltpu
from jax.sharding import Mesh
from jax.sharding import PartitionSpec as P

HEAD_DIM = 64
FF = 4096
SEQ_LEN = 1104
LAYERS = 2


epsilon = 1e-05


def norm_apply(values_in, gain, shift):
    center = values_in - jnp.mean(values_in, -1, keepdims=True)
    spread = jnp.mean(center * center, -1, keepdims=True)
    return center * lax.rsqrt(spread + epsilon) * gain + shift


def gelu_exact(values_in):
    return jax.nn.gelu(values_in, approximate=False)


def split_heads(triple_seq):
    head_count = triple_seq.shape[2] // HEAD_DIM
    return (triple_seq.reshape(SEQ_LEN, 3, head_count, HEAD_DIM), head_count)


def attend(triple_seq):
    heads_split, head_count = split_heads(triple_seq)
    query, key_rows, value_rows = (heads_split[:, 0], heads_split[:, 1], heads_split[:, 2])
    half_rows = SEQ_LEN // 2
    score_scale = HEAD_DIM ** (-0.5)
    outputs, totals = ([], [])
    for part_index in range(2):
        query_part = query[part_index * half_rows : (part_index + 1) * half_rows]
        scores = (
            jnp.einsum("qhd,khd->hqk", query_part, key_rows, preferred_element_type=jnp.float32)
            * score_scale
        )
        row_top = jnp.max(scores, -1, keepdims=True)
        exp_scores = jnp.exp(scores - row_top)
        row_total = jnp.sum(exp_scores, -1, keepdims=True)
        low_probs = (exp_scores / row_total).astype(jnp.bfloat16)
        mixed = jnp.einsum(
            "hqk,khd->qhd", low_probs, value_rows, preferred_element_type=jnp.float32
        )
        outputs.append(mixed.astype(jnp.bfloat16).reshape(half_rows, head_count * HEAD_DIM))
        totals.append((row_top + jnp.log(row_total))[..., 0])
    return (jnp.concatenate(outputs, 0), jnp.concatenate(totals, 1))


def attend_back(items):
    triple_seq, log_total, mixed_grad = items
    heads_split, head_count = split_heads(triple_seq)
    query, key_rows, value_rows = (heads_split[:, 0], heads_split[:, 1], heads_split[:, 2])
    grad_heads = mixed_grad.reshape(SEQ_LEN, head_count, HEAD_DIM)
    half_rows = SEQ_LEN // 2
    score_scale = HEAD_DIM ** (-0.5)
    key_grad = jnp.zeros((SEQ_LEN, head_count, HEAD_DIM), jnp.float32)
    value_grad = jnp.zeros((SEQ_LEN, head_count, HEAD_DIM), jnp.float32)
    query_grads = []
    for part_index in range(2):
        rows_here = slice(part_index * half_rows, (part_index + 1) * half_rows)
        query_part = query[rows_here]
        grad_part = grad_heads[rows_here]
        scores = (
            jnp.einsum("qhd,khd->hqk", query_part, key_rows, preferred_element_type=jnp.float32)
            * score_scale
        )
        probs = jnp.exp(scores - log_total[:, rows_here][..., None])
        low_probs = probs.astype(jnp.bfloat16)
        value_grad = value_grad + jnp.einsum(
            "hqk,qhd->khd", low_probs, grad_part, preferred_element_type=jnp.float32
        )
        prob_grad = jnp.einsum(
            "qhd,khd->hqk", grad_part, value_rows, preferred_element_type=jnp.float32
        )
        score_grad = (probs * (prob_grad - jnp.sum(prob_grad * probs, -1, keepdims=True))).astype(
            jnp.bfloat16
        )
        query_grads.append(
            jnp.einsum("hqk,khd->qhd", score_grad, key_rows, preferred_element_type=jnp.float32)
            * score_scale
        )
        key_grad = (
            key_grad
            + jnp.einsum("hqk,qhd->khd", score_grad, query_part, preferred_element_type=jnp.float32)
            * score_scale
        )
    stacked = jnp.stack([jnp.concatenate(query_grads, 0), key_grad, value_grad], 1)
    return stacked.reshape(SEQ_LEN, 3, head_count * HEAD_DIM).astype(jnp.bfloat16)


def general_body(
    inputs,
    skip_inputs,
    skip_weight,
    skip_bias,
    first_gain,
    first_shift,
    attention_in,
    attention_out,
    out_bias,
    second_gain,
    second_shift,
    up_weight,
    up_bias,
    down_weight,
    down_bias,
    cotangent,
):

    def fetch_layer(layer_index):
        small_params = (
            lax.all_gather(skip_bias[layer_index], ("fsdp", "tp"), axis=0, tiled=True),
            lax.all_gather(first_gain[layer_index], ("fsdp", "tp"), axis=0, tiled=True),
            lax.all_gather(first_shift[layer_index], ("fsdp", "tp"), axis=0, tiled=True),
            lax.all_gather(out_bias[layer_index], ("fsdp", "tp"), axis=0, tiled=True),
            lax.all_gather(second_gain[layer_index], ("fsdp", "tp"), axis=0, tiled=True),
            lax.all_gather(second_shift[layer_index], ("fsdp", "tp"), axis=0, tiled=True),
            lax.all_gather(up_bias[layer_index], ("fsdp", "tp"), axis=0, tiled=True),
            lax.all_gather(down_bias[layer_index], ("fsdp", "tp"), axis=0, tiled=True),
        )
        block = (
            lax.all_gather(skip_weight[layer_index], "fsdp", axis=0, tiled=True),
            lax.all_gather(attention_in[layer_index], "fsdp", axis=0, tiled=True),
            lax.all_gather(attention_out[layer_index], "fsdp", axis=1, tiled=True),
            lax.all_gather(up_weight[layer_index], "fsdp", axis=0, tiled=True),
            lax.all_gather(down_weight[layer_index], "fsdp", axis=1, tiled=True),
        )
        weight_up, weight_down = (block[3], block[4])
        unit_width = weight_up.shape[1]
        bias_up = lax.dynamic_slice_in_dim(
            small_params[6], lax.axis_index("tp") * unit_width, unit_width
        )
        return (small_params, block[0], block[1], block[2], weight_up, bias_up, weight_down)

    def rows_of(normed):
        return lax.all_gather(normed, "tp", axis=0, tiled=True)

    def sum_rows(partial_value):
        return lax.psum_scatter(
            partial_value.astype(jnp.bfloat16), "tp", scatter_dimension=0, tiled=True
        ).astype(jnp.float32)

    def grad_rows_of(grad_low):
        return lax.all_gather(grad_low, "tp", axis=0, tiled=True)

    def sum_row_grads(partial_value):
        return lax.psum_scatter(
            partial_value.astype(jnp.bfloat16), "tp", scatter_dimension=0, tiled=True
        ).astype(jnp.float32)

    def forward(stream, skip_rows, weights):
        small_params, weight_skip, weight_qkv, weight_out, weight_up, bias_up, weight_down = weights
        joined = jnp.concatenate([stream.astype(jnp.bfloat16), skip_rows], 1)
        rows_joined = rows_of(joined)
        hidden_part = jnp.dot(rows_joined, weight_skip, preferred_element_type=jnp.float32)
        hidden = (
            lax.all_to_all(
                hidden_part.astype(jnp.bfloat16), "tp", split_axis=0, concat_axis=1, tiled=True
            ).astype(hidden_part.dtype)
            + small_params[0]
        )
        first_norm = norm_apply(hidden, small_params[1], small_params[2]).astype(jnp.bfloat16)
        rows_first = rows_of(first_norm)
        triple = jnp.einsum(
            "td,dch->tch", rows_first, weight_qkv, preferred_element_type=jnp.float32
        ).astype(jnp.bfloat16)
        seq_count = rows_first.shape[0] // SEQ_LEN
        head_out, log_total = lax.map(attend, triple.reshape(seq_count, SEQ_LEN, 3, -1))
        head_out = head_out.reshape(rows_first.shape[0], -1)
        middle = (
            hidden
            + sum_rows(jnp.dot(head_out, weight_out, preferred_element_type=jnp.float32))
            + small_params[3]
        )
        second_norm = norm_apply(middle, small_params[4], small_params[5]).astype(jnp.bfloat16)
        rows_second = rows_of(second_norm)
        preact = jnp.dot(rows_second, weight_up, preferred_element_type=jnp.float32) + bias_up
        activated = gelu_exact(preact).astype(jnp.bfloat16)
        branch = sum_rows(jnp.dot(activated, weight_down, preferred_element_type=jnp.float32))
        result = middle + branch + small_params[7]
        kept = (
            rows_joined,
            hidden,
            rows_first,
            triple,
            head_out,
            log_total,
            middle,
            rows_second,
            preact,
            activated,
        )
        return (result, kept)

    streams = [inputs.astype(jnp.float32)]
    stored = []
    for layer_index in range(LAYERS):
        weights = fetch_layer(layer_index)
        result, kept_here = forward(streams[layer_index], skip_inputs[layer_index], weights)
        stored.append((weights, kept_here))
        streams.append(result)
    output = streams[LAYERS]
    stream_grad = cotangent.astype(jnp.float32)
    skip_parts = [None] * LAYERS
    small_parts = [None] * LAYERS
    block_parts = [None] * LAYERS
    for layer_index in reversed(range(LAYERS)):
        weights = fetch_layer(layer_index)
        unused_result, kept = forward(streams[layer_index], skip_inputs[layer_index], weights)
        (
            backward_small_params,
            backward_weight_skip,
            backward_weight_qkv,
            backward_weight_out,
            backward_weight_up,
            backward_bias_up,
            backward_weight_down,
        ) = weights
        (
            backward_rows_joined,
            backward_hidden,
            backward_rows_first,
            backward_triple,
            backward_head_out,
            backward_log_total,
            backward_middle,
            backward_rows_second,
            backward_preact,
            backward_activated,
        ) = kept
        down_bias_grad = jnp.sum(stream_grad, 0)
        grad_rows = grad_rows_of(stream_grad.astype(jnp.bfloat16))
        act_grad = jnp.einsum(
            "td,fd->tf", grad_rows, backward_weight_down, preferred_element_type=jnp.float32
        )
        down_weight_grad = jnp.einsum(
            "tf,td->fd", backward_activated, grad_rows, preferred_element_type=jnp.float32
        )
        gelu_unused, gelu_pull = jax.vjp(gelu_exact, backward_preact)
        pre_grad = gelu_pull(act_grad)[0]
        up_bias_part = jnp.sum(pre_grad, 0)
        pre_low = pre_grad.astype(jnp.bfloat16)
        up_weight_grad = jnp.einsum(
            "td,tf->df", backward_rows_second, pre_low, preferred_element_type=jnp.float32
        )
        second_grad = sum_row_grads(
            jnp.einsum("tf,df->td", pre_low, backward_weight_up, preferred_element_type=jnp.float32)
        )
        up_bias_full = lax.dynamic_update_slice_in_dim(
            jnp.zeros((FF,), jnp.float32),
            up_bias_part,
            lax.axis_index("tp") * up_bias_part.shape[0],
            0,
        )
        norm_unused, second_pull = jax.vjp(
            norm_apply, backward_middle, backward_small_params[4], backward_small_params[5]
        )
        middle_norm_grad, second_gain_grad, second_shift_grad = second_pull(second_grad)
        middle_grad = stream_grad + middle_norm_grad
        out_bias_grad = jnp.sum(middle_grad, 0)
        middle_rows = grad_rows_of(middle_grad.astype(jnp.bfloat16))
        mixed_grad = jnp.einsum(
            "td,hd->th", middle_rows, backward_weight_out, preferred_element_type=jnp.float32
        ).astype(jnp.bfloat16)
        out_weight_grad = jnp.einsum(
            "th,td->hd", backward_head_out, middle_rows, preferred_element_type=jnp.float32
        )
        backward_seq_count = backward_rows_first.shape[0] // SEQ_LEN
        triple_grad = lax.map(
            attend_back,
            (
                backward_triple.reshape(backward_seq_count, SEQ_LEN, 3, -1),
                backward_log_total,
                mixed_grad.reshape(backward_seq_count, SEQ_LEN, -1),
            ),
        )
        triple_grad = triple_grad.reshape(backward_triple.shape)
        qkv_weight_grad = jnp.einsum(
            "td,tch->dch", backward_rows_first, triple_grad, preferred_element_type=jnp.float32
        )
        first_grad = sum_row_grads(
            jnp.einsum(
                "tch,dch->td", triple_grad, backward_weight_qkv, preferred_element_type=jnp.float32
            )
        )
        norm_unused_two, first_pull = jax.vjp(
            norm_apply, backward_hidden, backward_small_params[1], backward_small_params[2]
        )
        hidden_norm_grad, first_gain_grad, first_shift_grad = first_pull(first_grad)
        hidden_grad = middle_grad + hidden_norm_grad
        skip_bias_grad = jnp.sum(hidden_grad, 0)
        hidden_low = hidden_grad.astype(jnp.bfloat16)
        hidden_cols = lax.all_to_all(hidden_low, "tp", split_axis=1, concat_axis=0, tiled=True)
        joined_grad = sum_row_grads(
            jnp.einsum(
                "te,ce->tc", hidden_cols, backward_weight_skip, preferred_element_type=jnp.float32
            )
        )
        skip_weight_grad = jnp.einsum(
            "tc,te->ce", backward_rows_joined, hidden_cols, preferred_element_type=jnp.float32
        )
        small_grads = (
            lax.psum_scatter(skip_bias_grad, ("fsdp", "tp"), scatter_dimension=0, tiled=True),
            lax.psum_scatter(
                first_gain_grad.astype(jnp.float32), ("fsdp", "tp"), scatter_dimension=0, tiled=True
            ),
            lax.psum_scatter(
                first_shift_grad.astype(jnp.float32),
                ("fsdp", "tp"),
                scatter_dimension=0,
                tiled=True,
            ),
            lax.psum_scatter(out_bias_grad, ("fsdp", "tp"), scatter_dimension=0, tiled=True),
            lax.psum_scatter(
                second_gain_grad.astype(jnp.float32),
                ("fsdp", "tp"),
                scatter_dimension=0,
                tiled=True,
            ),
            lax.psum_scatter(
                second_shift_grad.astype(jnp.float32),
                ("fsdp", "tp"),
                scatter_dimension=0,
                tiled=True,
            ),
            lax.psum_scatter(up_bias_full, ("fsdp", "tp"), scatter_dimension=0, tiled=True),
            lax.psum_scatter(down_bias_grad, ("fsdp", "tp"), scatter_dimension=0, tiled=True),
        )
        block_grads = (
            lax.psum_scatter(
                skip_weight_grad.astype(jnp.bfloat16), "fsdp", scatter_dimension=0, tiled=True
            ).astype(jnp.float32),
            lax.psum_scatter(
                qkv_weight_grad.astype(jnp.bfloat16), "fsdp", scatter_dimension=0, tiled=True
            ).astype(jnp.float32),
            lax.psum_scatter(
                out_weight_grad.astype(jnp.bfloat16), "fsdp", scatter_dimension=1, tiled=True
            ).astype(jnp.float32),
            lax.psum_scatter(
                up_weight_grad.astype(jnp.bfloat16), "fsdp", scatter_dimension=0, tiled=True
            ).astype(jnp.float32),
            lax.psum_scatter(
                down_weight_grad.astype(jnp.bfloat16), "fsdp", scatter_dimension=1, tiled=True
            ).astype(jnp.float32),
        )
        width = backward_weight_skip.shape[0] // 2
        stream_grad, skip_part, small_grads, block_grads = (
            joined_grad[:, :width],
            joined_grad[:, width:],
            small_grads,
            block_grads,
        )
        skip_parts[layer_index] = skip_part
        small_parts[layer_index] = small_grads
        block_parts[layer_index] = block_grads

    def stack_small(position):
        return jnp.stack([small_parts[index_layer][position] for index_layer in range(LAYERS)])

    def stack_block(position):
        return jnp.stack([block_parts[index_layer][position] for index_layer in range(LAYERS)])

    return (
        output,
        stream_grad,
        jnp.stack(skip_parts),
        stack_block(0),
        stack_small(0),
        stack_small(1),
        stack_small(2),
        stack_block(1),
        stack_block(2),
        stack_small(3),
        stack_small(4),
        stack_small(5),
        stack_block(3),
        stack_small(6),
        stack_block(4),
        stack_small(7),
    )


FSDP = ("chip", "core")
BOTH = ("chip", "core", "tp")
NETWORK = ("chip", "tp")
GAUSS = 0.3989422804014327


class Sequence:
    def __init__(self):
        self.last = None

    def at(self, value):
        if self.last is None:
            return value
        return lax.optimization_barrier((value, self.last))[0]

    def mark(self, value):
        self.last = value
        return value


class RingGather:
    def __init__(self, net, block):
        self.net, self.round = (net, 0)
        self.blocks = {0: block}
        self.ahead, self.behind = (block, block)
        self.send()

    def send(self):
        ahead, behind = (self.ahead, self.behind)
        if self.round + 1 == self.net.half_ring:
            middle = ahead.shape[1] // 256 * 128
            ahead, behind = (ahead[:, :middle], behind[:, middle:])
        self.coming = (self.net.along_ring(ahead, 1), self.net.along_ring(behind, -1))

    def advance(self, sequence):
        got = sequence.mark(sequence.at(self.coming))
        self.round += 1
        if self.round == self.net.half_ring:
            self.blocks[self.round] = got
            return
        self.ahead, self.behind = got
        self.blocks[-self.round], self.blocks[self.round] = got
        self.send()

    def whole(self, pieces):
        net, offsets = (self.net, sorted(self.blocks))
        operands, jobs = ([], [])
        pair_rows = self.blocks[0].shape[0]
        half_rows = pair_rows // 2
        shapes = [(net.chips * pair_rows * slabs, width) for begin, width, slabs in pieces]
        for at, offset in enumerate(offsets):
            held = self.blocks[offset]
            start = 0
            for part in held if isinstance(held, tuple) else (held,):
                stop = start + part.shape[1]
                for which, (begin, width, slabs) in enumerate(pieces):
                    for slab in range(slabs):
                        low = max(start, begin + slab * width)
                        high = min(stop, begin + (slab + 1) * width)
                        if low >= high:
                            continue
                        to = low - begin - slab * width
                        spans = [(0, pair_rows, 0)]
                        if slabs > 1:
                            spans = [
                                (i * half_rows, half_rows, (i * slabs + slab) * half_rows)
                                for i in range(2)
                            ]
                        for row, rows, to_row in spans:
                            jobs.append(
                                (len(operands), row, rows, low - start, high - low, which, at)
                                + (pair_rows * slabs, to_row, to)
                            )
                operands.append(part)
                start = stop
        table = [
            [net.order[(net.order.index(q) + offset) % net.chips] for offset in offsets]
            for q in range(net.chips)
        ]
        places = lax.dynamic_index_in_dim(jnp.asarray(table, jnp.int32), net.chip, 0, False, allow_negative_indices=False)
        return copy_kernel(places, operands, jobs, shapes)


def add_blocks(places, tensors, blocks, ahead, behind):
    rows = tensors[0].shape[0] // blocks
    widths = [t.shape[1] for t in tensors]
    total = sum(widths)
    spans = ((0, ahead.shape[1]), (total - behind.shape[1], total))

    def kernel(at_ref, *refs):
        count = len(tensors)
        for side in range(2):
            got_ref, out_ref = (refs[2 * count + side], refs[2 * count + 2 + side])
            low, high = spans[side]
            begin = 0
            for index, width in enumerate(widths):
                block_ref = refs[side * count + index]
                first, last = (max(begin, low), min(begin + width, high))
                if first >= last:
                    out_ref[:, begin : begin + width] = block_ref[...]
                else:
                    if first > begin:
                        out_ref[:, begin:first] = block_ref[:, : first - begin]
                    if last < begin + width:
                        out_ref[:, last : begin + width] = block_ref[:, last - begin :]
                    own = block_ref[:, first - begin : last - begin].astype(jnp.float32)
                    got = got_ref[:, first - low : last - low].astype(jnp.float32)
                    out_ref[:, first:last] = (own + got).astype(jnp.bfloat16)
                begin += width

    def whole(value):
        return pl.BlockSpec(value.shape, lambda i, at: (0, 0))

    def block(width, side):
        return pl.BlockSpec((rows, width), lambda i, at: (at[side], 0))

    out = jax.ShapeDtypeStruct((rows, total), jnp.bfloat16)
    return pl.pallas_call(
        kernel,
        grid_spec=pltpu.PrefetchScalarGridSpec(
            num_scalar_prefetch=1,
            grid=(1,),
            in_specs=[block(width, side) for side in range(2) for width in widths]
            + [whole(ahead), whole(behind)],
            out_specs=[whole(out), whole(out)],
        ),
        out_shape=[out, out],
        compiler_params=pltpu.CompilerParams(vmem_limit_bytes=24 << 20),
        cost_estimate=pl.CostEstimate(
            flops=2 * rows * total, bytes_accessed=12 * rows * total, transcendentals=0
        ),
    )(places, *tensors, *tensors, ahead, behind)


class RingSum:
    def __init__(self, net, tensors, columns_first):
        self.net, self.columns_first = (net, columns_first)
        self.views = [t.reshape(net.chips, 2, -1, t.shape[1]) for t in tensors]
        if columns_first:
            self.stage = "columns"
            self.coming = [
                net.to_column(lax.dynamic_index_in_dim(v, 1 - net.column, 1, False, allow_negative_indices=False))
                for v in self.views
            ]
        else:
            self.views = [v.reshape(net.chips, -1, v.shape[3]) for v in self.views]
            self.begin()

    def block(self, offset):
        at = self.net.chip_at(offset)
        parts = [lax.dynamic_index_in_dim(v, at, 0, False, allow_negative_indices=False) for v in self.views]
        return jnp.concatenate(parts, 1)

    def begin(self):
        self.stage, self.distance = ("ring", self.net.half_ring)
        far = self.block(self.net.half_ring)
        middle = far.shape[1] // 256 * 128
        self.coming = (
            self.net.along_ring(far[:, :middle], 1),
            self.net.along_ring(far[:, middle:], -1),
        )

    def advance(self, sequence):
        net, got = (self.net, sequence.at(self.coming))
        if self.stage == "columns":
            self.views = [
                (
                    lax.dynamic_index_in_dim(v, net.column, 1, False, allow_negative_indices=False).astype(jnp.float32)
                    + other.astype(jnp.float32)
                ).astype(jnp.bfloat16)
                for v, other in zip(self.views, got)
            ]
            sequence.mark(self.views)
            self.begin()
            return
        if self.stage == "last":
            total = self.keep + got.astype(jnp.float32)
            self.total = sequence.mark(total.astype(jnp.bfloat16))
            return
        ahead, behind = got
        self.distance -= 1
        if self.distance:
            places = jnp.stack([net.chip_at(self.distance), net.chip_at(-self.distance)])
            flat = [v.reshape(-1, v.shape[2]) for v in self.views]
            ahead, behind = sequence.mark(add_blocks(places, flat, net.chips, ahead, behind))
            self.coming = (net.along_ring(ahead, 1), net.along_ring(behind, -1))
            return
        ahead, behind = (ahead.astype(jnp.float32), behind.astype(jnp.float32))
        total = self.block(0).astype(jnp.float32) + ahead + behind
        if self.columns_first:
            self.total = sequence.mark(total.astype(jnp.bfloat16))
            return
        half_rows = total.shape[0] // 2
        self.keep = lax.dynamic_slice_in_dim(total, net.column * half_rows, half_rows, 0, allow_negative_indices=False)
        send = lax.dynamic_slice_in_dim(total, (1 - net.column) * half_rows, half_rows, 0, allow_negative_indices=False)
        send = sequence.mark(send.astype(jnp.bfloat16))
        self.stage, self.coming = ("last", net.to_column(send))


class HalvingSum:
    def __init__(self, net, tensors, bits):
        self.net, self.bits, self.round = (net, bits, 0)
        count = len(bits)
        self.views = [t.reshape((2,) * count + (-1, t.shape[1])) for t in tensors]
        self.left = list(reversed(range(count)))
        self.cut()

    def cut(self):
        bit = self.bits[self.round]
        axis = self.left.index(bit)
        self.left.remove(bit)
        side = self.net.side(bit)

        def half(which):
            parts = [lax.dynamic_index_in_dim(v, which, axis, False, allow_negative_indices=False) for v in self.views]
            return jnp.concatenate(parts, -1)

        self.keep = half(side)
        self.coming = self.net.to_partner(half(1 - side), bit)

    def advance(self, sequence):
        got = sequence.at(self.coming)
        total = self.keep.astype(jnp.float32) + got.astype(jnp.float32)
        self.round += 1
        self.total = sequence.mark(total.astype(jnp.bfloat16))
        if self.round < len(self.bits):
            self.views = [self.total]
            self.cut()


class HalvingSum:
    def __init__(self, net, tensors, bits):
        self.net, self.bits, self.round = (net, bits, 0)
        count = len(bits)
        self.views = [t.reshape((2,) * count + (-1, t.shape[1])) for t in tensors]
        self.left = list(reversed(range(count)))
        self.cut()

    def cut(self):
        bit = self.bits[self.round]
        axis = self.left.index(bit)
        self.left.remove(bit)
        side = self.net.side(bit)

        def half(which):
            parts = [lax.dynamic_index_in_dim(v, which, axis, False, allow_negative_indices=False) for v in self.views]
            return jnp.concatenate(parts, -1)

        self.keep = half(side)
        self.coming = self.net.to_partner(half(1 - side), bit)

    def advance(self, sequence):
        got = sequence.at(self.coming)
        total = self.keep.astype(jnp.float32) + got.astype(jnp.float32)
        self.round += 1
        self.total = sequence.mark(total.astype(jnp.bfloat16))
        if self.round < len(self.bits):
            self.views = [self.total]
            self.cut()


class HalvingSum:
    def __init__(self, net, tensors, bits):
        self.net, self.bits, self.round = (net, bits, 0)
        count = len(bits)
        self.views = [t.reshape((2,) * count + (-1, t.shape[1])) for t in tensors]
        self.left = list(reversed(range(count)))
        self.cut()

    def cut(self):
        bit = self.bits[self.round]
        axis = self.left.index(bit)
        self.left.remove(bit)
        side = self.net.side(bit)

        def half(which):
            parts = [lax.dynamic_index_in_dim(v, which, axis, False, allow_negative_indices=False) for v in self.views]
            return jnp.concatenate(parts, -1)

        self.keep = half(side)
        self.coming = self.net.to_partner(half(1 - side), bit)

    def advance(self, sequence):
        got = sequence.at(self.coming)
        total = self.keep.astype(jnp.float32) + got.astype(jnp.float32)
        self.round += 1
        self.total = sequence.mark(total.astype(jnp.bfloat16))
        if self.round < len(self.bits):
            self.views = [self.total]
            self.cut()


class HalvingSum:
    def __init__(self, net, tensors, bits):
        self.net, self.bits, self.round = (net, bits, 0)
        count = len(bits)
        self.views = [t.reshape((2,) * count + (-1, t.shape[1])) for t in tensors]
        self.left = list(reversed(range(count)))
        self.cut()

    def cut(self):
        bit = self.bits[self.round]
        axis = self.left.index(bit)
        self.left.remove(bit)
        side = self.net.side(bit)

        def half(which):
            parts = [lax.dynamic_index_in_dim(v, which, axis, False, allow_negative_indices=False) for v in self.views]
            return jnp.concatenate(parts, -1)

        self.keep = half(side)
        self.coming = self.net.to_partner(half(1 - side), bit)

    def advance(self, sequence):
        got = sequence.at(self.coming)
        total = self.keep.astype(jnp.float32) + got.astype(jnp.float32)
        self.round += 1
        self.total = sequence.mark(total.astype(jnp.bfloat16))
        if self.round < len(self.bits):
            self.views = [self.total]
            self.cut()


class Swap:
    def __init__(self, net, tensors):
        self.net, self.tensors = (net, tensors)
        self.coming = [net.diagonal_other(value) for value in tensors]

    def advance(self, sequence):
        self.coming = sequence.mark(sequence.at(self.coming))


class CoreNetwork:
    def __init__(self, fsdp_size):
        self.chips = fsdp_size // 2
        self.core = lax.axis_index("core")
        self.chip = lax.axis_index("chip")
        self.column = lax.axis_index("tp")
        self.bits = self.chips.bit_length()
        half = self.chips // 2
        self.half_ring = half
        self.order = [2 * i for i in range(half)] + [2 * i + 1 for i in reversed(range(half))]
        table = [
            [self.order[(self.order.index(q) + offset) % self.chips] for offset in range(self.chips)]
            for q in range(self.chips)
        ]
        self.chips_here = lax.dynamic_index_in_dim(
            jnp.asarray(table, jnp.int32), self.chip, 0, False, allow_negative_indices=False
        )
        self.ring_pairs = {}
        for step in (1, -1):
            self.ring_pairs[step] = [
                (self.order[i] * 2 + c, self.order[(i + step) % self.chips] * 2 + c)
                for i in range(self.chips)
                for c in range(2)
            ]
        self.core_pairs = [(i, i ^ 1) for i in range(fsdp_size)]
        self.diagonal_pairs = []
        for q in range(self.chips):
            one, two = (q * 4 + 2, q * 4 + 1)
            self.diagonal_pairs += [(one, two), (two, one)]

    def to_core(self, value):
        return lax.ppermute(value, FSDP, self.core_pairs)

    def chip_at(self, offset):
        return self.chips_here[offset % self.chips]

    def along_ring(self, value, step):
        return lax.ppermute(value, FSDP, self.ring_pairs[step])

    def to_column(self, value):
        return self.to_partner(value, 0)

    def diagonal_other(self, value):
        return lax.ppermute(value, BOTH, self.diagonal_pairs)

    def choose(self, own, other):
        return jnp.where(self.core == self.column, own, other)

    def diagonal(self, value):
        return self.choose(value, self.diagonal_other(value))

    def to_partner(self, value, bit):
        if bit == 0:
            return lax.ppermute(value, "tp", [(0, 1), (1, 0)])
        flip = 1 << (bit - 1)
        pairs = [(q * 2 + c, (q ^ flip) * 2 + c) for q in range(self.chips) for c in range(2)]
        return lax.ppermute(value, FSDP, pairs)

    def side(self, bit):
        return self.column if bit == 0 else (self.chip >> (bit - 1)) & 1

    def sum_small(self, packed):
        for bit in reversed(range(self.bits + 1)):
            count = packed.shape[0] // 2
            if bit == 1:
                side, send_to = (self.core, self.to_core)
            else:
                wire = max(bit - 1, 0)
                side = self.side(wire)
                send_to = lambda value, wire=wire: self.to_partner(value, wire)
            keep = jnp.where(side == 0, packed[:count], packed[count:])
            send = jnp.where(side == 0, packed[count:], packed[:count])
            packed = keep + send_to(send)
        return packed[0]


def copy_kernel(places, operands, jobs, shapes):
    def kernel(at_ref, *refs):
        sources, targets = (refs[: len(operands)], refs[len(operands) :][: len(shapes)])
        buffers = refs[len(operands) + len(shapes) : -2]
        sems, out_sems = refs[-2:]
        copies = [[] for _ in shapes]
        for which in range(len(shapes)):
            for index, job in enumerate(jobs):
                source, row, rows, col, width, target, at, scale, offset, to = job
                if target != which:
                    continue
                begin = pl.multiple_of(at_ref[at] * scale + offset, 16)
                copy = pltpu.make_async_copy(
                    sources[source].at[pl.ds(row, rows), pl.ds(col, width)],
                    buffers[which].at[pl.ds(begin, rows), pl.ds(to, width)],
                    sems.at[index],
                )
                copy.start()
                copies[which].append(copy)
        outs = []
        for which in range(len(shapes)):
            for copy in copies[which]:
                copy.wait()
            out = pltpu.make_async_copy(buffers[which], targets[which], out_sems.at[which])
            out.start()
            outs.append(out)
        for out in outs:
            out.wait()

    moved = sum(2 * 2 * r * w for r, w in shapes)
    return pl.pallas_call(
        kernel,
        out_shape=[jax.ShapeDtypeStruct(shape, jnp.bfloat16) for shape in shapes],
        in_specs=[pl.BlockSpec(memory_space=pltpu.SMEM)]
        + [pl.BlockSpec(memory_space=pl.ANY)] * len(operands),
        out_specs=[pl.BlockSpec(memory_space=pl.ANY)] * len(shapes),
        scratch_shapes=[pltpu.VMEM(shape, jnp.bfloat16) for shape in shapes]
        + [pltpu.SemaphoreType.DMA((len(jobs),)), pltpu.SemaphoreType.DMA((len(shapes),))],
        compiler_params=pltpu.CompilerParams(vmem_limit_bytes=24 << 20),
        cost_estimate=pl.CostEstimate(flops=0, bytes_accessed=moved, transcendentals=0),
    )(places, *operands)


def row_chunks(count):
    return [(begin, min(384, count - begin)) for begin in range(0, count, 384)]


NT = (((1,), (1,)), ((), ()))
TN = (((0,), (0,)), ((), ()))


def head_lanes(value, head):
    lane = lax.broadcasted_iota(jnp.int32, value.shape, 1)
    return jnp.where((lane >= HEAD_DIM) == (head == 1), value, jnp.zeros_like(value))


def attention_forward(triple):
    tokens, width = (triple.shape[0], triple.shape[1] // 3)
    pairs = width // (2 * HEAD_DIM)

    def kernel(query_ref, key_ref, value_ref, out_ref, total_ref):
        keys = key_ref[...]
        values = value_ref[...]
        for begin, rows in row_chunks(tokens):
            query = query_ref[begin : begin + rows, :] * jnp.bfloat16(HEAD_DIM**-0.5)
            mixed, totals = ([], [])
            for head in range(2):
                scores = lax.dot_general(
                    head_lanes(query, head), keys, NT, preferred_element_type=jnp.float32
                )
                top = jnp.max(scores, -1, keepdims=True)
                grown = jnp.exp(scores - top)
                total = jnp.sum(grown, -1, keepdims=True)
                mixed.append(
                    jnp.dot(
                        grown.astype(jnp.bfloat16), values, preferred_element_type=jnp.float32
                    )
                    / total
                )
                totals.append(top + jnp.log(total))
            lane = lax.broadcasted_iota(jnp.int32, mixed[0].shape, 1)
            out_ref[begin : begin + rows, :] = jnp.where(
                lane < HEAD_DIM, mixed[0], mixed[1]
            ).astype(jnp.bfloat16)
            both = jnp.where(lane < HEAD_DIM, totals[0], totals[1]).T
            total_ref[0, 0:1, begin : begin + rows] = both[0:1, :]
            total_ref[0, 1:2, begin : begin + rows] = both[HEAD_DIM : HEAD_DIM + 1, :]

    def part(index):
        return pl.BlockSpec((tokens, 2 * HEAD_DIM), lambda i: (0, index * pairs + i))

    return pl.pallas_call(
        kernel,
        grid=(pairs,),
        in_specs=[part(0), part(1), part(2)],
        out_specs=[part(0), pl.BlockSpec((1, 2, tokens), lambda i: (i, 0, 0))],
        out_shape=[
            jax.ShapeDtypeStruct((tokens, width), jnp.bfloat16),
            jax.ShapeDtypeStruct((pairs, 2, tokens), jnp.float32),
        ],
        compiler_params=pltpu.CompilerParams(vmem_limit_bytes=48 << 20),
        cost_estimate=pl.CostEstimate(
            flops=16 * pairs * tokens * tokens * HEAD_DIM,
            bytes_accessed=8 * tokens * width,
            transcendentals=2 * pairs * tokens * tokens,
        ),
    )(triple, triple, triple)


def attention_backward(triple, head_out, log_total, mixed_grad, first_pair, pair_count):
    tokens, width = (triple.shape[0], triple.shape[1] // 3)
    pairs = width // (2 * HEAD_DIM)
    score_scale = HEAD_DIM**-0.5

    def kernel(
        query_ref, key_ref, value_ref, out_ref, total_ref, grad_ref, dq_ref, dk_ref, dv_ref, sum_ref
    ):
        query = query_ref[...] * jnp.bfloat16(score_scale)
        grad = grad_ref[...]
        product = grad.astype(jnp.float32) * out_ref[...].astype(jnp.float32)
        ones = jnp.ones((8, 2 * HEAD_DIM), jnp.float32)
        deltas = [
            lax.dot_general(
                head_lanes(ones, head),
                product,
                NT,
                precision=lax.Precision.HIGHEST,
                preferred_element_type=jnp.float32,
            )[0:1, :]
            for head in range(2)
        ]
        for begin, rows in row_chunks(tokens):
            keys = key_ref[begin : begin + rows, :]
            values = value_ref[begin : begin + rows, :]
            key_grads, value_grads = ([], [])
            for head in range(2):
                keys_here = head_lanes(keys, head)
                scores = lax.dot_general(
                    keys_here, query, NT, preferred_element_type=jnp.float32
                )
                probs = jnp.exp(scores - total_ref[0, head : head + 1, :])
                prob_grad = lax.dot_general(
                    head_lanes(values, head), grad, NT, preferred_element_type=jnp.float32
                )
                score_grad = (probs * (prob_grad - deltas[head])).astype(jnp.bfloat16)
                value_grads.append(
                    jnp.dot(
                        probs.astype(jnp.bfloat16), grad, preferred_element_type=jnp.float32
                    )
                )
                key_grads.append(jnp.dot(score_grad, query, preferred_element_type=jnp.float32))
                query_grad = lax.dot_general(
                    score_grad, keys_here, TN, preferred_element_type=jnp.float32
                )
                if begin == 0 and head == 0:
                    sum_ref[...] = query_grad
                else:
                    sum_ref[...] += query_grad
            lane = lax.broadcasted_iota(jnp.int32, key_grads[0].shape, 1)
            dk_ref[begin : begin + rows, :] = jnp.where(
                lane < HEAD_DIM, key_grads[0], key_grads[1]
            ).astype(jnp.bfloat16)
            dv_ref[begin : begin + rows, :] = jnp.where(
                lane < HEAD_DIM, value_grads[0], value_grads[1]
            ).astype(jnp.bfloat16)
        dq_ref[...] = (sum_ref[...] * score_scale).astype(jnp.bfloat16)

    def part(index):
        return pl.BlockSpec((tokens, 2 * HEAD_DIM), lambda i: (0, index * pairs + first_pair + i))

    return pl.pallas_call(
        kernel,
        grid=(pair_count,),
        in_specs=[
            part(0),
            part(1),
            part(2),
            part(0),
            pl.BlockSpec((1, 2, tokens), lambda i: (first_pair + i, 0, 0)),
            part(0),
        ],
        out_specs=[pl.BlockSpec((tokens, 2 * HEAD_DIM), lambda i: (0, i))] * 3,
        out_shape=[jax.ShapeDtypeStruct((tokens, pair_count * 2 * HEAD_DIM), jnp.bfloat16)] * 3,
        scratch_shapes=[pltpu.VMEM((tokens, 2 * HEAD_DIM), jnp.float32)],
        compiler_params=pltpu.CompilerParams(vmem_limit_bytes=48 << 20),
        cost_estimate=pl.CostEstimate(
            flops=40 * pair_count * tokens * tokens * HEAD_DIM,
            bytes_accessed=32 * tokens * pair_count * HEAD_DIM,
            transcendentals=2 * pair_count * tokens * tokens,
        ),
    )(triple, triple, triple, head_out, log_total, mixed_grad)


SWAPPED = ("i1", "s1")
HALVED = {"w1": (0, 2, 1, 3), "u1": (1, 0, 2, 3), "u0": (1, 0, 2, 3), "w0": (2, 1, 0, 3)}
PLAN = (
    "+D0", "D0", "+P0", "+D1", "P0", "+R0", "D1", "+P1", "R0", "P1", "+R1", "+E", "R0", "+D2", "R1",
    "D2", "+P2", "R0", "R1", "P2", "+P3", "R0", "+U0", "R1", "E", "R1", "+W0", "skip 0", "U0", "full 0",
    "W0", "P3", "+L", "hid 0", "U0", "W0", "skip 1", "qkv 0", "U0", "attend 0", "W0", "L", "out 0", "U0",
    "+U1", "second_norm 0", "W0", "+W1", "up 0", "U1", "down_held 0", "down 0", "W1", "full 1", "next 0",
    "U1", "hid 1", "W1", "qkv 1", "U1", "attend 1", "W1", "out 1", "U1", "second_norm 1", "W1",
    "grad_rows 1", "up 1", "down_grad 1", "+w1", "down_held 1", "act 1", "second 1", "up_grad 1", "+u1",
    "middle 1", "mixed 1", "out_grad 1", "heads0 1", "heads1 1", "w1", "u1", "first 1",
    "qkv_grad 1", "+i1", "hidden_grad 1", "joined 1", "w1", "grad_rows 0", "skip_grad 1", "u1", "act 0",
    "w1", "u1", "skip_sum 1", "+s1", "second 0", "w1", "up_grad 0", "u1", "+u0", "down_grad 0",
    "+w0", "middle 0", "mixed 0", "out_grad 0", "i1", "heads0 0", "u0", "s1", "is", "+G1", "heads1 0",
    "w0", "first 0", "qkv_grad 0", "+i0", "u0", "hidden_grad 0", "i0", "G1", "skip_grad 0", "joined 0",
    "+G0", "w0", "skip_sum 0", "+s0", "i0", "u0", "s0", "down 1", "i0", "w0", "s0", "next 1", "+O", "i0",
    "s0", "u0", "i0", "s0", "G0", "w0", "s0", "O",
)


def fast_body(
    fsdp_size,
    inputs,
    skip_inputs,
    skip_weight,
    skip_bias,
    first_gain,
    first_shift,
    attention_in,
    attention_out,
    out_bias,
    second_gain,
    second_shift,
    up_weight,
    up_bias,
    down_weight,
    down_bias,
    cotangent,
):
    net = CoreNetwork(fsdp_size)
    core, to_core, diagonal = (net.core, net.to_core, net.diagonal)
    count, width = inputs.shape
    shard_rows = attention_in.shape[1]
    skip_rows, skip_width = skip_weight.shape[1:]
    qkv_width = attention_in.shape[2] * attention_in.shape[3]
    up_width = up_weight.shape[2]
    down_width = down_weight.shape[1]
    f32, low_type = (jnp.float32, jnp.bfloat16)

    small_values = (
        skip_bias,
        first_gain,
        first_shift,
        out_bias,
        second_gain,
        second_shift,
        up_bias,
        down_bias,
    )
    small_widths = [value.shape[1] for value in small_values]
    small_total = sum(small_widths) * LAYERS
    small_lanes = -(-small_total // (128 * shard_rows)) * 128
    packed_small = jnp.concatenate([value.reshape(-1) for value in small_values])
    packed_small = jnp.pad(packed_small, (0, shard_rows * small_lanes - small_total))
    packed_small = packed_small.reshape(shard_rows, small_lanes)
    out_width = attention_out.shape[1]
    slab_rows = skip_rows // shard_rows
    first_width = slab_rows * skip_width + qkv_width + out_width
    first_pieces = [
        (0, skip_width, slab_rows),
        (slab_rows * skip_width, qkv_width, 1),
        (slab_rows * skip_width + qkv_width, out_width, 1),
    ]

    def first_pack(layer_index, more):
        shard = skip_weight[layer_index].reshape(slab_rows, shard_rows, skip_width)
        return jnp.concatenate(
            [shard[i] for i in range(slab_rows)]
            + [attention_in[layer_index].reshape(shard_rows, -1), attention_out[layer_index].T]
            + more,
            1,
        )

    def second_pack(layer_index):
        return jnp.concatenate([up_weight[layer_index], down_weight[layer_index].T], 1)

    sequence = Sequence()
    sources = {
        "D0": lambda: first_pack(0, [packed_small]),
        "D2": lambda: second_pack(0),
        "D1": lambda: jnp.concatenate([first_pack(1, []), second_pack(1)], 1),
        "E": lambda: jnp.concatenate([inputs, skip_inputs[0]], 1),
        "L": lambda: jnp.concatenate([skip_inputs[1], cotangent], 1),
        "O": lambda: stream_lows[LAYERS],
        "G1": lambda: grads[1]["skip_part"],
        "G0": lambda: jnp.concatenate([grads[0]["input"], grads[0]["skip_part"]], 1),
    }
    moves, pairs, gathers, reduces, blocks, sums = ({}, {}, {}, {}, {}, {})

    def moved(key, value):
        blocks[key] = value
        if key == "D0":
            blocks["P0"] = value
        elif key == "D2":
            blocks["P2"] = value
        elif key == "D1":
            blocks["P1"] = value[:, :first_width]
            blocks["P3"] = value[:, first_width:]

    def paired(own, other):
        return jnp.where(
            net.column == 0,
            jnp.concatenate([own, other], 0),
            jnp.concatenate([other, own], 0),
        )

    def small_of(layer_index, all_small):
        values, begin = ([], 0)
        for size in small_widths:
            values.append(
                all_small[:, begin + layer_index * size : begin + (layer_index + 1) * size].reshape(
                    -1
                )
            )
            begin += LAYERS * size
        values[6] = lax.dynamic_slice_in_dim(values[6], core * up_width, up_width, allow_negative_indices=False)
        return values

    weights = [{}, {}]
    smalls = [None, None]
    kept = [{}, {}]
    streams = [None] * (LAYERS + 1)
    stream_lows = [None] * (LAYERS + 1)

    def send(now, name, value):
        now[name] = to_core(sequence.mark(value))

    def received(now, name):
        return sequence.at(now.pop(name))

    def rows_with(own, other):
        return jnp.concatenate([own, other], 0)

    def skip_step(index):
        held, now = (weights[index], kept[index])
        if index == 0:
            held["half"], held["qkv"], held["out"], small_here = gathers["R0"].whole(
                first_pieces + [(first_width, small_lanes, 1)]
            )
            small_here = small_here.reshape(2 * net.chips, -1)
            small_other = to_core(small_here)
            all_small = jnp.where(
                core == 0,
                jnp.stack([small_here, small_other], 1),
                jnp.stack([small_other, small_here], 1),
            ).reshape(2 * fsdp_size, -1)
            for layer_index in range(LAYERS):
                smalls[layer_index] = small_of(layer_index, all_small)
        else:
            held["half"], held["qkv"], held["out"] = gathers["R1"].whole(first_pieces)
        send(now, "skip_other", held["half"])

    def in_columns(own, other):
        return jnp.where(
            core == 0, jnp.concatenate([own, other], 1), jnp.concatenate([other, own], 1)
        )

    def full_step(index):
        held, other = (weights[index], received(kept[index], "skip_other"))
        held["skip"] = sequence.mark(in_columns(held["half"], other))

    def hid_step(index):
        held, now, small = (weights[index], kept[index], smalls[index])
        if index == 0:
            stream_lows[0] = blocks["E"][:, :width]
            streams[0] = stream_lows[0].astype(f32)
            skip_here = blocks["E"][:, width:]
        else:
            skip_here = blocks["L"][:, :width]
        now["joined"] = jnp.concatenate([sequence.at(stream_lows[index]), skip_here], 1)
        part = jnp.dot(now["joined"], held["skip"], preferred_element_type=f32)
        now["hidden"] = part + small[0]
        now["first_norm"] = norm_apply(now["hidden"], small[1], small[2]).astype(low_type)
        send(now, "first_other", now["first_norm"])

    def qkv_step(index):
        held, now = (weights[index], kept[index])
        now["rows_first"] = rows_with(now["first_norm"], received(now, "first_other"))
        now["triple"] = sequence.mark(
            jnp.dot(now["rows_first"], held["qkv"], preferred_element_type=f32).astype(low_type)
        )

    def attend_step(index):
        now = kept[index]
        now["head_out"], now["log_total"] = attention_forward(sequence.at(now["triple"]))
        sequence.mark(now["head_out"])

    def out_step(index):
        held, now = (weights[index], kept[index])
        part = jnp.einsum(
            "th,dh->td", sequence.at(now["head_out"]), held["out"], preferred_element_type=f32
        )
        now["mixed_own"] = part[:count]
        send(now, "mixed_other", part[count:].astype(low_type))

    def second_norm_step(index):
        now, small = (kept[index], smalls[index])
        branch = now["mixed_own"] + received(now, "mixed_other").astype(f32)
        now["middle"] = now["hidden"] + branch + small[3]
        now["second_norm"] = norm_apply(now["middle"], small[4], small[5]).astype(low_type)
        send(now, "second_other", now["second_norm"])

    def up_step(index):
        held, now = (weights[index], kept[index])
        held["up"] = gathers["U%d" % index].whole([(0, up_width, 1)])[0]
        now["rows_second"] = rows_with(now["second_norm"], received(now, "second_other"))
        preact = (
            jnp.dot(now["rows_second"], held["up"], preferred_element_type=f32) + smalls[index][6]
        )
        below = 0.5 + 0.5 * lax.erf(preact * (0.5**0.5))
        now["activated"] = (preact * below).astype(low_type)
        now["slope"] = (below + preact * jnp.exp(-0.5 * preact * preact) * GAUSS).astype(low_type)
        sequence.mark(now["activated"])

    def down_held_step(index):
        weights[index]["down"] = gathers["W%d" % index].whole([(0, down_width, 1)])[0]

    def down_step(index):
        now = kept[index]
        part = jnp.einsum(
            "tf,df->td",
            sequence.at(now["activated"]),
            weights[index]["down"],
            preferred_element_type=f32,
        )
        now["branch_own"] = part[:count]
        send(now, "branch_other", part[count:].astype(low_type))

    def next_step(index):
        now = kept[index]
        branch = now["branch_own"] + received(now, "branch_other").astype(f32)
        streams[index + 1] = now["middle"] + branch + smalls[index][7]
        stream_lows[index + 1] = sequence.mark(streams[index + 1].astype(low_type))

    grads = [{}, {}]
    summed = {}

    def grad_rows_step(index):
        now = grads[index]
        if index == LAYERS - 1:
            now["stream_low"] = blocks["L"][:, width:]
            now["stream"] = now["stream_low"].astype(f32)
        else:
            now["stream_low"] = now["stream"].astype(low_type)
        now["down_bias"] = jnp.sum(now["stream"], 0)
        send(now, "stream_other", now["stream_low"])

    def grad_rows(index):
        now = grads[index]
        if "rows" not in now:
            now["rows"] = rows_with(now["stream_low"], received(now, "stream_other"))
            return now["rows"]
        return sequence.at(now["rows"])

    def down_grad_step(index):
        now = grads[index]
        now["down"] = sequence.mark(
            jnp.einsum(
                "td,tf->df",
                grad_rows(index),
                kept[index]["activated"],
                preferred_element_type=f32,
            ).astype(low_type)
        )
        sums["w%d" % index] = [now["down"]]

    def act_step(index):
        now = grads[index]
        act_grad = jnp.dot(
            grad_rows(index), weights[index]["down"], preferred_element_type=f32
        )
        pre_grad = act_grad * kept[index]["slope"]
        now["up_bias"] = jnp.sum(pre_grad, 0)
        now["pre_low"] = sequence.mark(pre_grad.astype(low_type))

    def second_step(index):
        now = grads[index]
        part = jnp.einsum(
            "tf,df->td",
            sequence.at(now["pre_low"]),
            weights[index]["up"],
            preferred_element_type=f32,
        )
        now["second_own"] = part[:count]
        send(now, "second_other", part[count:].astype(low_type))

    def up_grad_step(index):
        now = grads[index]
        now["up"] = sequence.mark(
            jnp.einsum(
                "td,tf->df",
                sequence.at(kept[index]["rows_second"]),
                now["pre_low"],
                preferred_element_type=f32,
            ).astype(low_type)
        )
        sums["u%d" % index] = [now["up"]]

    def middle_step(index):
        now, small = (grads[index], smalls[index])
        second_grad = now["second_own"] + received(now, "second_other").astype(f32)
        unused, pull = jax.vjp(norm_apply, kept[index]["middle"], small[4], small[5])
        norm_grad, now["second_gain"], now["second_shift"] = pull(second_grad)
        now["middle"] = now["stream"] + norm_grad
        now["out_bias"] = jnp.sum(now["middle"], 0)
        now["middle_low"] = now["middle"].astype(low_type)
        send(now, "middle_other", now["middle_low"])

    def mixed_step(index):
        now = grads[index]
        now["middle_rows"] = rows_with(now["middle_low"], received(now, "middle_other"))
        now["mixed"] = sequence.mark(
            jnp.dot(
                now["middle_rows"], weights[index]["out"], preferred_element_type=f32
            ).astype(low_type)
        )

    def out_grad_step(index):
        now = grads[index]
        now["out"] = sequence.mark(
            jnp.einsum(
                "td,th->dh",
                sequence.at(now["middle_rows"]),
                kept[index]["head_out"],
                preferred_element_type=f32,
            ).astype(low_type)
        )

    def attend_grad_step(index, part):
        now, old = (grads[index], kept[index])
        pairs = old["log_total"].shape[0]
        first, last = (pairs * part // 2, pairs * (part + 1) // 2)
        now["heads%d" % part] = attention_backward(
            old["triple"],
            old["head_out"],
            old["log_total"],
            sequence.at(now["mixed"]),
            first,
            last - first,
        )
        sequence.mark(now["heads%d" % part][0])

    def first_step(index):
        now = grads[index]
        now["triple"] = jnp.concatenate(
            [part for both in zip(now["heads0"], now["heads1"]) for part in both], 1
        )
        part = jnp.einsum(
            "tc,dc->td",
            sequence.at(now["triple"]),
            weights[index]["qkv"],
            preferred_element_type=f32,
        )
        now["first_own"] = part[:count]
        send(now, "first_other", part[count:].astype(low_type))

    def qkv_grad_step(index):
        now = grads[index]
        now["qkv"] = sequence.mark(
            jnp.einsum(
                "td,tc->dc",
                sequence.at(kept[index]["rows_first"]),
                now["triple"],
                preferred_element_type=f32,
            ).astype(low_type)
        )
        sums["i%d" % index] = [now["qkv"], now["out"]]

    def hidden_grad_step(index):
        now, small = (grads[index], smalls[index])
        first_grad = now["first_own"] + received(now, "first_other").astype(f32)
        unused, pull = jax.vjp(norm_apply, kept[index]["hidden"], small[1], small[2])
        norm_grad, now["first_gain"], now["first_shift"] = pull(first_grad)
        hidden_grad = now["middle"] + norm_grad
        now["skip_bias"] = jnp.sum(hidden_grad, 0)
        now["hidden_low"] = sequence.mark(hidden_grad.astype(low_type))

    def joined_step(index):
        now = grads[index]
        joined_grad = jnp.einsum(
            "te,ce->tc",
            sequence.at(now["hidden_low"]),
            weights[index]["skip"],
            preferred_element_type=f32,
        )
        now["skip_part"] = joined_grad[:, width:].astype(low_type)
        before = joined_grad[:, :width]
        if index:
            grads[index - 1]["stream"] = before
        else:
            now["input"] = before.astype(low_type)
        sequence.mark(now["skip_part"])

    def skip_grad_step(index):
        now = grads[index]
        low = sequence.at(now["hidden_low"])

        def half(which):
            columns = lax.dynamic_slice_in_dim(
                low, which * skip_width, skip_width, 1, allow_negative_indices=False
            )
            return jnp.einsum(
                "tc,te->ce", kept[index]["joined"], columns, preferred_element_type=f32
            )

        send(now, "skip_other", half(1 - core).astype(low_type))
        now["skip_keep"] = half(core)

    def skip_sum_step(index):
        now = grads[index]
        other = received(now, "skip_other").astype(f32)
        now["skip"] = sequence.mark((now["skip_keep"] + other).astype(low_type))
        slabs = now["skip"].reshape(-1, slab_rows, shard_rows, skip_width)
        sums["s%d" % index] = [
            slabs[:, i].reshape(-1, skip_width) for i in range(slab_rows)
        ]

    steps = {
        "skip": skip_step,
        "full": full_step,
        "hid": hid_step,
        "qkv": qkv_step,
        "attend": attend_step,
        "out": out_step,
        "second_norm": second_norm_step,
        "up": up_step,
        "down_held": down_held_step,
        "down": down_step,
        "next": next_step,
        "grad_rows": grad_rows_step,
        "down_grad": down_grad_step,
        "act": act_step,
        "second": second_step,
        "up_grad": up_grad_step,
        "middle": middle_step,
        "out_grad": out_grad_step,
        "mixed": mixed_step,
        "heads0": lambda index: attend_grad_step(index, 0),
        "heads1": lambda index: attend_grad_step(index, 1),
        "first": first_step,
        "qkv_grad": qkv_grad_step,
        "hidden_grad": hidden_grad_step,
        "joined": joined_step,
        "skip_grad": skip_grad_step,
        "skip_sum": skip_sum_step,
    }

    for item in PLAN:
        key = item[1:]
        if " " in item:
            name, index = item.split()
            steps[name](int(index))
        elif item[0] == "+":
            if key in sources:
                own = sources[key]()
                moves[key] = (own, net.diagonal_other(sequence.at(own)))
            elif key[0] == "P":
                pairs[key] = (blocks[key], net.to_column(sequence.at(blocks[key])))
            elif key[0] in "RUW":
                gathers[key] = RingGather(net, sequence.at(blocks[key]))
            elif key in SWAPPED:
                reduces[key] = Swap(net, sequence.at(sums[key]))
            else:
                tensors = sequence.at(sums[key])
                if key in HALVED:
                    bits = [bit for bit in HALVED[key] if bit < net.bits]
                    bits += range(len(bits), net.bits)
                    reduces[key] = HalvingSum(net, tensors, bits)
                else:
                    reduces[key] = RingSum(net, tensors, False)
        elif item in moves:
            own, other = moves.pop(item)
            moved(item, sequence.mark(net.choose(own, sequence.at(other))))
        elif item in pairs:
            own, other = pairs.pop(item)
            other = sequence.at(other)
            both = sequence.mark(paired(own, other))
            if key in "01":
                blocks["R" + key] = both
            else:
                layer = str(int(key) - 2)
                blocks["U" + layer], blocks["W" + layer] = (both[:, :up_width], both[:, up_width:])
        elif item in gathers:
            gathers[item].advance(sequence)
        elif item in reduces:
            reduces[item].advance(sequence)
        else:
            chosen = [reduces[letter + "1"] for letter in item]
            own = jnp.concatenate([v for swap in chosen for v in swap.tensors], 1)
            other = sequence.at([v for swap in chosen for v in swap.coming])
            operand = sequence.mark(net.choose(own, jnp.concatenate(other, 1)))
            summed[item] = lax.psum_scatter(operand, FSDP, scatter_dimension=0, tiled=True)
    output = blocks["O"].astype(f32)

    def back(*keys):
        return diagonal(jnp.concatenate([reduces[key].total for key in keys], 1)).astype(f32)

    def slabs_below(value):
        return jnp.concatenate(
            [value[:, i * skip_width : (i + 1) * skip_width] for i in range(slab_rows)], 0
        )

    first_one = summed["is"].astype(f32)
    second_zero = back("w0", "u0")
    second_one = back("w1", "u1")
    inner_zero = back("i0")
    skip_zero = back("s0")
    inner_one = first_one[:, : qkv_width + out_width]
    skip_grads = (slabs_below(skip_zero), slabs_below(first_one[:, qkv_width + out_width :]))
    down_grads = (second_zero[:, :down_width].T, second_one[:, :down_width].T)
    up_grads = (second_zero[:, down_width:], second_one[:, down_width:])
    out_grads = (inner_zero[:, qkv_width:].T, inner_one[:, qkv_width:].T)
    qkv_grads = [v[:, :qkv_width].reshape(attention_in.shape[1:]) for v in (inner_zero, inner_one)]

    names = (
        "skip_bias",
        "first_gain",
        "first_shift",
        "out_bias",
        "second_gain",
        "second_shift",
        "up_bias",
        "down_bias",
    )
    parts = []
    for now in grads:
        full = jnp.zeros((2 * up_width,), f32)
        now["up_bias"] = lax.dynamic_update_slice_in_dim(full, now["up_bias"], core * up_width, 0, allow_negative_indices=False)
        parts += [now[name].astype(f32).reshape(2 * fsdp_size, -1) for name in names]
    small_sums = net.sum_small(jnp.concatenate(parts, 1)).reshape(LAYERS, -1)
    small_out, begin = ({}, 0)
    for name, size in zip(names, small_widths):
        small_out[name] = small_sums[:, begin : begin + size]
        begin += size
    return (
        output,
        blocks["G0"][:, :width].astype(f32),
        jnp.stack([blocks["G0"][:, width:].astype(f32), blocks["G1"].astype(f32)]),
        jnp.stack(skip_grads),
        small_out["skip_bias"],
        small_out["first_gain"],
        small_out["first_shift"],
        jnp.stack(qkv_grads),
        jnp.stack(out_grads),
        small_out["out_bias"],
        small_out["second_gain"],
        small_out["second_shift"],
        jnp.stack(up_grads),
        small_out["up_bias"],
        jnp.stack(down_grads),
        small_out["down_bias"],
    )


def solution(mesh):
    fsdp, tensor, body = ("fsdp", "tp", general_body)
    size = mesh.shape["fsdp"]
    if mesh.shape["tp"] == 2 and size >= 4 and size & (size - 1) == 0:
        mesh = Mesh(mesh.devices.reshape(size // 2, 2, 2), BOTH)
        fsdp, body = (FSDP, lambda *arrays: fast_body(size, *arrays))
    both = (*(fsdp if fsdp == FSDP else (fsdp,)), tensor)
    tokens, vector = (P(both, None), P(None, both))
    layers = P(None, both, None)
    rows, columns = (P(None, fsdp, tensor), P(None, tensor, fsdp))
    qkv = P(None, fsdp, None, tensor)
    weights = (rows, vector, vector, vector, qkv, columns, vector, vector, vector)
    weights += (rows, vector, columns, vector)
    return jax.shard_map(
        body,
        mesh=mesh,
        in_specs=(tokens, layers, *weights, tokens),
        out_specs=(tokens, tokens, layers, *weights),
        check_vma=False,
    )
```

```python
import jax
import jax.numpy as jnp
from jax import lax
from jax.experimental import pallas as pl
from jax.experimental.pallas import tpu as pltpu
from jax.sharding import Mesh
from jax.sharding import PartitionSpec as P

HEAD_DIM = 64
FF = 4096
SEQ_LEN = 1104
LAYERS = 2


epsilon = 1e-05


def norm_apply(values_in, gain, shift):
    center = values_in - jnp.mean(values_in, -1, keepdims=True)
    spread = jnp.mean(center * center, -1, keepdims=True)
    return center * lax.rsqrt(spread + epsilon) * gain + shift


def gelu_exact(values_in):
    return jax.nn.gelu(values_in, approximate=False)


def split_heads(triple_seq):
    head_count = triple_seq.shape[2] // HEAD_DIM
    return (triple_seq.reshape(SEQ_LEN, 3, head_count, HEAD_DIM), head_count)


def attend(triple_seq):
    heads_split, head_count = split_heads(triple_seq)
    query, key_rows, value_rows = (heads_split[:, 0], heads_split[:, 1], heads_split[:, 2])
    half_rows = SEQ_LEN // 2
    score_scale = HEAD_DIM ** (-0.5)
    outputs, totals = ([], [])
    for part_index in range(2):
        query_part = query[part_index * half_rows : (part_index + 1) * half_rows]
        scores = (
            jnp.einsum("qhd,khd->hqk", query_part, key_rows, preferred_element_type=jnp.float32)
            * score_scale
        )
        row_top = jnp.max(scores, -1, keepdims=True)
        exp_scores = jnp.exp(scores - row_top)
        row_total = jnp.sum(exp_scores, -1, keepdims=True)
        low_probs = (exp_scores / row_total).astype(jnp.bfloat16)
        mixed = jnp.einsum(
            "hqk,khd->qhd", low_probs, value_rows, preferred_element_type=jnp.float32
        )
        outputs.append(mixed.astype(jnp.bfloat16).reshape(half_rows, head_count * HEAD_DIM))
        totals.append((row_top + jnp.log(row_total))[..., 0])
    return (jnp.concatenate(outputs, 0), jnp.concatenate(totals, 1))


def attend_back(items):
    triple_seq, log_total, mixed_grad = items
    heads_split, head_count = split_heads(triple_seq)
    query, key_rows, value_rows = (heads_split[:, 0], heads_split[:, 1], heads_split[:, 2])
    grad_heads = mixed_grad.reshape(SEQ_LEN, head_count, HEAD_DIM)
    half_rows = SEQ_LEN // 2
    score_scale = HEAD_DIM ** (-0.5)
    key_grad = jnp.zeros((SEQ_LEN, head_count, HEAD_DIM), jnp.float32)
    value_grad = jnp.zeros((SEQ_LEN, head_count, HEAD_DIM), jnp.float32)
    query_grads = []
    for part_index in range(2):
        rows_here = slice(part_index * half_rows, (part_index + 1) * half_rows)
        query_part = query[rows_here]
        grad_part = grad_heads[rows_here]
        scores = (
            jnp.einsum("qhd,khd->hqk", query_part, key_rows, preferred_element_type=jnp.float32)
            * score_scale
        )
        probs = jnp.exp(scores - log_total[:, rows_here][..., None])
        low_probs = probs.astype(jnp.bfloat16)
        value_grad = value_grad + jnp.einsum(
            "hqk,qhd->khd", low_probs, grad_part, preferred_element_type=jnp.float32
        )
        prob_grad = jnp.einsum(
            "qhd,khd->hqk", grad_part, value_rows, preferred_element_type=jnp.float32
        )
        score_grad = (probs * (prob_grad - jnp.sum(prob_grad * probs, -1, keepdims=True))).astype(
            jnp.bfloat16
        )
        query_grads.append(
            jnp.einsum("hqk,khd->qhd", score_grad, key_rows, preferred_element_type=jnp.float32)
            * score_scale
        )
        key_grad = (
            key_grad
            + jnp.einsum("hqk,qhd->khd", score_grad, query_part, preferred_element_type=jnp.float32)
            * score_scale
        )
    stacked = jnp.stack([jnp.concatenate(query_grads, 0), key_grad, value_grad], 1)
    return stacked.reshape(SEQ_LEN, 3, head_count * HEAD_DIM).astype(jnp.bfloat16)


def general_body(
    inputs,
    skip_inputs,
    skip_weight,
    skip_bias,
    first_gain,
    first_shift,
    attention_in,
    attention_out,
    out_bias,
    second_gain,
    second_shift,
    up_weight,
    up_bias,
    down_weight,
    down_bias,
    cotangent,
):

    def fetch_layer(layer_index):
        small_params = (
            lax.all_gather(skip_bias[layer_index], ("fsdp", "tp"), axis=0, tiled=True),
            lax.all_gather(first_gain[layer_index], ("fsdp", "tp"), axis=0, tiled=True),
            lax.all_gather(first_shift[layer_index], ("fsdp", "tp"), axis=0, tiled=True),
            lax.all_gather(out_bias[layer_index], ("fsdp", "tp"), axis=0, tiled=True),
            lax.all_gather(second_gain[layer_index], ("fsdp", "tp"), axis=0, tiled=True),
            lax.all_gather(second_shift[layer_index], ("fsdp", "tp"), axis=0, tiled=True),
            lax.all_gather(up_bias[layer_index], ("fsdp", "tp"), axis=0, tiled=True),
            lax.all_gather(down_bias[layer_index], ("fsdp", "tp"), axis=0, tiled=True),
        )
        block = (
            lax.all_gather(skip_weight[layer_index], "fsdp", axis=0, tiled=True),
            lax.all_gather(attention_in[layer_index], "fsdp", axis=0, tiled=True),
            lax.all_gather(attention_out[layer_index], "fsdp", axis=1, tiled=True),
            lax.all_gather(up_weight[layer_index], "fsdp", axis=0, tiled=True),
            lax.all_gather(down_weight[layer_index], "fsdp", axis=1, tiled=True),
        )
        weight_up, weight_down = (block[3], block[4])
        unit_width = weight_up.shape[1]
        bias_up = lax.dynamic_slice_in_dim(
            small_params[6], lax.axis_index("tp") * unit_width, unit_width
        )
        return (small_params, block[0], block[1], block[2], weight_up, bias_up, weight_down)

    def rows_of(normed):
        return lax.all_gather(normed, "tp", axis=0, tiled=True)

    def sum_rows(partial_value):
        return lax.psum_scatter(
            partial_value.astype(jnp.bfloat16), "tp", scatter_dimension=0, tiled=True
        ).astype(jnp.float32)

    def grad_rows_of(grad_low):
        return lax.all_gather(grad_low, "tp", axis=0, tiled=True)

    def sum_row_grads(partial_value):
        return lax.psum_scatter(
            partial_value.astype(jnp.bfloat16), "tp", scatter_dimension=0, tiled=True
        ).astype(jnp.float32)

    def forward(stream, skip_rows, weights):
        small_params, weight_skip, weight_qkv, weight_out, weight_up, bias_up, weight_down = weights
        joined = jnp.concatenate([stream.astype(jnp.bfloat16), skip_rows], 1)
        rows_joined = rows_of(joined)
        hidden_part = jnp.dot(rows_joined, weight_skip, preferred_element_type=jnp.float32)
        hidden = (
            lax.all_to_all(
                hidden_part.astype(jnp.bfloat16), "tp", split_axis=0, concat_axis=1, tiled=True
            ).astype(hidden_part.dtype)
            + small_params[0]
        )
        first_norm = norm_apply(hidden, small_params[1], small_params[2]).astype(jnp.bfloat16)
        rows_first = rows_of(first_norm)
        triple = jnp.einsum(
            "td,dch->tch", rows_first, weight_qkv, preferred_element_type=jnp.float32
        ).astype(jnp.bfloat16)
        seq_count = rows_first.shape[0] // SEQ_LEN
        head_out, log_total = lax.map(attend, triple.reshape(seq_count, SEQ_LEN, 3, -1))
        head_out = head_out.reshape(rows_first.shape[0], -1)
        middle = (
            hidden
            + sum_rows(jnp.dot(head_out, weight_out, preferred_element_type=jnp.float32))
            + small_params[3]
        )
        second_norm = norm_apply(middle, small_params[4], small_params[5]).astype(jnp.bfloat16)
        rows_second = rows_of(second_norm)
        preact = jnp.dot(rows_second, weight_up, preferred_element_type=jnp.float32) + bias_up
        activated = gelu_exact(preact).astype(jnp.bfloat16)
        branch = sum_rows(jnp.dot(activated, weight_down, preferred_element_type=jnp.float32))
        result = middle + branch + small_params[7]
        kept = (
            rows_joined,
            hidden,
            rows_first,
            triple,
            head_out,
            log_total,
            middle,
            rows_second,
            preact,
            activated,
        )
        return (result, kept)

    streams = [inputs.astype(jnp.float32)]
    stored = []
    for layer_index in range(LAYERS):
        weights = fetch_layer(layer_index)
        result, kept_here = forward(streams[layer_index], skip_inputs[layer_index], weights)
        stored.append((weights, kept_here))
        streams.append(result)
    output = streams[LAYERS]
    stream_grad = cotangent.astype(jnp.float32)
    skip_parts = [None] * LAYERS
    small_parts = [None] * LAYERS
    block_parts = [None] * LAYERS
    for layer_index in reversed(range(LAYERS)):
        weights = fetch_layer(layer_index)
        unused_result, kept = forward(streams[layer_index], skip_inputs[layer_index], weights)
        (
            backward_small_params,
            backward_weight_skip,
            backward_weight_qkv,
            backward_weight_out,
            backward_weight_up,
            backward_bias_up,
            backward_weight_down,
        ) = weights
        (
            backward_rows_joined,
            backward_hidden,
            backward_rows_first,
            backward_triple,
            backward_head_out,
            backward_log_total,
            backward_middle,
            backward_rows_second,
            backward_preact,
            backward_activated,
        ) = kept
        down_bias_grad = jnp.sum(stream_grad, 0)
        grad_rows = grad_rows_of(stream_grad.astype(jnp.bfloat16))
        act_grad = jnp.einsum(
            "td,fd->tf", grad_rows, backward_weight_down, preferred_element_type=jnp.float32
        )
        down_weight_grad = jnp.einsum(
            "tf,td->fd", backward_activated, grad_rows, preferred_element_type=jnp.float32
        )
        gelu_unused, gelu_pull = jax.vjp(gelu_exact, backward_preact)
        pre_grad = gelu_pull(act_grad)[0]
        up_bias_part = jnp.sum(pre_grad, 0)
        pre_low = pre_grad.astype(jnp.bfloat16)
        up_weight_grad = jnp.einsum(
            "td,tf->df", backward_rows_second, pre_low, preferred_element_type=jnp.float32
        )
        second_grad = sum_row_grads(
            jnp.einsum("tf,df->td", pre_low, backward_weight_up, preferred_element_type=jnp.float32)
        )
        up_bias_full = lax.dynamic_update_slice_in_dim(
            jnp.zeros((FF,), jnp.float32),
            up_bias_part,
            lax.axis_index("tp") * up_bias_part.shape[0],
            0,
        )
        norm_unused, second_pull = jax.vjp(
            norm_apply, backward_middle, backward_small_params[4], backward_small_params[5]
        )
        middle_norm_grad, second_gain_grad, second_shift_grad = second_pull(second_grad)
        middle_grad = stream_grad + middle_norm_grad
        out_bias_grad = jnp.sum(middle_grad, 0)
        middle_rows = grad_rows_of(middle_grad.astype(jnp.bfloat16))
        mixed_grad = jnp.einsum(
            "td,hd->th", middle_rows, backward_weight_out, preferred_element_type=jnp.float32
        ).astype(jnp.bfloat16)
        out_weight_grad = jnp.einsum(
            "th,td->hd", backward_head_out, middle_rows, preferred_element_type=jnp.float32
        )
        backward_seq_count = backward_rows_first.shape[0] // SEQ_LEN
        triple_grad = lax.map(
            attend_back,
            (
                backward_triple.reshape(backward_seq_count, SEQ_LEN, 3, -1),
                backward_log_total,
                mixed_grad.reshape(backward_seq_count, SEQ_LEN, -1),
            ),
        )
        triple_grad = triple_grad.reshape(backward_triple.shape)
        qkv_weight_grad = jnp.einsum(
            "td,tch->dch", backward_rows_first, triple_grad, preferred_element_type=jnp.float32
        )
        first_grad = sum_row_grads(
            jnp.einsum(
                "tch,dch->td", triple_grad, backward_weight_qkv, preferred_element_type=jnp.float32
            )
        )
        norm_unused_two, first_pull = jax.vjp(
            norm_apply, backward_hidden, backward_small_params[1], backward_small_params[2]
        )
        hidden_norm_grad, first_gain_grad, first_shift_grad = first_pull(first_grad)
        hidden_grad = middle_grad + hidden_norm_grad
        skip_bias_grad = jnp.sum(hidden_grad, 0)
        hidden_low = hidden_grad.astype(jnp.bfloat16)
        hidden_cols = lax.all_to_all(hidden_low, "tp", split_axis=1, concat_axis=0, tiled=True)
        joined_grad = sum_row_grads(
            jnp.einsum(
                "te,ce->tc", hidden_cols, backward_weight_skip, preferred_element_type=jnp.float32
            )
        )
        skip_weight_grad = jnp.einsum(
            "tc,te->ce", backward_rows_joined, hidden_cols, preferred_element_type=jnp.float32
        )
        small_grads = (
            lax.psum_scatter(skip_bias_grad, ("fsdp", "tp"), scatter_dimension=0, tiled=True),
            lax.psum_scatter(
                first_gain_grad.astype(jnp.float32), ("fsdp", "tp"), scatter_dimension=0, tiled=True
            ),
            lax.psum_scatter(
                first_shift_grad.astype(jnp.float32),
                ("fsdp", "tp"),
                scatter_dimension=0,
                tiled=True,
            ),
            lax.psum_scatter(out_bias_grad, ("fsdp", "tp"), scatter_dimension=0, tiled=True),
            lax.psum_scatter(
                second_gain_grad.astype(jnp.float32),
                ("fsdp", "tp"),
                scatter_dimension=0,
                tiled=True,
            ),
            lax.psum_scatter(
                second_shift_grad.astype(jnp.float32),
                ("fsdp", "tp"),
                scatter_dimension=0,
                tiled=True,
            ),
            lax.psum_scatter(up_bias_full, ("fsdp", "tp"), scatter_dimension=0, tiled=True),
            lax.psum_scatter(down_bias_grad, ("fsdp", "tp"), scatter_dimension=0, tiled=True),
        )
        block_grads = (
            lax.psum_scatter(
                skip_weight_grad.astype(jnp.bfloat16), "fsdp", scatter_dimension=0, tiled=True
            ).astype(jnp.float32),
            lax.psum_scatter(
                qkv_weight_grad.astype(jnp.bfloat16), "fsdp", scatter_dimension=0, tiled=True
            ).astype(jnp.float32),
            lax.psum_scatter(
                out_weight_grad.astype(jnp.bfloat16), "fsdp", scatter_dimension=1, tiled=True
            ).astype(jnp.float32),
            lax.psum_scatter(
                up_weight_grad.astype(jnp.bfloat16), "fsdp", scatter_dimension=0, tiled=True
            ).astype(jnp.float32),
            lax.psum_scatter(
                down_weight_grad.astype(jnp.bfloat16), "fsdp", scatter_dimension=1, tiled=True
            ).astype(jnp.float32),
        )
        width = backward_weight_skip.shape[0] // 2
        stream_grad, skip_part, small_grads, block_grads = (
            joined_grad[:, :width],
            joined_grad[:, width:],
            small_grads,
            block_grads,
        )
        skip_parts[layer_index] = skip_part
        small_parts[layer_index] = small_grads
        block_parts[layer_index] = block_grads

    def stack_small(position):
        return jnp.stack([small_parts[index_layer][position] for index_layer in range(LAYERS)])

    def stack_block(position):
        return jnp.stack([block_parts[index_layer][position] for index_layer in range(LAYERS)])

    return (
        output,
        stream_grad,
        jnp.stack(skip_parts),
        stack_block(0),
        stack_small(0),
        stack_small(1),
        stack_small(2),
        stack_block(1),
        stack_block(2),
        stack_small(3),
        stack_small(4),
        stack_small(5),
        stack_block(3),
        stack_small(6),
        stack_block(4),
        stack_small(7),
    )


FSDP = ("chip", "core")
BOTH = ("chip", "core", "tp")
NETWORK = ("chip", "tp")
GAUSS = 0.3989422804014327


class Sequence:
    def __init__(self):
        self.last = None

    def at(self, value):
        if self.last is None:
            return value
        return lax.optimization_barrier((value, self.last))[0]

    def mark(self, value):
        self.last = value
        return value


class RingGather:
    def __init__(self, net, block):
        self.net, self.round = (net, 0)
        self.blocks = {0: block}
        self.ahead, self.behind = (block, block)
        self.send()

    def send(self):
        ahead, behind = (self.ahead, self.behind)
        if self.round + 1 == self.net.half_ring:
            middle = ahead.shape[1] // 256 * 128
            ahead, behind = (ahead[:, :middle], behind[:, middle:])
        self.coming = (self.net.along_ring(ahead, 1), self.net.along_ring(behind, -1))

    def advance(self, sequence):
        got = sequence.mark(sequence.at(self.coming))
        self.round += 1
        if self.round == self.net.half_ring:
            self.blocks[self.round] = got
            return
        self.ahead, self.behind = got
        self.blocks[-self.round], self.blocks[self.round] = got
        self.send()

    def whole(self, pieces):
        net, offsets = (self.net, sorted(self.blocks))
        operands, jobs = ([], [])
        pair_rows = self.blocks[0].shape[0]
        half_rows = pair_rows // 2
        shapes = [(net.chips * pair_rows * slabs, width) for begin, width, slabs in pieces]
        for at, offset in enumerate(offsets):
            held = self.blocks[offset]
            start = 0
            for part in held if isinstance(held, tuple) else (held,):
                stop = start + part.shape[1]
                for which, (begin, width, slabs) in enumerate(pieces):
                    for slab in range(slabs):
                        low = max(start, begin + slab * width)
                        high = min(stop, begin + (slab + 1) * width)
                        if low >= high:
                            continue
                        to = low - begin - slab * width
                        spans = [(0, pair_rows, 0)]
                        if slabs > 1:
                            spans = [
                                (i * half_rows, half_rows, (i * slabs + slab) * half_rows)
                                for i in range(2)
                            ]
                        for row, rows, to_row in spans:
                            jobs.append(
                                (len(operands), row, rows, low - start, high - low, which, at)
                                + (pair_rows * slabs, to_row, to)
                            )
                operands.append(part)
                start = stop
        table = [
            [net.order[(net.order.index(q) + offset) % net.chips] for offset in offsets]
            for q in range(net.chips)
        ]
        places = lax.dynamic_index_in_dim(jnp.asarray(table, jnp.int32), net.chip, 0, False, allow_negative_indices=False)
        return copy_kernel(places, operands, jobs, shapes)


def add_blocks(places, tensors, blocks, ahead, behind):
    rows = tensors[0].shape[0] // blocks
    widths = [t.shape[1] for t in tensors]
    total = sum(widths)
    spans = ((0, ahead.shape[1]), (total - behind.shape[1], total))

    def kernel(at_ref, *refs):
        count = len(tensors)
        for side in range(2):
            got_ref, out_ref = (refs[2 * count + side], refs[2 * count + 2 + side])
            low, high = spans[side]
            begin = 0
            for index, width in enumerate(widths):
                block_ref = refs[side * count + index]
                first, last = (max(begin, low), min(begin + width, high))
                if first >= last:
                    out_ref[:, begin : begin + width] = block_ref[...]
                else:
                    if first > begin:
                        out_ref[:, begin:first] = block_ref[:, : first - begin]
                    if last < begin + width:
                        out_ref[:, last : begin + width] = block_ref[:, last - begin :]
                    own = block_ref[:, first - begin : last - begin].astype(jnp.float32)
                    got = got_ref[:, first - low : last - low].astype(jnp.float32)
                    out_ref[:, first:last] = (own + got).astype(jnp.bfloat16)
                begin += width

    def whole(value):
        return pl.BlockSpec(value.shape, lambda i, at: (0, 0))

    def block(width, side):
        return pl.BlockSpec((rows, width), lambda i, at: (at[side], 0))

    out = jax.ShapeDtypeStruct((rows, total), jnp.bfloat16)
    return pl.pallas_call(
        kernel,
        grid_spec=pltpu.PrefetchScalarGridSpec(
            num_scalar_prefetch=1,
            grid=(1,),
            in_specs=[block(width, side) for side in range(2) for width in widths]
            + [whole(ahead), whole(behind)],
            out_specs=[whole(out), whole(out)],
        ),
        out_shape=[out, out],
        compiler_params=pltpu.CompilerParams(vmem_limit_bytes=24 << 20),
        cost_estimate=pl.CostEstimate(
            flops=2 * rows * total, bytes_accessed=12 * rows * total, transcendentals=0
        ),
    )(places, *tensors, *tensors, ahead, behind)


class RingSum:
    def __init__(self, net, tensors, columns_first):
        self.net, self.columns_first = (net, columns_first)
        self.views = [t.reshape(net.chips, 2, -1, t.shape[1]) for t in tensors]
        if columns_first:
            self.stage = "columns"
            self.coming = [
                net.to_column(lax.dynamic_index_in_dim(v, 1 - net.column, 1, False, allow_negative_indices=False))
                for v in self.views
            ]
        else:
            self.views = [v.reshape(net.chips, -1, v.shape[3]) for v in self.views]
            self.begin()

    def block(self, offset):
        at = self.net.chip_at(offset)
        parts = [lax.dynamic_index_in_dim(v, at, 0, False, allow_negative_indices=False) for v in self.views]
        return jnp.concatenate(parts, 1)

    def begin(self):
        self.stage, self.distance = ("ring", self.net.half_ring)
        far = self.block(self.net.half_ring)
        middle = far.shape[1] // 256 * 128
        self.coming = (
            self.net.along_ring(far[:, :middle], 1),
            self.net.along_ring(far[:, middle:], -1),
        )

    def advance(self, sequence):
        net, got = (self.net, sequence.at(self.coming))
        if self.stage == "columns":
            self.views = [
                (
                    lax.dynamic_index_in_dim(v, net.column, 1, False, allow_negative_indices=False).astype(jnp.float32)
                    + other.astype(jnp.float32)
                ).astype(jnp.bfloat16)
                for v, other in zip(self.views, got)
            ]
            sequence.mark(self.views)
            self.begin()
            return
        if self.stage == "last":
            total = self.keep + got.astype(jnp.float32)
            self.total = sequence.mark(total.astype(jnp.bfloat16))
            return
        ahead, behind = got
        self.distance -= 1
        if self.distance:
            places = jnp.stack([net.chip_at(self.distance), net.chip_at(-self.distance)])
            flat = [v.reshape(-1, v.shape[2]) for v in self.views]
            ahead, behind = sequence.mark(add_blocks(places, flat, net.chips, ahead, behind))
            self.coming = (net.along_ring(ahead, 1), net.along_ring(behind, -1))
            return
        ahead, behind = (ahead.astype(jnp.float32), behind.astype(jnp.float32))
        total = self.block(0).astype(jnp.float32) + ahead + behind
        if self.columns_first:
            self.total = sequence.mark(total.astype(jnp.bfloat16))
            return
        half_rows = total.shape[0] // 2
        self.keep = lax.dynamic_slice_in_dim(total, net.column * half_rows, half_rows, 0, allow_negative_indices=False)
        send = lax.dynamic_slice_in_dim(total, (1 - net.column) * half_rows, half_rows, 0, allow_negative_indices=False)
        send = sequence.mark(send.astype(jnp.bfloat16))
        self.stage, self.coming = ("last", net.to_column(send))


class HalvingSum:
    def __init__(self, net, tensors, bits):
        self.net, self.bits, self.round = (net, bits, 0)
        count = len(bits)
        self.views = [t.reshape((2,) * count + (-1, t.shape[1])) for t in tensors]
        self.left = list(reversed(range(count)))
        self.cut()

    def cut(self):
        bit = self.bits[self.round]
        axis = self.left.index(bit)
        self.left.remove(bit)
        side = self.net.side(bit)

        def half(which):
            parts = [lax.dynamic_index_in_dim(v, which, axis, False, allow_negative_indices=False) for v in self.views]
            return jnp.concatenate(parts, -1)

        self.keep = half(side)
        self.coming = self.net.to_partner(half(1 - side), bit)

    def advance(self, sequence):
        got = sequence.at(self.coming)
        total = self.keep.astype(jnp.float32) + got.astype(jnp.float32)
        self.round += 1
        self.total = sequence.mark(total.astype(jnp.bfloat16))
        if self.round < len(self.bits):
            self.views = [self.total]
            self.cut()


class HalvingSum:
    def __init__(self, net, tensors, bits):
        self.net, self.bits, self.round = (net, bits, 0)
        count = len(bits)
        self.views = [t.reshape((2,) * count + (-1, t.shape[1])) for t in tensors]
        self.left = list(reversed(range(count)))
        self.cut()

    def cut(self):
        bit = self.bits[self.round]
        axis = self.left.index(bit)
        self.left.remove(bit)
        side = self.net.side(bit)

        def half(which):
            parts = [lax.dynamic_index_in_dim(v, which, axis, False, allow_negative_indices=False) for v in self.views]
            return jnp.concatenate(parts, -1)

        self.keep = half(side)
        self.coming = self.net.to_partner(half(1 - side), bit)

    def advance(self, sequence):
        got = sequence.at(self.coming)
        total = self.keep.astype(jnp.float32) + got.astype(jnp.float32)
        self.round += 1
        self.total = sequence.mark(total.astype(jnp.bfloat16))
        if self.round < len(self.bits):
            self.views = [self.total]
            self.cut()


class HalvingSum:
    def __init__(self, net, tensors, bits):
        self.net, self.bits, self.round = (net, bits, 0)
        count = len(bits)
        self.views = [t.reshape((2,) * count + (-1, t.shape[1])) for t in tensors]
        self.left = list(reversed(range(count)))
        self.cut()

    def cut(self):
        bit = self.bits[self.round]
        axis = self.left.index(bit)
        self.left.remove(bit)
        side = self.net.side(bit)

        def half(which):
            parts = [lax.dynamic_index_in_dim(v, which, axis, False, allow_negative_indices=False) for v in self.views]
            return jnp.concatenate(parts, -1)

        self.keep = half(side)
        self.coming = self.net.to_partner(half(1 - side), bit)

    def advance(self, sequence):
        got = sequence.at(self.coming)
        total = self.keep.astype(jnp.float32) + got.astype(jnp.float32)
        self.round += 1
        self.total = sequence.mark(total.astype(jnp.bfloat16))
        if self.round < len(self.bits):
            self.views = [self.total]
            self.cut()


class HalvingSum:
    def __init__(self, net, tensors, bits):
        self.net, self.bits, self.round = (net, bits, 0)
        count = len(bits)
        self.views = [t.reshape((2,) * count + (-1, t.shape[1])) for t in tensors]
        self.left = list(reversed(range(count)))
        self.cut()

    def cut(self):
        bit = self.bits[self.round]
        axis = self.left.index(bit)
        self.left.remove(bit)
        side = self.net.side(bit)

        def half(which):
            parts = [lax.dynamic_index_in_dim(v, which, axis, False, allow_negative_indices=False) for v in self.views]
            return jnp.concatenate(parts, -1)

        self.keep = half(side)
        self.coming = self.net.to_partner(half(1 - side), bit)

    def advance(self, sequence):
        got = sequence.at(self.coming)
        total = self.keep.astype(jnp.float32) + got.astype(jnp.float32)
        self.round += 1
        self.total = sequence.mark(total.astype(jnp.bfloat16))
        if self.round < len(self.bits):
            self.views = [self.total]
            self.cut()


class Swap:
    def __init__(self, net, tensors):
        self.net, self.tensors = (net, tensors)
        self.coming = [net.diagonal_other(value) for value in tensors]

    def advance(self, sequence):
        self.coming = sequence.mark(sequence.at(self.coming))


class CoreNetwork:
    def __init__(self, fsdp_size):
        self.chips = fsdp_size // 2
        self.core = lax.axis_index("core")
        self.chip = lax.axis_index("chip")
        self.column = lax.axis_index("tp")
        self.bits = self.chips.bit_length()
        half = self.chips // 2
        self.half_ring = half
        self.order = [2 * i for i in range(half)] + [2 * i + 1 for i in reversed(range(half))]
        table = [
            [self.order[(self.order.index(q) + offset) % self.chips] for offset in range(self.chips)]
            for q in range(self.chips)
        ]
        self.chips_here = lax.dynamic_index_in_dim(
            jnp.asarray(table, jnp.int32), self.chip, 0, False, allow_negative_indices=False
        )
        self.ring_pairs = {}
        for step in (1, -1):
            self.ring_pairs[step] = [
                (self.order[i] * 2 + c, self.order[(i + step) % self.chips] * 2 + c)
                for i in range(self.chips)
                for c in range(2)
            ]
        self.core_pairs = [(i, i ^ 1) for i in range(fsdp_size)]
        self.diagonal_pairs = []
        for q in range(self.chips):
            one, two = (q * 4 + 2, q * 4 + 1)
            self.diagonal_pairs += [(one, two), (two, one)]

    def to_core(self, value):
        return lax.ppermute(value, FSDP, self.core_pairs)

    def chip_at(self, offset):
        return self.chips_here[offset % self.chips]

    def along_ring(self, value, step):
        return lax.ppermute(value, FSDP, self.ring_pairs[step])

    def to_column(self, value):
        return self.to_partner(value, 0)

    def diagonal_other(self, value):
        return lax.ppermute(value, BOTH, self.diagonal_pairs)

    def choose(self, own, other):
        return jnp.where(self.core == self.column, own, other)

    def diagonal(self, value):
        return self.choose(value, self.diagonal_other(value))

    def to_partner(self, value, bit):
        if bit == 0:
            return lax.ppermute(value, "tp", [(0, 1), (1, 0)])
        flip = 1 << (bit - 1)
        pairs = [(q * 2 + c, (q ^ flip) * 2 + c) for q in range(self.chips) for c in range(2)]
        return lax.ppermute(value, FSDP, pairs)

    def side(self, bit):
        return self.column if bit == 0 else (self.chip >> (bit - 1)) & 1

    def sum_small(self, packed):
        for bit in reversed(range(self.bits + 1)):
            count = packed.shape[0] // 2
            if bit == 1:
                side, send_to = (self.core, self.to_core)
            else:
                wire = max(bit - 1, 0)
                side = self.side(wire)
                send_to = lambda value, wire=wire: self.to_partner(value, wire)
            keep = jnp.where(side == 0, packed[:count], packed[count:])
            send = jnp.where(side == 0, packed[count:], packed[:count])
            packed = keep + send_to(send)
        return packed[0]


def copy_kernel(places, operands, jobs, shapes):
    def kernel(at_ref, *refs):
        sources, targets = (refs[: len(operands)], refs[len(operands) :][: len(shapes)])
        buffers = refs[len(operands) + len(shapes) : -2]
        sems, out_sems = refs[-2:]
        copies = [[] for _ in shapes]
        for which in range(len(shapes)):
            for index, job in enumerate(jobs):
                source, row, rows, col, width, target, at, scale, offset, to = job
                if target != which:
                    continue
                begin = pl.multiple_of(at_ref[at] * scale + offset, 16)
                copy = pltpu.make_async_copy(
                    sources[source].at[pl.ds(row, rows), pl.ds(col, width)],
                    buffers[which].at[pl.ds(begin, rows), pl.ds(to, width)],
                    sems.at[index],
                )
                copy.start()
                copies[which].append(copy)
        outs = []
        for which in range(len(shapes)):
            for copy in copies[which]:
                copy.wait()
            out = pltpu.make_async_copy(buffers[which], targets[which], out_sems.at[which])
            out.start()
            outs.append(out)
        for out in outs:
            out.wait()

    moved = sum(2 * 2 * r * w for r, w in shapes)
    return pl.pallas_call(
        kernel,
        out_shape=[jax.ShapeDtypeStruct(shape, jnp.bfloat16) for shape in shapes],
        in_specs=[pl.BlockSpec(memory_space=pltpu.SMEM)]
        + [pl.BlockSpec(memory_space=pl.ANY)] * len(operands),
        out_specs=[pl.BlockSpec(memory_space=pl.ANY)] * len(shapes),
        scratch_shapes=[pltpu.VMEM(shape, jnp.bfloat16) for shape in shapes]
        + [pltpu.SemaphoreType.DMA((len(jobs),)), pltpu.SemaphoreType.DMA((len(shapes),))],
        compiler_params=pltpu.CompilerParams(vmem_limit_bytes=24 << 20),
        cost_estimate=pl.CostEstimate(flops=0, bytes_accessed=moved, transcendentals=0),
    )(places, *operands)


def row_chunks(count, size):
    return [(begin, min(size, count - begin)) for begin in range(0, count, size)]


NT = (((1,), (1,)), ((), ()))
TN = (((0,), (0,)), ((), ()))


def head_lanes(value, head):
    lane = lax.broadcasted_iota(jnp.int32, value.shape, 1)
    return jnp.where((lane >= HEAD_DIM) == (head == 1), value, jnp.zeros_like(value))


def attention_forward(triple):
    tokens, width = (triple.shape[0], triple.shape[1] // 3)
    pairs = width // (2 * HEAD_DIM)

    def kernel(query_ref, key_ref, value_ref, out_ref, total_ref):
        keys = key_ref[...]
        values = value_ref[...]
        for begin, rows in row_chunks(tokens, 640):
            query = query_ref[begin : begin + rows, :] * jnp.bfloat16(HEAD_DIM**-0.5)
            mixed, totals = ([], [])
            for head in range(2):
                scores = lax.dot_general(
                    head_lanes(query, head), keys, NT, preferred_element_type=jnp.float32
                )
                top = jnp.max(scores, -1, keepdims=True)
                grown = jnp.exp(scores - top)
                total = jnp.sum(grown, -1, keepdims=True)
                mixed.append(
                    jnp.dot(
                        grown.astype(jnp.bfloat16), values, preferred_element_type=jnp.float32
                    )
                    / total
                )
                totals.append(top + jnp.log(total))
            lane = lax.broadcasted_iota(jnp.int32, mixed[0].shape, 1)
            out_ref[begin : begin + rows, :] = jnp.where(
                lane < HEAD_DIM, mixed[0], mixed[1]
            ).astype(jnp.bfloat16)
            both = jnp.where(lane < HEAD_DIM, totals[0], totals[1]).T
            total_ref[0, 0:1, begin : begin + rows] = both[0:1, :]
            total_ref[0, 1:2, begin : begin + rows] = both[HEAD_DIM : HEAD_DIM + 1, :]

    def part(index):
        return pl.BlockSpec((tokens, 2 * HEAD_DIM), lambda i: (0, index * pairs + i))

    return pl.pallas_call(
        kernel,
        grid=(pairs,),
        in_specs=[part(0), part(1), part(2)],
        out_specs=[part(0), pl.BlockSpec((1, 2, tokens), lambda i: (i, 0, 0))],
        out_shape=[
            jax.ShapeDtypeStruct((tokens, width), jnp.bfloat16),
            jax.ShapeDtypeStruct((pairs, 2, tokens), jnp.float32),
        ],
        compiler_params=pltpu.CompilerParams(vmem_limit_bytes=48 << 20),
        cost_estimate=pl.CostEstimate(
            flops=16 * pairs * tokens * tokens * HEAD_DIM,
            bytes_accessed=8 * tokens * width,
            transcendentals=2 * pairs * tokens * tokens,
        ),
    )(triple, triple, triple)


def attention_backward(triple, head_out, log_total, mixed_grad, first_pair, pair_count):
    tokens, width = (triple.shape[0], triple.shape[1] // 3)
    pairs = width // (2 * HEAD_DIM)
    score_scale = HEAD_DIM**-0.5

    def kernel(
        query_ref, key_ref, value_ref, out_ref, total_ref, grad_ref, dq_ref, dk_ref, dv_ref, sum_ref
    ):
        query = query_ref[...] * jnp.bfloat16(score_scale)
        grad = grad_ref[...]
        product = grad.astype(jnp.float32) * out_ref[...].astype(jnp.float32)
        ones = jnp.ones((8, 2 * HEAD_DIM), jnp.float32)
        deltas = [
            lax.dot_general(
                head_lanes(ones, head),
                product,
                NT,
                precision=lax.Precision.HIGHEST,
                preferred_element_type=jnp.float32,
            )[0:1, :]
            for head in range(2)
        ]
        for begin, rows in row_chunks(tokens, 256):
            keys = key_ref[begin : begin + rows, :]
            values = value_ref[begin : begin + rows, :]
            key_grads, value_grads = ([], [])
            for head in range(2):
                keys_here = head_lanes(keys, head)
                scores = lax.dot_general(
                    keys_here, query, NT, preferred_element_type=jnp.float32
                )
                probs = jnp.exp(scores - total_ref[0, head : head + 1, :])
                prob_grad = lax.dot_general(
                    head_lanes(values, head), grad, NT, preferred_element_type=jnp.float32
                )
                score_grad = (probs * (prob_grad - deltas[head])).astype(jnp.bfloat16)
                value_grads.append(
                    jnp.dot(
                        probs.astype(jnp.bfloat16), grad, preferred_element_type=jnp.float32
                    )
                )
                key_grads.append(jnp.dot(score_grad, query, preferred_element_type=jnp.float32))
                query_grad = lax.dot_general(
                    score_grad, keys_here, TN, preferred_element_type=jnp.float32
                )
                if begin == 0 and head == 0:
                    sum_ref[...] = query_grad
                else:
                    sum_ref[...] += query_grad
            lane = lax.broadcasted_iota(jnp.int32, key_grads[0].shape, 1)
            dk_ref[begin : begin + rows, :] = jnp.where(
                lane < HEAD_DIM, key_grads[0], key_grads[1]
            ).astype(jnp.bfloat16)
            dv_ref[begin : begin + rows, :] = jnp.where(
                lane < HEAD_DIM, value_grads[0], value_grads[1]
            ).astype(jnp.bfloat16)
        dq_ref[...] = (sum_ref[...] * score_scale).astype(jnp.bfloat16)

    def part(index):
        return pl.BlockSpec((tokens, 2 * HEAD_DIM), lambda i: (0, index * pairs + first_pair + i))

    return pl.pallas_call(
        kernel,
        grid=(pair_count,),
        in_specs=[
            part(0),
            part(1),
            part(2),
            part(0),
            pl.BlockSpec((1, 2, tokens), lambda i: (first_pair + i, 0, 0)),
            part(0),
        ],
        out_specs=[pl.BlockSpec((tokens, 2 * HEAD_DIM), lambda i: (0, i))] * 3,
        out_shape=[jax.ShapeDtypeStruct((tokens, pair_count * 2 * HEAD_DIM), jnp.bfloat16)] * 3,
        scratch_shapes=[pltpu.VMEM((tokens, 2 * HEAD_DIM), jnp.float32)],
        compiler_params=pltpu.CompilerParams(vmem_limit_bytes=48 << 20),
        cost_estimate=pl.CostEstimate(
            flops=40 * pair_count * tokens * tokens * HEAD_DIM,
            bytes_accessed=32 * tokens * pair_count * HEAD_DIM,
            transcendentals=2 * pair_count * tokens * tokens,
        ),
    )(triple, triple, triple, head_out, log_total, mixed_grad)


SWAPPED = ("i1", "s1")
HALVED = {"w1": (0, 2, 1, 3), "u1": (1, 0, 2, 3), "u0": (1, 0, 2, 3), "w0": (2, 1, 0, 3)}
PLAN = (
    "+D0", "D0", "+P0", "+D1", "P0", "+R0", "D1", "+P1", "R0", "P1", "+R1", "+E", "R0", "+D2", "R1",
    "D2", "+P2", "R0", "R1", "P2", "+P3", "R0", "+U0", "R1", "E", "R1", "+W0", "skip 0", "U0", "full 0",
    "W0", "P3", "+L", "hid 0", "U0", "W0", "skip 1", "qkv 0", "U0", "attend 0", "W0", "L", "out 0", "U0",
    "+U1", "second_norm 0", "W0", "+W1", "up 0", "U1", "down_held 0", "down 0", "W1", "full 1", "next 0",
    "U1", "hid 1", "W1", "qkv 1", "U1", "attend 1", "W1", "out 1", "U1", "second_norm 1", "W1",
    "grad_rows 1", "up 1", "down_grad 1", "+w1", "down_held 1", "act 1", "second 1", "up_grad 1", "+u1",
    "middle 1", "mixed 1", "out_grad 1", "heads0 1", "heads1 1", "w1", "u1", "first 1",
    "qkv_grad 1", "+i1", "hidden_grad 1", "joined 1", "w1", "grad_rows 0", "skip_grad 1", "u1", "act 0",
    "w1", "u1", "skip_sum 1", "+s1", "second 0", "w1", "up_grad 0", "u1", "+u0", "down_grad 0",
    "+w0", "middle 0", "mixed 0", "out_grad 0", "i1", "heads0 0", "u0", "s1", "is", "+G1", "heads1 0",
    "w0", "first 0", "qkv_grad 0", "+i0", "u0", "hidden_grad 0", "i0", "G1", "skip_grad 0", "joined 0",
    "+G0", "w0", "skip_sum 0", "+s0", "i0", "u0", "s0", "down 1", "i0", "w0", "s0", "next 1", "+O", "i0",
    "s0", "u0", "i0", "s0", "G0", "w0", "s0", "O",
)


def fast_body(
    fsdp_size,
    inputs,
    skip_inputs,
    skip_weight,
    skip_bias,
    first_gain,
    first_shift,
    attention_in,
    attention_out,
    out_bias,
    second_gain,
    second_shift,
    up_weight,
    up_bias,
    down_weight,
    down_bias,
    cotangent,
):
    net = CoreNetwork(fsdp_size)
    core, to_core, diagonal = (net.core, net.to_core, net.diagonal)
    count, width = inputs.shape
    shard_rows = attention_in.shape[1]
    skip_rows, skip_width = skip_weight.shape[1:]
    qkv_width = attention_in.shape[2] * attention_in.shape[3]
    up_width = up_weight.shape[2]
    down_width = down_weight.shape[1]
    f32, low_type = (jnp.float32, jnp.bfloat16)

    small_values = (
        skip_bias,
        first_gain,
        first_shift,
        out_bias,
        second_gain,
        second_shift,
        up_bias,
        down_bias,
    )
    small_widths = [value.shape[1] for value in small_values]
    small_total = sum(small_widths) * LAYERS
    small_lanes = -(-small_total // (128 * shard_rows)) * 128
    packed_small = jnp.concatenate([value.reshape(-1) for value in small_values])
    packed_small = jnp.pad(packed_small, (0, shard_rows * small_lanes - small_total))
    packed_small = packed_small.reshape(shard_rows, small_lanes)
    out_width = attention_out.shape[1]
    slab_rows = skip_rows // shard_rows
    first_width = slab_rows * skip_width + qkv_width + out_width
    first_pieces = [
        (0, skip_width, slab_rows),
        (slab_rows * skip_width, qkv_width, 1),
        (slab_rows * skip_width + qkv_width, out_width, 1),
    ]

    def first_pack(layer_index, more):
        shard = skip_weight[layer_index].reshape(slab_rows, shard_rows, skip_width)
        return jnp.concatenate(
            [shard[i] for i in range(slab_rows)]
            + [attention_in[layer_index].reshape(shard_rows, -1), attention_out[layer_index].T]
            + more,
            1,
        )

    def second_pack(layer_index):
        return jnp.concatenate([up_weight[layer_index], down_weight[layer_index].T], 1)

    sequence = Sequence()
    sources = {
        "D0": lambda: first_pack(0, [packed_small]),
        "D2": lambda: second_pack(0),
        "D1": lambda: jnp.concatenate([first_pack(1, []), second_pack(1)], 1),
        "E": lambda: jnp.concatenate([inputs, skip_inputs[0]], 1),
        "L": lambda: jnp.concatenate([skip_inputs[1], cotangent], 1),
        "O": lambda: stream_lows[LAYERS],
        "G1": lambda: grads[1]["skip_part"],
        "G0": lambda: jnp.concatenate([grads[0]["input"], grads[0]["skip_part"]], 1),
    }
    moves, pairs, gathers, reduces, blocks, sums = ({}, {}, {}, {}, {}, {})

    def moved(key, value):
        blocks[key] = value
        if key == "D0":
            blocks["P0"] = value
        elif key == "D2":
            blocks["P2"] = value
        elif key == "D1":
            blocks["P1"] = value[:, :first_width]
            blocks["P3"] = value[:, first_width:]

    def paired(own, other):
        return jnp.where(
            net.column == 0,
            jnp.concatenate([own, other], 0),
            jnp.concatenate([other, own], 0),
        )

    def small_of(layer_index, all_small):
        values, begin = ([], 0)
        for size in small_widths:
            values.append(
                all_small[:, begin + layer_index * size : begin + (layer_index + 1) * size].reshape(
                    -1
                )
            )
            begin += LAYERS * size
        values[6] = lax.dynamic_slice_in_dim(values[6], core * up_width, up_width, allow_negative_indices=False)
        return values

    weights = [{}, {}]
    smalls = [None, None]
    kept = [{}, {}]
    streams = [None] * (LAYERS + 1)
    stream_lows = [None] * (LAYERS + 1)

    def send(now, name, value):
        now[name] = to_core(sequence.mark(value))

    def received(now, name):
        return sequence.at(now.pop(name))

    def rows_with(own, other):
        return jnp.concatenate([own, other], 0)

    def skip_step(index):
        held, now = (weights[index], kept[index])
        if index == 0:
            held["half"], held["qkv"], held["out"], small_here = gathers["R0"].whole(
                first_pieces + [(first_width, small_lanes, 1)]
            )
            small_here = small_here.reshape(2 * net.chips, -1)
            small_other = to_core(small_here)
            all_small = jnp.where(
                core == 0,
                jnp.stack([small_here, small_other], 1),
                jnp.stack([small_other, small_here], 1),
            ).reshape(2 * fsdp_size, -1)
            for layer_index in range(LAYERS):
                smalls[layer_index] = small_of(layer_index, all_small)
        else:
            held["half"], held["qkv"], held["out"] = gathers["R1"].whole(first_pieces)
        send(now, "skip_other", held["half"])

    def in_columns(own, other):
        return jnp.where(
            core == 0, jnp.concatenate([own, other], 1), jnp.concatenate([other, own], 1)
        )

    def full_step(index):
        held, other = (weights[index], received(kept[index], "skip_other"))
        held["skip"] = sequence.mark(in_columns(held["half"], other))

    def hid_step(index):
        held, now, small = (weights[index], kept[index], smalls[index])
        if index == 0:
            stream_lows[0] = blocks["E"][:, :width]
            streams[0] = stream_lows[0].astype(f32)
            skip_here = blocks["E"][:, width:]
        else:
            skip_here = blocks["L"][:, :width]
        now["joined"] = jnp.concatenate([sequence.at(stream_lows[index]), skip_here], 1)
        part = jnp.dot(now["joined"], held["skip"], preferred_element_type=f32)
        now["hidden"] = part + small[0]
        now["first_norm"] = norm_apply(now["hidden"], small[1], small[2]).astype(low_type)
        send(now, "first_other", now["first_norm"])

    def qkv_step(index):
        held, now = (weights[index], kept[index])
        now["rows_first"] = rows_with(now["first_norm"], received(now, "first_other"))
        now["triple"] = sequence.mark(
            jnp.dot(now["rows_first"], held["qkv"], preferred_element_type=f32).astype(low_type)
        )

    def attend_step(index):
        now = kept[index]
        now["head_out"], now["log_total"] = attention_forward(sequence.at(now["triple"]))
        sequence.mark(now["head_out"])

    def out_step(index):
        held, now = (weights[index], kept[index])
        part = jnp.einsum(
            "th,dh->td", sequence.at(now["head_out"]), held["out"], preferred_element_type=f32
        )
        now["mixed_own"] = part[:count]
        send(now, "mixed_other", part[count:].astype(low_type))

    def second_norm_step(index):
        now, small = (kept[index], smalls[index])
        branch = now["mixed_own"] + received(now, "mixed_other").astype(f32)
        now["middle"] = now["hidden"] + branch + small[3]
        now["second_norm"] = norm_apply(now["middle"], small[4], small[5]).astype(low_type)
        send(now, "second_other", now["second_norm"])

    def up_step(index):
        held, now = (weights[index], kept[index])
        held["up"] = gathers["U%d" % index].whole([(0, up_width, 1)])[0]
        now["rows_second"] = rows_with(now["second_norm"], received(now, "second_other"))
        preact = (
            jnp.dot(now["rows_second"], held["up"], preferred_element_type=f32) + smalls[index][6]
        )
        below = 0.5 + 0.5 * lax.erf(preact * (0.5**0.5))
        now["activated"] = (preact * below).astype(low_type)
        now["slope"] = (below + preact * jnp.exp(-0.5 * preact * preact) * GAUSS).astype(low_type)
        sequence.mark(now["activated"])

    def down_held_step(index):
        weights[index]["down"] = gathers["W%d" % index].whole([(0, down_width, 1)])[0]

    def down_step(index):
        now = kept[index]
        part = jnp.einsum(
            "tf,df->td",
            sequence.at(now["activated"]),
            weights[index]["down"],
            preferred_element_type=f32,
        )
        now["branch_own"] = part[:count]
        send(now, "branch_other", part[count:].astype(low_type))

    def next_step(index):
        now = kept[index]
        branch = now["branch_own"] + received(now, "branch_other").astype(f32)
        streams[index + 1] = now["middle"] + branch + smalls[index][7]
        stream_lows[index + 1] = sequence.mark(streams[index + 1].astype(low_type))

    grads = [{}, {}]
    summed = {}

    def grad_rows_step(index):
        now = grads[index]
        if index == LAYERS - 1:
            now["stream_low"] = blocks["L"][:, width:]
            now["stream"] = now["stream_low"].astype(f32)
        else:
            now["stream_low"] = now["stream"].astype(low_type)
        now["down_bias"] = jnp.sum(now["stream"], 0)
        send(now, "stream_other", now["stream_low"])

    def grad_rows(index):
        now = grads[index]
        if "rows" not in now:
            now["rows"] = rows_with(now["stream_low"], received(now, "stream_other"))
            return now["rows"]
        return sequence.at(now["rows"])

    def down_grad_step(index):
        now = grads[index]
        now["down"] = sequence.mark(
            jnp.einsum(
                "td,tf->df",
                grad_rows(index),
                kept[index]["activated"],
                preferred_element_type=f32,
            ).astype(low_type)
        )
        sums["w%d" % index] = [now["down"]]

    def act_step(index):
        now = grads[index]
        act_grad = jnp.dot(
            grad_rows(index), weights[index]["down"], preferred_element_type=f32
        )
        pre_grad = act_grad * kept[index]["slope"]
        now["up_bias"] = jnp.sum(pre_grad, 0)
        now["pre_low"] = sequence.mark(pre_grad.astype(low_type))

    def second_step(index):
        now = grads[index]
        part = jnp.einsum(
            "tf,df->td",
            sequence.at(now["pre_low"]),
            weights[index]["up"],
            preferred_element_type=f32,
        )
        now["second_own"] = part[:count]
        send(now, "second_other", part[count:].astype(low_type))

    def up_grad_step(index):
        now = grads[index]
        now["up"] = sequence.mark(
            jnp.einsum(
                "td,tf->df",
                sequence.at(kept[index]["rows_second"]),
                now["pre_low"],
                preferred_element_type=f32,
            ).astype(low_type)
        )
        sums["u%d" % index] = [now["up"]]

    def middle_step(index):
        now, small = (grads[index], smalls[index])
        second_grad = now["second_own"] + received(now, "second_other").astype(f32)
        unused, pull = jax.vjp(norm_apply, kept[index]["middle"], small[4], small[5])
        norm_grad, now["second_gain"], now["second_shift"] = pull(second_grad)
        now["middle"] = now["stream"] + norm_grad
        now["out_bias"] = jnp.sum(now["middle"], 0)
        now["middle_low"] = now["middle"].astype(low_type)
        send(now, "middle_other", now["middle_low"])

    def mixed_step(index):
        now = grads[index]
        now["middle_rows"] = rows_with(now["middle_low"], received(now, "middle_other"))
        now["mixed"] = sequence.mark(
            jnp.dot(
                now["middle_rows"], weights[index]["out"], preferred_element_type=f32
            ).astype(low_type)
        )

    def out_grad_step(index):
        now = grads[index]
        now["out"] = sequence.mark(
            jnp.einsum(
                "td,th->dh",
                sequence.at(now["middle_rows"]),
                kept[index]["head_out"],
                preferred_element_type=f32,
            ).astype(low_type)
        )

    def attend_grad_step(index, part):
        now, old = (grads[index], kept[index])
        pairs = old["log_total"].shape[0]
        first, last = (pairs * part // 2, pairs * (part + 1) // 2)
        now["heads%d" % part] = attention_backward(
            old["triple"],
            old["head_out"],
            old["log_total"],
            sequence.at(now["mixed"]),
            first,
            last - first,
        )
        sequence.mark(now["heads%d" % part][0])

    def first_step(index):
        now = grads[index]
        now["triple"] = jnp.concatenate(
            [part for both in zip(now["heads0"], now["heads1"]) for part in both], 1
        )
        part = jnp.einsum(
            "tc,dc->td",
            sequence.at(now["triple"]),
            weights[index]["qkv"],
            preferred_element_type=f32,
        )
        now["first_own"] = part[:count]
        send(now, "first_other", part[count:].astype(low_type))

    def qkv_grad_step(index):
        now = grads[index]
        now["qkv"] = sequence.mark(
            jnp.einsum(
                "td,tc->dc",
                sequence.at(kept[index]["rows_first"]),
                now["triple"],
                preferred_element_type=f32,
            ).astype(low_type)
        )
        sums["i%d" % index] = [now["qkv"], now["out"]]

    def hidden_grad_step(index):
        now, small = (grads[index], smalls[index])
        first_grad = now["first_own"] + received(now, "first_other").astype(f32)
        unused, pull = jax.vjp(norm_apply, kept[index]["hidden"], small[1], small[2])
        norm_grad, now["first_gain"], now["first_shift"] = pull(first_grad)
        hidden_grad = now["middle"] + norm_grad
        now["skip_bias"] = jnp.sum(hidden_grad, 0)
        now["hidden_low"] = sequence.mark(hidden_grad.astype(low_type))

    def joined_step(index):
        now = grads[index]
        joined_grad = jnp.einsum(
            "te,ce->tc",
            sequence.at(now["hidden_low"]),
            weights[index]["skip"],
            preferred_element_type=f32,
        )
        now["skip_part"] = joined_grad[:, width:].astype(low_type)
        before = joined_grad[:, :width]
        if index:
            grads[index - 1]["stream"] = before
        else:
            now["input"] = before.astype(low_type)
        sequence.mark(now["skip_part"])

    def skip_grad_step(index):
        now = grads[index]
        low = sequence.at(now["hidden_low"])

        def half(which):
            columns = lax.dynamic_slice_in_dim(
                low, which * skip_width, skip_width, 1, allow_negative_indices=False
            )
            return jnp.einsum(
                "tc,te->ce", kept[index]["joined"], columns, preferred_element_type=f32
            )

        send(now, "skip_other", half(1 - core).astype(low_type))
        now["skip_keep"] = half(core)

    def skip_sum_step(index):
        now = grads[index]
        other = received(now, "skip_other").astype(f32)
        now["skip"] = sequence.mark((now["skip_keep"] + other).astype(low_type))
        slabs = now["skip"].reshape(-1, slab_rows, shard_rows, skip_width)
        sums["s%d" % index] = [
            slabs[:, i].reshape(-1, skip_width) for i in range(slab_rows)
        ]

    steps = {
        "skip": skip_step,
        "full": full_step,
        "hid": hid_step,
        "qkv": qkv_step,
        "attend": attend_step,
        "out": out_step,
        "second_norm": second_norm_step,
        "up": up_step,
        "down_held": down_held_step,
        "down": down_step,
        "next": next_step,
        "grad_rows": grad_rows_step,
        "down_grad": down_grad_step,
        "act": act_step,
        "second": second_step,
        "up_grad": up_grad_step,
        "middle": middle_step,
        "out_grad": out_grad_step,
        "mixed": mixed_step,
        "heads0": lambda index: attend_grad_step(index, 0),
        "heads1": lambda index: attend_grad_step(index, 1),
        "first": first_step,
        "qkv_grad": qkv_grad_step,
        "hidden_grad": hidden_grad_step,
        "joined": joined_step,
        "skip_grad": skip_grad_step,
        "skip_sum": skip_sum_step,
    }

    for item in PLAN:
        key = item[1:]
        if " " in item:
            name, index = item.split()
            steps[name](int(index))
        elif item[0] == "+":
            if key in sources:
                own = sources[key]()
                moves[key] = (own, net.diagonal_other(sequence.at(own)))
            elif key[0] == "P":
                pairs[key] = (blocks[key], net.to_column(sequence.at(blocks[key])))
            elif key[0] in "RUW":
                gathers[key] = RingGather(net, sequence.at(blocks[key]))
            elif key in SWAPPED:
                reduces[key] = Swap(net, sequence.at(sums[key]))
            else:
                tensors = sequence.at(sums[key])
                if key in HALVED:
                    bits = [bit for bit in HALVED[key] if bit < net.bits]
                    bits += range(len(bits), net.bits)
                    reduces[key] = HalvingSum(net, tensors, bits)
                else:
                    reduces[key] = RingSum(net, tensors, False)
        elif item in moves:
            own, other = moves.pop(item)
            moved(item, sequence.mark(net.choose(own, sequence.at(other))))
        elif item in pairs:
            own, other = pairs.pop(item)
            other = sequence.at(other)
            both = sequence.mark(paired(own, other))
            if key in "01":
                blocks["R" + key] = both
            else:
                layer = str(int(key) - 2)
                blocks["U" + layer], blocks["W" + layer] = (both[:, :up_width], both[:, up_width:])
        elif item in gathers:
            gathers[item].advance(sequence)
        elif item in reduces:
            reduces[item].advance(sequence)
        else:
            chosen = [reduces[letter + "1"] for letter in item]
            own = jnp.concatenate([v for swap in chosen for v in swap.tensors], 1)
            other = sequence.at([v for swap in chosen for v in swap.coming])
            operand = sequence.mark(net.choose(own, jnp.concatenate(other, 1)))
            summed[item] = lax.psum_scatter(operand, FSDP, scatter_dimension=0, tiled=True)
    output = blocks["O"].astype(f32)

    def back(*keys):
        return diagonal(jnp.concatenate([reduces[key].total for key in keys], 1)).astype(f32)

    def slabs_below(value):
        return jnp.concatenate(
            [value[:, i * skip_width : (i + 1) * skip_width] for i in range(slab_rows)], 0
        )

    first_one = summed["is"].astype(f32)
    second_zero = back("w0", "u0")
    second_one = back("w1", "u1")
    inner_zero = back("i0")
    skip_zero = back("s0")
    inner_one = first_one[:, : qkv_width + out_width]
    skip_grads = (slabs_below(skip_zero), slabs_below(first_one[:, qkv_width + out_width :]))
    down_grads = (second_zero[:, :down_width].T, second_one[:, :down_width].T)
    up_grads = (second_zero[:, down_width:], second_one[:, down_width:])
    out_grads = (inner_zero[:, qkv_width:].T, inner_one[:, qkv_width:].T)
    qkv_grads = [v[:, :qkv_width].reshape(attention_in.shape[1:]) for v in (inner_zero, inner_one)]

    names = (
        "skip_bias",
        "first_gain",
        "first_shift",
        "out_bias",
        "second_gain",
        "second_shift",
        "up_bias",
        "down_bias",
    )
    parts = []
    for now in grads:
        full = jnp.zeros((2 * up_width,), f32)
        now["up_bias"] = lax.dynamic_update_slice_in_dim(full, now["up_bias"], core * up_width, 0, allow_negative_indices=False)
        parts += [now[name].astype(f32).reshape(2 * fsdp_size, -1) for name in names]
    small_sums = net.sum_small(jnp.concatenate(parts, 1)).reshape(LAYERS, -1)
    small_out, begin = ({}, 0)
    for name, size in zip(names, small_widths):
        small_out[name] = small_sums[:, begin : begin + size]
        begin += size
    return (
        output,
        blocks["G0"][:, :width].astype(f32),
        jnp.stack([blocks["G0"][:, width:].astype(f32), blocks["G1"].astype(f32)]),
        jnp.stack(skip_grads),
        small_out["skip_bias"],
        small_out["first_gain"],
        small_out["first_shift"],
        jnp.stack(qkv_grads),
        jnp.stack(out_grads),
        small_out["out_bias"],
        small_out["second_gain"],
        small_out["second_shift"],
        jnp.stack(up_grads),
        small_out["up_bias"],
        jnp.stack(down_grads),
        small_out["down_bias"],
    )


def solution(mesh):
    fsdp, tensor, body = ("fsdp", "tp", general_body)
    size = mesh.shape["fsdp"]
    if mesh.shape["tp"] == 2 and size >= 4 and size & (size - 1) == 0:
        mesh = Mesh(mesh.devices.reshape(size // 2, 2, 2), BOTH)
        fsdp, body = (FSDP, lambda *arrays: fast_body(size, *arrays))
    both = (*(fsdp if fsdp == FSDP else (fsdp,)), tensor)
    tokens, vector = (P(both, None), P(None, both))
    layers = P(None, both, None)
    rows, columns = (P(None, fsdp, tensor), P(None, tensor, fsdp))
    qkv = P(None, fsdp, None, tensor)
    weights = (rows, vector, vector, vector, qkv, columns, vector, vector, vector)
    weights += (rows, vector, columns, vector)
    return jax.shard_map(
        body,
        mesh=mesh,
        in_specs=(tokens, layers, *weights, tokens),
        out_specs=(tokens, tokens, layers, *weights),
        check_vma=False,
    )
```
